512 devices in a mesh: dp: 4 (over z_hi, core), row: 32 (over y, z_lo), chan: 4 (over x).
Axes of the slice: x: 4, y: 4, z: 16 (z_hi: 2, z_lo: 8; z = z_hi * 8 + z_lo), core: 2. Of those that a mesh axis runs over, the one named last changes fastest.
Arguments:
- pair: bfloat16 [1024, 256, 128], P(('dp', 'row', 'chan')), parts along dimension 0, may hold values from -256 to 256
- chain: int32 [1024], P('dp'), parts along dimension 0, may hold values from 0 to 4, never falling along the last dimension, each value on 1 to 85 neighbouring positions
- targets: int32 [1024, 256], P(('dp', 'row', 'chan')), parts along dimension 0, may hold values from 0 to 63
- pair_mask: int32 [1024, 256], P(('dp', 'row', 'chan')), parts along dimension 0, may hold values 0 or 1
- ln_in_gain: float32 [128], replicated, may hold values from 0.5 to 1.5
- ln_in_bias: float32 [128], replicated, may hold values from -3 to 3
- in_weight: bfloat16 [128, 512], replicated, may hold values from -0.5 to 0.5
- out_gate_weight: bfloat16 [128, 128], replicated, may hold values from -0.5 to 0.5
- ln_out_gain: float32 [128], replicated, may hold values from 0.5 to 1.5
- ln_out_bias: float32 [128], replicated, may hold values from -3 to 3
- out_weight: bfloat16 [128, 128], replicated, may hold values from -0.5 to 0.5
- dist_weight: bfloat16 [512, 64], P('dp'), parts along dimension 0, may hold values from -1 to 1
- dist_bias: float32 [64], replicated, may hold values from -4 to 4
Outputs:
- pair_out: bfloat16 [1024, 256, 128], P(('dp', 'row', 'chan')), parts along dimension 0
- grad_pair: float32 [1024, 256, 128], P(('dp', 'row', 'chan')), parts along dimension 0
- grad_weight: float32 [512, 64], P('dp'), parts along dimension 0
- loss: float32 [4], P('dp'), parts along dimension 0
The draws below stay inside these ranges and needn't reach their ends.
There are 4 independent parts, one for each index of `dp`. The reference program is written for one: setup_inputs(seed, part) draws one part's arguments, and reference() takes and returns one part's arrays. A program takes and returns all parts, laid end to end along the dimension named above; an argument that names none is the same for every part. Nothing has to cross between parts.
Inputs may be any that keep to these rules, and one draw needn't show every extreme that they name: chain ids never fall along the tokens.
All inputs are finite; a program needn't handle non-finite values. No bound on the sum of `pair_mask` on one device may be relied on, other than what follows from the above.
Results may differ from the reference program's by a relative error of at most 0.007.
Values may be sent and summed in bfloat16 or wider, within the bound.
No kernel may reach another device: no remote copies, remote signals or barrier semaphores. Data moves between devices by JAX's collectives and lax.ppermute only.
A program may use at most 64 MiB of HBM per device.

```python
import math
import jax
import jax.numpy as jnp
import numpy as np
from jax import lax

PAIR_WIDTH = 128
TRI_WIDTH = 128
DIST_BINS = 64
TOKENS = 256


def dist_columns(key):
    noise = jax.random.normal(jax.random.fold_in(key, 7), (PAIR_WIDTH, DIST_BINS), jnp.float32)
    return (noise * PAIR_WIDTH ** (-0.5)).astype(jnp.bfloat16).astype(jnp.float32)


def draw_dist_weight(key, part):
    columns = dist_columns(key)
    return columns.astype(jnp.bfloat16)


def draw_pair(key, part):
    key = jax.random.fold_in(key, 3)
    base = jnp.clip(jax.random.normal(key, (TOKENS, TOKENS, PAIR_WIDTH), jnp.float32), -6.0, 6.0)
    return base.astype(jnp.bfloat16)


def place_ends(result, key, least, high):
    spot = [jax.random.randint(jax.random.fold_in(key, axis), (), 0, length) for axis, length in enumerate(result.shape)]
    longest = result.shape.index(max(result.shape))
    beside = spot[:longest] + [(spot[longest] + 1) % result.shape[longest]] + spot[longest + 1:]
    return result.at[tuple(spot)].set(least).at[tuple(beside)].set(high)


def split_up(number_of, total, limit, slope):
    loads = [(1 << 20) // math.isqrt(rank ** slope) + 1 for rank in range(2, number_of + 1)]
    rest, given = total - limit - (number_of - 1), [1] * (number_of - 1)
    while rest > 0:
        movable = [i for i in range(number_of - 1) if given[i] < limit]
        pool, left = sum([loads[i] for i in movable]), rest
        for i in movable:
            addition = min(limit - given[i], max(1, left * loads[i] // pool), rest)
            given[i] = given[i] + addition
            rest = rest - addition
    return np.array([limit] + given)


def ragged_sizes(own_key, number_of, total, most, slope):
    if number_of == 2:
        one = jax.random.randint(own_key, (), max(1, total - most), min(most, total - 1) + 1)
        return jnp.stack([one, total - one])
    lengths = jnp.asarray(split_up(number_of, total, most, slope), jnp.int32)
    pairs = (number_of - 1) // 2
    giver, taker = lengths[1:1 + 2 * pairs:2], lengths[2:2 + 2 * pairs:2]
    room = jnp.minimum(giver - 1, most - taker)
    passed = jax.random.randint(jax.random.fold_in(own_key, 1), (pairs,), 0, 1 << 20) % (room + 1)
    lengths = lengths.at[1:1 + 2 * pairs:2].set(giver - passed).at[2:2 + 2 * pairs:2].set(taker + passed)
    return lengths[jax.random.permutation(jax.random.fold_in(own_key, 2), number_of)]


def centred(key, shape, deviation, limit, held_as=jnp.bfloat16):
    entries = jax.random.normal(key, shape, jnp.float32) * deviation
    return jnp.minimum(jnp.maximum(entries, -limit), limit).astype(held_as)


def setup_inputs(seed: int = 0, part: int = 0) -> dict:
    splits = jax.random.split(jax.random.key(seed), 14)
    own_keys = jax.random.split(jax.random.fold_in(splits[13], part), 14)
    pair = draw_pair(jax.random.fold_in(jax.random.fold_in(splits[13], part), 71), part)
    chain = jnp.searchsorted(jnp.cumsum(ragged_sizes(own_keys[1], 5, TOKENS, TOKENS // 3, 0)), jnp.arange(TOKENS), side="right").astype(jnp.int32)
    targets = place_ends(jax.random.randint(own_keys[2], (TOKENS, TOKENS), 0, DIST_BINS), jax.random.fold_in(own_keys[2], 1), 0, DIST_BINS - 1).astype(jnp.int32)
    pair_mask = place_ends((jax.random.randint(own_keys[3], (TOKENS, TOKENS), 0, 8) < 7).astype(jnp.int32), jax.random.fold_in(own_keys[3], 1), 0, 1)
    ln_in_gain = jnp.clip(1.0 + 0.1 * jax.random.normal(splits[4], (PAIR_WIDTH,), jnp.float32), 0.5, 1.5)
    ln_in_bias = centred(splits[5], (PAIR_WIDTH,), 0.5, 3.0, jnp.float32)
    in_weight = centred(splits[6], (PAIR_WIDTH, 4 * TRI_WIDTH), PAIR_WIDTH ** -0.5, 0.5)
    out_gate_weight = centred(splits[7], (PAIR_WIDTH, PAIR_WIDTH), PAIR_WIDTH ** -0.5, 0.5)
    ln_out_gain = jnp.clip(1.0 + 0.1 * jax.random.normal(splits[8], (TRI_WIDTH,), jnp.float32), 0.5, 1.5)
    ln_out_bias = centred(splits[9], (TRI_WIDTH,), 0.5, 3.0, jnp.float32)
    out_weight = centred(splits[10], (TRI_WIDTH, PAIR_WIDTH), TRI_WIDTH ** -0.5, 0.5)
    dist_weight = draw_dist_weight(jax.random.fold_in(jax.random.fold_in(splits[13], part), 71), part)
    dist_bias = centred(splits[12], (DIST_BINS,), 1.0, 4.0, jnp.float32)
    return {"pair": pair, "chain": chain, "targets": targets, "pair_mask": pair_mask, "ln_in_gain": ln_in_gain, "ln_in_bias": ln_in_bias, "in_weight": in_weight, "out_gate_weight": out_gate_weight, "ln_out_gain": ln_out_gain, "ln_out_bias": ln_out_bias, "out_weight": out_weight, "dist_weight": dist_weight, "dist_bias": dist_bias}


def layer_norm(values, gain, bias, axis):
    center = lax.optimization_barrier(jnp.mean(values, axis=axis, keepdims=True))
    spread = lax.optimization_barrier(jnp.mean(jnp.square(values - center), axis=axis, keepdims=True))
    return (values - center) * lax.rsqrt(spread + 1e-05) * gain + bias

def reference(pair, chain, targets, pair_mask, ln_in_gain, ln_in_bias, in_weight, out_gate_weight, ln_out_gain, ln_out_bias, out_weight, dist_weight, dist_bias):
    tokens = pair.shape[0]
    pair_full = pair.astype(jnp.float32)
    normed = layer_norm(pair_full, ln_in_gain, ln_in_bias, -1).astype(jnp.bfloat16)
    flat = normed.reshape(tokens * tokens, PAIR_WIDTH)
    proj = jnp.dot(flat, in_weight, preferred_element_type=jnp.float32).reshape(tokens, tokens, 4 * TRI_WIDTH)
    maskf = pair_mask.astype(jnp.float32)[:, :, None]
    projected = (proj[:, :, :2 * TRI_WIDTH] * jax.nn.sigmoid(proj[:, :, 2 * TRI_WIDTH:]) * maskf).astype(jnp.bfloat16)
    left = projected[:, :, :TRI_WIDTH].astype(jnp.float32)
    right = projected[:, :, TRI_WIDTH:].astype(jnp.float32)
    mixed = jnp.einsum('ikh,jkh->ijh', left, right)
    hidden_norm = layer_norm(mixed, ln_out_gain, ln_out_bias, -1).astype(jnp.bfloat16)
    gating = jax.nn.sigmoid(jnp.dot(flat, out_gate_weight, preferred_element_type=jnp.float32))
    update = jnp.dot(hidden_norm.reshape(tokens * tokens, TRI_WIDTH), out_weight, preferred_element_type=jnp.float32)
    pair_out = (pair_full.reshape(tokens * tokens, PAIR_WIDTH) + gating * update).astype(jnp.bfloat16)
    q_all = jnp.dot(pair_out, dist_weight, preferred_element_type=jnp.float32).reshape(tokens, tokens, DIST_BINS)
    logits = q_all + jnp.transpose(q_all, (1, 0, 2)) + dist_bias
    log_probs = jax.nn.log_softmax(logits, axis=-1)
    onehot = (targets[:, :, None] == jnp.arange(DIST_BINS, dtype=jnp.int32)[None, None, :]).astype(jnp.float32)
    weight = pair_mask.astype(jnp.float32) * (1.0 + (chain[:, None] != chain[None, :]).astype(jnp.float32))
    summed = jnp.sum(weight * -lax.optimization_barrier(jnp.sum(onehot * log_probs, axis=-1)))
    loss = (summed / (tokens * tokens)).reshape(1)
    gradient = weight[:, :, None] * (jnp.exp(log_probs) - onehot)
    grad_sym = (gradient + jnp.transpose(gradient, (1, 0, 2))).reshape(tokens * tokens, DIST_BINS)
    grad_pair = jnp.dot(grad_sym, dist_weight.astype(jnp.float32).T, precision=lax.Precision.HIGHEST).reshape(tokens, tokens, PAIR_WIDTH)
    grad_weight = jnp.dot(pair_out.astype(jnp.float32).T, grad_sym, precision=lax.Precision.HIGHEST) / tokens
    return (pair_out.reshape(tokens, tokens, PAIR_WIDTH), grad_pair, grad_weight, loss)
```

```python
import jax
import jax.numpy as jnp
from jax import lax
from jax.sharding import Mesh
from jax.sharding import PartitionSpec as P

EVERY = ("zhi", "core", "y", "zlo", "x")
GROUP = ("y", "zlo", "x")
PLANE = ("y", "x")


def layer_norm(values, gain, bias, axis):
    center = jnp.mean(values, axis=axis, keepdims=True)
    spread = jnp.mean(jnp.square(values - center), axis=axis, keepdims=True)
    return (values - center) * lax.rsqrt(spread + 1e-05) * gain + bias


def group_sum(values, axes, peers):
    copies = jnp.broadcast_to(values[None], (peers,) + values.shape)
    return jnp.sum(lax.all_to_all(copies, axes, 0, 0, tiled=True), axis=0)


def on_device(
    pair,
    chain,
    targets,
    pair_mask,
    ln_in_gain,
    ln_in_bias,
    in_weight,
    out_gate_weight,
    ln_out_gain,
    ln_out_bias,
    out_weight,
    dist_weight,
    dist_bias,
):
    tokens = 256
    bf16, f32 = jnp.bfloat16, jnp.float32
    flat = pair.reshape(512, 128)
    normed = layer_norm(flat.astype(f32), ln_in_gain, ln_in_bias, -1).astype(bf16)
    proj = jnp.einsum("cm,tc->mt", in_weight, normed, preferred_element_type=f32)
    maskf = pair_mask.astype(f32).reshape(1, 512)
    projected = (proj[:256] * jax.nn.sigmoid(proj[256:]) * maskf).astype(bf16)
    pair_part = pair.reshape(2, 128, 2, 128).transpose(1, 2, 0, 3).reshape(128, 4, 128)
    marks = jnp.stack([targets, pair_mask]).reshape(2, 2, 128, 2).transpose(2, 0, 3, 1)
    marks = jnp.pad(marks.reshape(128, 1, 8).astype(bf16), ((0, 0), (0, 3), (0, 120)))
    send = jnp.concatenate(
        [projected[:128].reshape(128, 4, 128), projected[128:].reshape(128, 4, 128), pair_part, marks], axis=1
    )
    got = lax.all_to_all(send, GROUP, 0, 0, tiled=True)
    a = got[:, :4].reshape(256, 256)
    b = got[:, 4:8].reshape(256, 256)
    mixed = jnp.einsum("ik,jk->ij", a, b, preferred_element_type=f32).astype(bf16)
    mirrored = jnp.einsum("jk,ik->ji", b, a, preferred_element_type=f32).astype(bf16)
    send2 = jnp.concatenate(
        [mixed.reshape(128, 4, 128), mirrored.reshape(128, 4, 128)], axis=1
    )
    got2 = lax.all_to_all(send2, GROUP, 0, 0, tiled=True)
    pair_back = got[:, 8:12].reshape(128, 2, 2, 128).transpose(1, 0, 2, 3).reshape(512, 128)
    marks_back = got[:, 12, :8].reshape(128, 2, 2, 2).transpose(1, 2, 0, 3).reshape(2, 512)
    targets_back = marks_back[0].astype(jnp.int32)
    mask_back = marks_back[1].astype(f32)
    both = jnp.concatenate([flat, pair_back], axis=0).astype(f32)
    normed_back = layer_norm(pair_back.astype(f32), ln_in_gain, ln_in_bias, -1).astype(bf16)
    normed_both = jnp.concatenate([normed, normed_back], axis=0)
    gating = jax.nn.sigmoid(jnp.dot(normed_both, out_gate_weight, preferred_element_type=f32))
    hidden = got2.astype(f32)
    hidden_norm = layer_norm(
        hidden, ln_out_gain[:, None, None], ln_out_bias[:, None, None], 0
    ).astype(bf16)
    update = jnp.einsum(
        "ht,hd->td", hidden_norm.reshape(128, 1024), out_weight, preferred_element_type=f32
    )
    updated = (both + gating * update).astype(bf16)
    q = jnp.einsum("cb,tc->bt", dist_weight, updated, preferred_element_type=f32)
    logits = q[:, :512] + q[:, 512:] + dist_bias[:, None]
    log_probs = jax.nn.log_softmax(logits, axis=0)
    bins = jnp.arange(64, dtype=jnp.int32)[:, None]
    onehot = (targets.reshape(1, 512) == bins).astype(f32)
    onehot_back = (targets_back.reshape(1, 512) == bins).astype(f32)
    place = lax.axis_index(GROUP) * 2
    own_chain = lax.dynamic_slice_in_dim(chain, place, 2)
    factor = (1.0 + (own_chain[:, None] != chain[None, :]).astype(f32)).reshape(1, 512)
    weight = maskf * factor
    weight_back = mask_back.reshape(1, 512) * factor
    partial_loss = jnp.sum(weight * -jnp.sum(onehot * log_probs, axis=0, keepdims=True))
    probs = jnp.exp(log_probs)
    grad_sym = weight * (probs - onehot) + weight_back * (probs - onehot_back)
    own = updated[:512]
    grad_weight = jnp.einsum(
        "bt,tc->bc", grad_sym, own.astype(f32), precision=lax.Precision.HIGHEST
    )
    grad_pair = jnp.einsum(
        "bt,cb->tc", grad_sym, dist_weight.astype(f32), precision=lax.Precision.HIGHEST
    )
    loss_row = jnp.pad(jnp.broadcast_to(partial_loss, (1, 128)), ((0, 7), (0, 0)))
    total = jnp.concatenate([grad_weight, loss_row], axis=0)
    total = group_sum(total, PLANE, 16)
    total = group_sum(total, "zlo", 8)
    return (
        own.reshape(2, 256, 128),
        grad_pair.reshape(2, 256, 128),
        jnp.swapaxes(total[:64], 0, 1) / tokens,
        (total[64, :1] / (tokens * tokens)).reshape(1),
    )


def solution(mesh):
    fine = Mesh(mesh.devices.reshape(2, 2, 4, 8, 4), EVERY)
    part = ("zhi", "core")
    in_specs = (
        P(EVERY, None, None),
        P(part),
        P(EVERY, None),
        P(EVERY, None),
        P(),
        P(),
        P(),
        P(),
        P(),
        P(),
        P(),
        P(part, None),
        P(),
    )
    out_specs = (
        P(EVERY, None, None),
        P(EVERY, None, None),
        P(part, None),
        P(part),
    )
    return jax.shard_map(
        on_device, mesh=fine, in_specs=in_specs, out_specs=out_specs, check_vma=False
    )
```

```python
import jax
import jax.numpy as jnp
from jax import lax
from jax.experimental import pallas as pl
from jax.experimental.pallas import tpu as pltpu
from jax.sharding import Mesh
from jax.sharding import PartitionSpec as P

EVERY = ("zhi", "core", "y", "zlo", "x")
GROUP = ("y", "zlo", "x")
PLANE = ("y", "x")
BF16, F32 = jnp.bfloat16, jnp.float32
TN = (((0,), (0,)), ((), ()))
NT = (((1,), (1,)), ((), ()))
NN = (((1,), (0,)), ((), ()))
TT = (((0,), (1,)), ((), ()))


def dot(left, right, dims):
    return lax.dot_general(left, right, dims, preferred_element_type=F32)


def norm_lanes(values, gain, bias):
    center = jnp.mean(values, axis=1, keepdims=True)
    spread = jnp.mean(jnp.square(values - center), axis=1, keepdims=True)
    return (values - center) * lax.rsqrt(spread + 1e-05) * gain + bias


def picker(parity):
    rows = lax.broadcasted_iota(jnp.int32, (128, 256), 0)
    columns = lax.broadcasted_iota(jnp.int32, (128, 256), 1)
    return (columns == 2 * rows + parity).astype(F32).astype(BF16)


def pack_kernel(pair, targets, mask, gain, bias, in_weight, send, flat, marks, rows):
    flat[...] = pair[...].astype(F32)
    maskf = mask[...].astype(F32)
    for r in range(2):
        normed = norm_lanes(flat[r * 256 : (r + 1) * 256, :], gain[...], bias[...]).astype(BF16)
        proj = dot(in_weight[...], normed, TT)
        projected = proj[:256] * jax.nn.sigmoid(proj[256:]) * maskf[r : r + 1]
        for side in range(2):
            for half in range(2):
                rows[pl.ds(side * 4 + r * 2 + half, 128, stride=16), :] = projected[
                    side * 128 : (side + 1) * 128, half * 128 : (half + 1) * 128
                ]
    marks[...] = jnp.zeros_like(marks)
    for ir in range(2):
        marks[ir, 4 * ir : 4 * ir + 2, :] = targets[...].astype(F32)
        marks[ir, 4 * ir + 2 : 4 * ir + 4, :] = maskf
        for jr in range(2):
            rows[pl.ds(8 + ir * 2 + jr, 128, stride=16), :] = flat[
                pl.ds(jr * 256 + ir, 128, stride=2), :
            ]
    rows[pl.ds(12, 128, stride=16), :] = dot(picker(0), marks[0].astype(BF16), NT) + dot(
        picker(1), marks[1].astype(BF16), NT
    )
    for row in range(13, 16):
        rows[pl.ds(row, 128, stride=16), :] = jnp.zeros((128, 128), F32)
    send[...] = rows[...].astype(BF16)


def triangle_kernel(got, send, rows, products):
    rows[...] = got[...].astype(F32)
    sides = []
    for side in range(2):
        for r in range(2):
            halves = [rows[pl.ds(side * 4 + r * 2 + half, 128, stride=16), :] for half in range(2)]
            sides.append(jnp.concatenate(halves, axis=1).astype(BF16))
    for r in range(2):
        for jr in range(2):
            products[pl.ds(r * 2 + jr, 128, stride=8), :] = dot(sides[r], sides[2 + jr], NT)
            products[pl.ds(4 + r * 2 + jr, 128, stride=8), :] = dot(sides[2 + r], sides[jr], NT)
    send[...] = products[...].astype(BF16)


def gate_kernel(
    pair, got, targets, mask, factor, gain, bias, gate_weight, base, gate, marks, flat, rows, own
):
    flat[...] = pair[...].astype(F32)
    rows[...] = got[...].astype(F32)
    for r in range(2):
        for jr in range(2):
            block = r * 2 + jr
            base[block * 128 : (block + 1) * 128, :] = flat[pl.ds(r * 256 + jr, 128, stride=2), :]
            base[(4 + block) * 128 : (5 + block) * 128, :] = rows[
                pl.ds(8 + block, 128, stride=16), :
            ]
    normed = norm_lanes(base[...], gain[...], bias[...]).astype(BF16)
    gate[...] = jax.nn.sigmoid(dot(normed, gate_weight[...], NN))
    own[...] = jnp.zeros_like(own)
    own[0:2, :] = targets[...].astype(F32)
    own[2:4, :] = mask[...].astype(F32)
    own[4:6, :] = factor[...]
    back = jnp.transpose(rows[pl.ds(12, 128, stride=16), :])
    for jr in range(2):
        picked = dot(own[...].astype(BF16), picker(jr), NT)
        for r in range(2):
            block = r * 2 + jr
            weight = picked[4 + r : 5 + r]
            at = r * 4 + jr
            marks[block : block + 1, :] = picked[2 + r : 3 + r] * weight
            marks[4 + block : 5 + block, :] = back[at + 2 : at + 3] * weight
            marks[8 + block : 9 + block, :] = picked[r : r + 1]
            marks[12 + block : 13 + block, :] = back[at : at + 1]


def head_kernel(
    got, base, gate, marks, gain, bias, out_weight, dist_weight, dist_bias, updated, grad, total, hidden
):
    values = got[...].astype(F32).reshape(128, 8, 128)
    hidden[...] = got[...].astype(F32)
    center = jnp.mean(values, axis=0)
    spread = jnp.mean(jnp.square(values - center[None]), axis=0)
    scale = lax.rsqrt(spread + 1e-05)
    q = []
    kept = []
    for block in range(8):
        here = hidden[pl.ds(block, 128, stride=8), :]
        normed = (here - center[block : block + 1]) * scale[block : block + 1]
        normed = (normed * gain[...] + bias[...]).astype(BF16)
        update = dot(normed, out_weight[...], TN)
        at = pl.ds(block * 128, 128)
        sums = (base[at, :] + gate[at, :] * update).astype(BF16)
        q.append(dot(dist_weight[...], sums, TT))
        if block < 4:
            kept.append(sums)
            updated[at, :] = sums
    bins = lax.broadcasted_iota(jnp.int32, (64, 128), 0).astype(F32)
    losses = jnp.zeros((1, 128), F32)
    weights = jnp.zeros((64, 128), F32)
    for block in range(4):
        logits = q[block] + q[4 + block] + dist_bias[...]
        shifted = logits - jnp.max(logits, axis=0, keepdims=True)
        powers = jnp.exp(shifted)
        norms = jnp.sum(powers, axis=0, keepdims=True)
        log_probs = shifted - jnp.log(norms)
        probs = powers / norms
        row = lambda at: marks[at + block : at + block + 1, :]
        onehot = (bins == row(8)).astype(F32)
        onehot_back = (bins == row(12)).astype(F32)
        losses = losses - row(0) * jnp.sum(onehot * log_probs, axis=0, keepdims=True)
        slope = row(0) * (probs - onehot) + row(4) * (probs - onehot_back)
        grad[block * 64 : (block + 1) * 64, :] = slope
        high = slope.astype(BF16)
        low = (slope - high.astype(F32)).astype(BF16)
        weights = weights + dot(high, kept[block], NN) + dot(low, kept[block], NN)
    loss = jnp.broadcast_to(jnp.sum(losses, axis=1, keepdims=True), (8, 128))
    for peer in range(16):
        total[peer * 72 : peer * 72 + 64, :] = weights
        total[peer * 72 + 64 : peer * 72 + 72, :] = loss


def output_kernel(updated, grad, dist_weight, pair_out, grad_pair, rows):
    for r in range(2):
        for jr in range(2):
            block = r * 2 + jr
            at = pl.ds(r * 256 + jr, 128, stride=2)
            rows[at, :] = updated[block * 128 : (block + 1) * 128, :].astype(F32)
            slope = grad[block * 64 : (block + 1) * 64, :]
            high = slope.astype(BF16)
            rest = slope - high.astype(F32)
            middle = rest.astype(BF16)
            grad_pair[at, :] = dot(high, dist_weight[...], TT) + dot(middle, dist_weight[...], TT)
    pair_out[...] = rows[...].astype(BF16)


def run(kernel, outs, scratch, args, flops=10_000_000):
    shapes = [jax.ShapeDtypeStruct(s, d) for s, d in outs]
    moved = sum(x.size * x.dtype.itemsize for x in args)
    return pl.pallas_call(
        kernel,
        out_shape=shapes,
        scratch_shapes=[pltpu.VMEM(s, d) for s, d in scratch],
        compiler_params=pltpu.CompilerParams(vmem_limit_bytes=24 * 1024 * 1024),
        cost_estimate=pl.CostEstimate(flops=flops, bytes_accessed=moved, transcendentals=0),
    )(*args)


def pack(pair, targets, mask, gain, bias, in_weight):
    scratch = [((512, 128), F32), ((2, 128, 256), F32), ((2048, 128), F32)]
    return run(pack_kernel, [((2048, 128), BF16)], scratch, (pair, targets, mask, gain, bias, in_weight))[0]


def triangle(got):
    scratch = [((2048, 128), F32), ((1024, 128), F32)]
    return run(triangle_kernel, [((1024, 128), BF16)], scratch, (got,))[0]


def gates(pair, got, targets, mask, factor, gain, bias, gate_weight):
    outs = [((1024, 128), F32), ((1024, 128), F32), ((16, 128), F32)]
    scratch = [((512, 128), F32), ((2048, 128), F32), ((16, 256), F32)]
    return run(gate_kernel, outs, scratch, (pair, got, targets, mask, factor, gain, bias, gate_weight))


def head(*args):
    outs = [((512, 128), BF16), ((256, 128), F32), ((1152, 128), F32)]
    return run(head_kernel, outs, [((1024, 128), F32)], args)


def outputs(updated, grad, dist_weight):
    outs = [((512, 128), BF16), ((512, 128), F32)]
    return run(output_kernel, outs, [((512, 128), F32)], (updated, grad, dist_weight))


def exchange(values, axes):
    return lax.all_to_all(values, axes, 0, 0, tiled=True)


def on_device(
    pair,
    chain,
    targets,
    pair_mask,
    ln_in_gain,
    ln_in_bias,
    in_weight,
    out_gate_weight,
    ln_out_gain,
    ln_out_bias,
    out_weight,
    dist_weight,
    dist_bias,
):
    tokens = 256
    flat = pair.reshape(512, 128)
    gain, bias = ln_in_gain.reshape(1, 128), ln_in_bias.reshape(1, 128)
    place = lax.axis_index(GROUP) * 2
    own_chain = lax.dynamic_slice_in_dim(chain, place, 2)
    factor = 1.0 + (own_chain[:, None] != chain[None, :]).astype(F32)

    send = pack(flat, targets, pair_mask, gain, bias, in_weight)
    got = exchange(send.reshape(128, 16, 128), GROUP).reshape(2048, 128)
    products = triangle(got)
    base, gate, marks = gates(flat, got, targets, pair_mask, factor, gain, bias, out_gate_weight)
    hidden = exchange(products.reshape(128, 8, 128), GROUP).reshape(1024, 128)
    updated, grad, total = head(
        hidden,
        base,
        gate,
        marks,
        ln_out_gain.reshape(128, 1),
        ln_out_bias.reshape(128, 1),
        out_weight,
        dist_weight,
        dist_bias.reshape(64, 1),
    )
    total = jnp.sum(exchange(total.reshape(16, 72, 128), PLANE), axis=0)
    pair_out, grad_pair = outputs(updated, grad, dist_weight)
    total = exchange(jnp.broadcast_to(total[None], (8, 72, 128)), "zlo")
    total = jnp.sum(total, axis=0)
    return (
        pair_out.reshape(2, 256, 128),
        grad_pair.reshape(2, 256, 128),
        jnp.swapaxes(total[:64], 0, 1) / tokens,
        (total[64, :1] / (tokens * tokens)).reshape(1),
    )


def solution(mesh):
    fine = Mesh(mesh.devices.reshape(2, 2, 4, 8, 4), EVERY)
    part = ("zhi", "core")
    in_specs = (
        P(EVERY, None, None),
        P(part),
        P(EVERY, None),
        P(EVERY, None),
        P(),
        P(),
        P(),
        P(),
        P(),
        P(),
        P(),
        P(part, None),
        P(),
    )
    out_specs = (
        P(EVERY, None, None),
        P(EVERY, None, None),
        P(part, None),
        P(part),
    )
    return jax.shard_map(
        on_device, mesh=fine, in_specs=in_specs, out_specs=out_specs, check_vma=False
    )
```

```python
import jax
import jax.numpy as jnp
from jax import lax
from jax.experimental import pallas as pl
from jax.experimental.pallas import tpu as pltpu
from jax.sharding import Mesh
from jax.sharding import PartitionSpec as P

EVERY = ("zhi", "core", "y", "zlo", "x")
GROUP = ("y", "zlo", "x")
PLANE = ("y", "x")
BF16, F32 = jnp.bfloat16, jnp.float32
TN = (((0,), (0,)), ((), ()))
NT = (((1,), (1,)), ((), ()))
NN = (((1,), (0,)), ((), ()))
TT = (((0,), (1,)), ((), ()))


def dot(left, right, dims):
    return lax.dot_general(left, right, dims, preferred_element_type=F32)


def norm_lanes(values, gain, bias):
    center = jnp.mean(values, axis=1, keepdims=True)
    spread = jnp.mean(jnp.square(values - center), axis=1, keepdims=True)
    return (values - center) * lax.rsqrt(spread + 1e-05) * gain + bias


def picker(parity):
    rows = lax.broadcasted_iota(jnp.int32, (128, 256), 0)
    columns = lax.broadcasted_iota(jnp.int32, (128, 256), 1)
    return (columns == 2 * rows + parity).astype(F32).astype(BF16)


def pack_kernel(
    pair_far, targets_far, mask_far, gain_far, bias_far, weight_far, send,
    pair, targets, mask, gain, bias, in_weight, flat, marks, rows, sems,
):
    far = (targets_far, mask_far, pair_far, gain_far, bias_far, weight_far)
    near = (targets, mask, pair, gain, bias, in_weight)
    copies = [pltpu.make_async_copy(far[n], near[n], sems.at[n]) for n in range(6)]
    for copy in copies:
        copy.start()
    copies[0].wait()
    copies[1].wait()
    maskf = mask[...].astype(F32)
    marks[...] = jnp.zeros_like(marks)
    for ir in range(2):
        marks[ir, 4 * ir : 4 * ir + 2, :] = targets[...].astype(F32)
        marks[ir, 4 * ir + 2 : 4 * ir + 4, :] = maskf
    rows[pl.ds(12, 128, stride=14), :] = dot(picker(0), marks[0].astype(BF16), NT) + dot(
        picker(1), marks[1].astype(BF16), NT
    )
    rows[pl.ds(13, 128, stride=14), :] = jnp.zeros((128, 128), F32)
    copies[2].wait()
    flat[...] = pair[...].astype(F32)
    for ir in range(2):
        for jr in range(2):
            rows[pl.ds(8 + ir * 2 + jr, 128, stride=14), :] = flat[
                pl.ds(jr * 256 + ir, 128, stride=2), :
            ]
    for copy in copies[3:]:
        copy.wait()
    for r in range(2):
        normed = norm_lanes(flat[r * 256 : (r + 1) * 256, :], gain[...], bias[...]).astype(BF16)
        proj = dot(in_weight[...], normed, TT)
        projected = proj[:256] * jax.nn.sigmoid(proj[256:]) * maskf[r : r + 1]
        for side in range(2):
            for half in range(2):
                rows[pl.ds(side * 4 + r * 2 + half, 128, stride=14), :] = projected[
                    side * 128 : (side + 1) * 128, half * 128 : (half + 1) * 128
                ]
    send[...] = rows[...].astype(BF16)


def triangle_kernel(got, send, rows, products):
    rows[...] = got[...].astype(F32)
    sides = []
    for side in range(2):
        for r in range(2):
            halves = [rows[pl.ds(side * 4 + r * 2 + half, 128, stride=14), :] for half in range(2)]
            sides.append(jnp.concatenate(halves, axis=1).astype(BF16))
    for r in range(2):
        for jr in range(2):
            products[pl.ds(r * 2 + jr, 128, stride=8), :] = dot(sides[r], sides[2 + jr], NT)
            products[pl.ds(4 + r * 2 + jr, 128, stride=8), :] = dot(sides[2 + r], sides[jr], NT)
    send[...] = products[...].astype(BF16)


def gate_kernel(
    pair, got, targets, mask, chain, place, gain, bias, gate_weight, base, gate, marks, flat, rows, own
):
    flat[...] = pair[...].astype(F32)
    rows[...] = got[...].astype(F32)
    for r in range(2):
        for jr in range(2):
            block = r * 2 + jr
            base[block * 128 : (block + 1) * 128, :] = flat[pl.ds(r * 256 + jr, 128, stride=2), :]
            base[(4 + block) * 128 : (5 + block) * 128, :] = rows[
                pl.ds(8 + block, 128, stride=14), :
            ]
    normed = norm_lanes(base[...], gain[...], bias[...]).astype(BF16)
    gate[...] = jax.nn.sigmoid(dot(normed, gate_weight[...], NN))
    own[...] = jnp.zeros_like(own)
    own[0:2, :] = targets[...].astype(F32)
    own[2:4, :] = mask[...].astype(F32)
    columns = lax.broadcasted_iota(jnp.int32, (1, 256), 1)
    for r in range(2):
        here = jnp.sum(jnp.where(columns == place[0] + r, chain[...], 0), axis=1, keepdims=True)
        own[4 + r : 5 + r, :] = 1.0 + (chain[...] != here).astype(F32)
    back = jnp.transpose(rows[pl.ds(12, 128, stride=14), :])
    for jr in range(2):
        picked = dot(own[...].astype(BF16), picker(jr), NT)
        for r in range(2):
            block = r * 2 + jr
            weight = picked[4 + r : 5 + r]
            at = r * 4 + jr
            marks[block : block + 1, :] = picked[2 + r : 3 + r] * weight
            marks[4 + block : 5 + block, :] = back[at + 2 : at + 3] * weight
            marks[8 + block : 9 + block, :] = picked[r : r + 1]
            marks[12 + block : 13 + block, :] = back[at : at + 1]


def spread_sums(weights, loss, peers):
    row = lax.broadcasted_iota(jnp.int32, (8, 128), 0)
    high = loss.astype(BF16).astype(F32)
    terms = jnp.where(row == 0, high, jnp.where(row == 1, loss - high, 0.0))
    return jnp.concatenate([weights, terms] * peers, axis=0).astype(BF16)


def add_sums(got, peers):
    sums = jnp.sum(got[...].astype(F32).reshape(peers, 72, 128), axis=0)
    return sums[:64], sums[64:65, 0:1] + sums[65:66, 0:1]


def middle_kernel(got, send):
    weights, loss = add_sums(got, 16)
    send[...] = spread_sums(weights, loss, 8)


def last_kernel(got, grad_weight, loss):
    weights, total = add_sums(got, 8)
    grad_weight[...] = weights * (1.0 / 256)
    loss[0] = total[0, 0] * (1.0 / 65536)


def head_kernel(
    got, base, gate, marks, gain, bias, out_weight, dist_weight, dist_bias, updated, grad, total, hidden
):
    values = got[...].astype(F32).reshape(128, 8, 128)
    hidden[...] = got[...].astype(F32)
    gain = jnp.transpose(jnp.broadcast_to(gain[...], (8, 128)))[:, :1]
    bias = jnp.transpose(jnp.broadcast_to(bias[...], (8, 128)))[:, :1]
    dist_bias = jnp.transpose(jnp.broadcast_to(dist_bias[...], (8, 64)))[:, :1]
    center = jnp.mean(values, axis=0)
    spread = jnp.mean(jnp.square(values - center[None]), axis=0)
    scale = lax.rsqrt(spread + 1e-05)
    q = []
    kept = []
    for block in range(8):
        here = hidden[pl.ds(block, 128, stride=8), :]
        normed = (here - center[block : block + 1]) * scale[block : block + 1]
        normed = (normed * gain + bias).astype(BF16)
        update = dot(normed, out_weight[...], TN)
        at = pl.ds(block * 128, 128)
        sums = (base[at, :] + gate[at, :] * update).astype(BF16)
        q.append(dot(dist_weight[...], sums, NT))
        if block < 4:
            kept.append(sums)
            updated[at, :] = sums
    bins = lax.broadcasted_iota(jnp.int32, (64, 128), 0).astype(F32)
    losses = jnp.zeros((1, 128), F32)
    weights = jnp.zeros((64, 128), F32)
    for block in range(4):
        logits = q[block] + q[4 + block] + dist_bias
        shifted = logits - jnp.max(logits, axis=0, keepdims=True)
        powers = jnp.exp(shifted)
        norms = jnp.sum(powers, axis=0, keepdims=True)
        log_probs = shifted - jnp.log(norms)
        probs = powers / norms
        row = lambda at: marks[at + block : at + block + 1, :]
        onehot = (bins == row(8)).astype(F32)
        onehot_back = (bins == row(12)).astype(F32)
        losses = losses - row(0) * jnp.sum(onehot * log_probs, axis=0, keepdims=True)
        slope = row(0) * (probs - onehot) + row(4) * (probs - onehot_back)
        grad[block * 64 : (block + 1) * 64, :] = slope
        high = slope.astype(BF16)
        low = (slope - high.astype(F32)).astype(BF16)
        weights = weights + dot(high, kept[block], NN) + dot(low, kept[block], NN)
    total[...] = spread_sums(weights, jnp.sum(losses, axis=1, keepdims=True), 16)


def output_kernel(updated, grad, dist_weight, pair_out, grad_pair, rows):
    for r in range(2):
        for jr in range(2):
            block = r * 2 + jr
            at = pl.ds(r * 256 + jr, 128, stride=2)
            rows[at, :] = updated[block * 128 : (block + 1) * 128, :].astype(F32)
            slope = grad[block * 64 : (block + 1) * 64, :]
            high = slope.astype(BF16)
            rest = slope - high.astype(F32)
            middle = rest.astype(BF16)
            grad_pair[at, :] = dot(high, dist_weight[...], TN) + dot(middle, dist_weight[...], TN)
    pair_out[...] = rows[...].astype(BF16)


def run(kernel, outs, scratch, args, room=24, **specs):
    shapes = [jax.ShapeDtypeStruct(s, d) for s, d in outs]
    moved = sum(x.size * x.dtype.itemsize for x in args)
    scratch = [pltpu.VMEM(*s) if isinstance(s, tuple) else s for s in scratch]
    return pl.pallas_call(
        kernel,
        out_shape=shapes,
        scratch_shapes=scratch,
        compiler_params=pltpu.CompilerParams(vmem_limit_bytes=room * 1024 * 1024),
        cost_estimate=pl.CostEstimate(flops=10_000_000, bytes_accessed=moved, transcendentals=0),
        **specs,
    )(*args)


VMEM, FAR = pl.BlockSpec(memory_space=pltpu.VMEM), pl.BlockSpec(memory_space=pl.ANY)
SMEM = pl.BlockSpec(memory_space=pltpu.SMEM)


def pack(pair, targets, mask, gain, bias, in_weight):
    scratch = [
        ((512, 128), BF16),
        ((2, 256), jnp.int32),
        ((2, 256), jnp.int32),
        ((1, 128), F32),
        ((1, 128), F32),
        ((128, 512), BF16),
        ((512, 128), F32),
        ((2, 128, 256), F32),
        ((1792, 128), F32),
        pltpu.SemaphoreType.DMA((6,)),
    ]
    args = (pair, targets, mask, gain, bias, in_weight)
    return run(pack_kernel, [((1792, 128), BF16)], scratch, args, 60, in_specs=[FAR] * 6)[0]


def triangle(got):
    scratch = [((1792, 128), F32), ((1024, 128), F32)]
    return run(triangle_kernel, [((1024, 128), BF16)], scratch, (got,))[0]


def gates(*args):
    outs = [((1024, 128), F32), ((1024, 128), F32), ((16, 128), F32)]
    scratch = [((512, 128), F32), ((1792, 128), F32), ((16, 256), F32)]
    return run(gate_kernel, outs, scratch, args, in_specs=[VMEM] * 5 + [SMEM] + [VMEM] * 3)


def head(*args):
    outs = [((512, 128), BF16), ((256, 128), F32), ((1152, 128), BF16)]
    return run(head_kernel, outs, [((1024, 128), F32)], args)


def outputs(updated, grad, dist_weight):
    outs = [((512, 128), BF16), ((512, 128), F32)]
    return run(output_kernel, outs, [((512, 128), F32)], (updated, grad, dist_weight))


def middle(got):
    return run(middle_kernel, [((576, 128), BF16)], [], (got,))[0]


def last(got):
    outs = [((64, 128), F32), ((1,), F32)]
    return run(last_kernel, outs, [], (got,), out_specs=[VMEM, SMEM])


def exchange(values, axes):
    return lax.all_to_all(values, axes, 0, 0, tiled=True)


def on_device(
    pair,
    chain,
    targets,
    pair_mask,
    ln_in_gain,
    ln_in_bias,
    in_weight,
    out_gate_weight,
    ln_out_gain,
    ln_out_bias,
    out_weight,
    dist_weight,
    dist_bias,
):
    flat = pair.reshape(512, 128)
    gain, bias = ln_in_gain.reshape(1, 128), ln_in_bias.reshape(1, 128)
    place = (lax.axis_index(GROUP) * 2).reshape(1)
    dist_weight = jnp.swapaxes(dist_weight, 0, 1)

    send = pack(flat, targets, pair_mask, gain, bias, in_weight)
    got = exchange(send.reshape(128, 7, 2, 128), GROUP).reshape(1792, 128)
    products = triangle(got)
    base, gate, marks = gates(
        flat, got, targets, pair_mask, chain.reshape(1, 256), place, gain, bias, out_gate_weight
    )
    hidden = exchange(products.reshape(128, 8, 128), GROUP).reshape(1024, 128)
    updated, grad, total = head(
        hidden,
        base,
        gate,
        marks,
        ln_out_gain.reshape(1, 128),
        ln_out_bias.reshape(1, 128),
        out_weight,
        dist_weight,
        dist_bias.reshape(1, 64),
    )
    total = middle(exchange(total.reshape(16, 72, 128), PLANE).reshape(1152, 128))
    pair_out, grad_pair = outputs(updated, grad, dist_weight)
    grad_weight, loss = last(exchange(total.reshape(8, 72, 128), "zlo").reshape(576, 128))
    return (
        pair_out.reshape(2, 256, 128),
        grad_pair.reshape(2, 256, 128),
        jnp.swapaxes(grad_weight, 0, 1),
        loss,
    )


def solution(mesh):
    fine = Mesh(mesh.devices.reshape(2, 2, 4, 8, 4), EVERY)
    part = ("zhi", "core")
    in_specs = (
        P(EVERY, None, None),
        P(part),
        P(EVERY, None),
        P(EVERY, None),
        P(),
        P(),
        P(),
        P(),
        P(),
        P(),
        P(),
        P(part, None),
        P(),
    )
    out_specs = (
        P(EVERY, None, None),
        P(EVERY, None, None),
        P(part, None),
        P(part),
    )
    return jax.shard_map(
        on_device, mesh=fine, in_specs=in_specs, out_specs=out_specs, check_vma=False
    )
```

```python
import jax
import jax.numpy as jnp
from jax import lax
from jax.experimental import pallas as pl
from jax.experimental.pallas import tpu as pltpu
from jax.sharding import Mesh
from jax.sharding import PartitionSpec as P

EVERY = ("zhi", "core", "y", "zlo", "x")
GROUP = ("y", "zlo", "x")
PLANE = ("y", "x")
BF16, F32 = jnp.bfloat16, jnp.float32
TN = (((0,), (0,)), ((), ()))
NT = (((1,), (1,)), ((), ()))
NN = (((1,), (0,)), ((), ()))
TT = (((0,), (1,)), ((), ()))


def dot(left, right, dims):
    return lax.dot_general(left, right, dims, preferred_element_type=F32)


def norm_lanes(values, gain, bias):
    center = jnp.mean(values, axis=1, keepdims=True)
    spread = jnp.mean(jnp.square(values - center), axis=1, keepdims=True)
    return (values - center) * lax.rsqrt(spread + 1e-05) * gain + bias


def picker(parity):
    rows = lax.broadcasted_iota(jnp.int32, (128, 256), 0)
    columns = lax.broadcasted_iota(jnp.int32, (128, 256), 1)
    return (columns == 2 * rows + parity).astype(F32).astype(BF16)


def pack_kernel(
    place, pair_far, targets_far, mask_far, gain_far, bias_far, weight_far, send,
    pair, targets, mask, gain, bias, in_weight, flat, marks, rows, sems,
):
    far = (targets_far, mask_far, pair_far, gain_far, bias_far, weight_far)
    near = (targets, mask, pair, gain, bias, in_weight)
    copies = [pltpu.make_async_copy(far[n], near[n], sems.at[n]) for n in range(6)]
    for copy in copies:
        copy.start()
    copies[0].wait()
    copies[1].wait()
    lower = lax.broadcasted_iota(jnp.int32, (128, 128), 0) * 2 <= place[0]
    maskf = mask[...].astype(F32)
    targetsf = targets[...].astype(F32)
    marks[...] = jnp.zeros_like(marks)
    for form, row, jr in ((0, 0, 0), (1, 2, 0), (2, 0, 0), (2, 2, 1)):
        marks[form, row : row + 1, :] = targetsf[jr : jr + 1]
        marks[form, row + 1 : row + 2, :] = maskf[jr : jr + 1]
    rows[pl.ds(10, 128, stride=12), :] = jnp.where(
        lower,
        dot(picker(0), marks[0].astype(BF16), NT) + dot(picker(1), marks[1].astype(BF16), NT),
        dot(picker(1), marks[2].astype(BF16), NT),
    )
    rows[pl.ds(11, 128, stride=12), :] = jnp.zeros((128, 128), F32)
    copies[2].wait()
    flat[...] = pair[...].astype(F32)
    first, second, third = (
        flat[pl.ds(jr * 256 + ir, 128, stride=2), :] for ir, jr in ((0, 0), (1, 0), (1, 1))
    )
    rows[pl.ds(8, 128, stride=12), :] = jnp.where(lower, first, second)
    rows[pl.ds(9, 128, stride=12), :] = jnp.where(lower, second, third)
    for copy in copies[3:]:
        copy.wait()
    for r in range(2):
        normed = norm_lanes(flat[r * 256 : (r + 1) * 256, :], gain[...], bias[...]).astype(BF16)
        proj = dot(in_weight[...], normed, TT)
        projected = proj[:256] * jax.nn.sigmoid(proj[256:]) * maskf[r : r + 1]
        for side in range(2):
            for half in range(2):
                rows[pl.ds(side * 4 + r * 2 + half, 128, stride=12), :] = projected[
                    side * 128 : (side + 1) * 128, half * 128 : (half + 1) * 128
                ]
    send[...] = rows[...].astype(BF16)


def triangle_kernel(got, send, rows, products):
    rows[...] = got[...].astype(F32)
    sides = []
    for side in range(2):
        for r in range(2):
            halves = [rows[pl.ds(side * 4 + r * 2 + half, 128, stride=12), :] for half in range(2)]
            sides.append(jnp.concatenate(halves, axis=1).astype(BF16))
    for r in range(2):
        for jr in range(2):
            products[pl.ds(r * 2 + jr, 128, stride=6), :] = dot(sides[r], sides[2 + jr], NT)
    first, second, third = (
        dot(sides[2 + r], sides[jr], NT) for r, jr in ((0, 0), (1, 0), (1, 1))
    )
    higher = lax.broadcasted_iota(jnp.int32, (128, 128), 1) >= lax.broadcasted_iota(
        jnp.int32, (128, 128), 0
    )
    products[pl.ds(4, 128, stride=6), :] = jnp.where(higher, first, second)
    products[pl.ds(5, 128, stride=6), :] = jnp.where(higher, second, third)
    send[...] = products[...].astype(BF16)


def gate_kernel(
    pair, got, targets, mask, chain, place, gain, bias, gate_weight, out_gain, out_bias, dist_bias,
    base, gate, marks, flat, rows, own,
):
    marks[...] = jnp.zeros((24, 128), F32)
    marks[16:17, :] = out_gain[...]
    marks[17:18, :] = out_bias[...]
    marks[18:19, :64] = dist_bias[...]
    flat[...] = pair[...].astype(F32)
    rows[...] = got[...].astype(F32)
    for block in range(4):
        base[block * 128 : (block + 1) * 128, :] = flat[
            pl.ds(block // 2 * 256 + block % 2, 128, stride=2), :
        ]
    base[512:640, :] = rows[pl.ds(8, 128, stride=12), :]
    base[640:768, :] = rows[pl.ds(9, 128, stride=12), :]
    normed = norm_lanes(base[...], gain[...], bias[...]).astype(BF16)
    gate[...] = jax.nn.sigmoid(dot(normed, gate_weight[...], NN))
    own[...] = jnp.zeros_like(own)
    own[0:2, :] = targets[...].astype(F32)
    own[2:4, :] = mask[...].astype(F32)
    columns = lax.broadcasted_iota(jnp.int32, (1, 256), 1)
    for r in range(2):
        here = jnp.sum(jnp.where(columns == place[0] + r, chain[...], 0), axis=1, keepdims=True)
        own[4 + r : 5 + r, :] = 1.0 + (chain[...] != here).astype(F32)
    even, odd = (dot(own[...].astype(BF16), picker(jr), NT) for jr in range(2))
    back = jnp.transpose(rows[pl.ds(10, 128, stride=12), :])
    lanes = lax.broadcasted_iota(jnp.int32, (1, 128), 1) * 2
    higher, same = lanes >= place[0], lanes == place[0]
    target, valid, factor = (
        (
            jnp.where(higher, even[at : at + 1], even[at + 1 : at + 2]),
            jnp.where(higher, even[at + 1 : at + 2], odd[at + 1 : at + 2]),
            odd[at + 1 : at + 2],
        )
        for at in (0, 2, 4)
    )
    for group in range(2):
        marks[group : group + 1, :] = valid[group] * factor[group]
        marks[3 + group : 4 + group, :] = back[2 * group + 1 : 2 * group + 2] * factor[group]
        marks[9 + group : 10 + group, :] = back[2 * group : 2 * group + 1]
    alone = jnp.where(same, valid[2] * factor[2], 0.0)
    marks[2:3, :] = alone
    marks[5:6, :] = alone
    for group in range(3):
        marks[6 + group : 7 + group, :] = target[group]
    marks[11:12, :] = target[2]
    marks[12:13, :] = jnp.where(same, 0.0, back[1:2] * factor[0])


def message(weights, loss, others):
    row = lax.broadcasted_iota(jnp.int32, (8, 128), 0)
    high = loss.astype(BF16).astype(F32)
    terms = jnp.where(row == 0, high, jnp.where(row == 1, loss - high, 0.0))
    pieces = [piece for other in others for piece in (weights, terms, other)]
    return jnp.concatenate(pieces, axis=0).astype(BF16)


def add_sums(values, peers):
    sums = jnp.sum(values.reshape(peers, values.shape[0] // peers, 128), axis=0)
    return sums[:64], sums[64:65, 0:1] + sums[65:66, 0:1]


def head_kernel(
    got, base, gate, marks, place, out_weight, dist_weight, updated, grad, total, hidden, slopes
):
    hidden[...] = got[...].astype(F32)
    columns = jnp.transpose(marks[16:24, :])
    gain, bias, dist_bias = columns[:, 0:1], columns[:, 1:2], columns[:64, 2:3]
    q = []
    kept = []
    for block in range(6):
        here = hidden[pl.ds(block, 128, stride=6), :]
        center = jnp.mean(here, axis=0, keepdims=True)
        spread = jnp.mean(jnp.square(here - center), axis=0, keepdims=True)
        normed = (here - center) * lax.rsqrt(spread + 1e-05)
        normed = (normed * gain + bias).astype(BF16)
        update = dot(normed, out_weight[...], TN)
        at = pl.ds(block * 128, 128)
        sums = (base[at, :] + gate[at, :] * update).astype(BF16)
        q.append(dot(dist_weight[...], sums, NT))
        kept.append(sums)
        if block < 4:
            updated[at, :] = sums
    lanes = lax.broadcasted_iota(jnp.int32, (64, 128), 1) * 2
    higher = lanes >= place[0]
    pairs = (
        jnp.where(higher, q[0], q[2]) + q[4],
        jnp.where(higher, q[2], q[3]) + q[5],
        q[3] + q[3],
    )
    bins = lax.broadcasted_iota(jnp.int32, (64, 128), 0).astype(F32)
    row = lambda at: marks[at : at + 1, :]
    losses = jnp.zeros((1, 128), F32)
    slope = []
    for group in range(3):
        logits = pairs[group] + dist_bias
        shifted = logits - jnp.max(logits, axis=0, keepdims=True)
        powers = jnp.exp(shifted)
        norms = jnp.sum(powers, axis=0, keepdims=True)
        log_probs = shifted - jnp.log(norms)
        probs = powers / norms
        onehot = (bins == row(6 + group)).astype(F32)
        onehot_back = (bins == row(9 + group)).astype(F32)
        losses = losses - row(group) * jnp.sum(onehot * log_probs, axis=0, keepdims=True)
        if group < 2:
            counted = row(12) if group == 0 else row(4)
            losses = losses - counted * jnp.sum(onehot_back * log_probs, axis=0, keepdims=True)
        slope.append(row(group) * (probs - onehot) + row(3 + group) * (probs - onehot_back))
    blocks = (
        (0, jnp.where(higher, slope[0], 0.0)),
        (2, jnp.where(higher, slope[1], slope[0])),
        (3, jnp.where(higher, 0.0, slope[1]) + slope[2]),
        (4, jnp.where(lanes == place[0], 0.0, slope[0])),
        (5, slope[1]),
    )
    weights = jnp.zeros((64, 128), F32)
    for block, values in blocks:
        high = values.astype(BF16)
        low = (values - high.astype(F32)).astype(BF16)
        weights = weights + dot(high, kept[block], NN) + dot(low, kept[block], NN)
    for n in range(3):
        grad[n * 64 : (n + 1) * 64, :] = blocks[n][1]
    slopes[...] = jnp.transpose(jnp.concatenate(slope[:2], axis=0))
    others = [slopes[pl.ds(y * 32 + x, 8, stride=4), :] for y in range(4) for x in range(4)]
    total[...] = message(weights, jnp.sum(losses, axis=1, keepdims=True), others)


def middle_kernel(got, send, values):
    values[...] = got[...].astype(F32)
    weights, loss = add_sums(values[...], 16)
    send[...] = message(weights, loss, [values[pl.ds(72 + z, 16, stride=80), :] for z in range(8)])


def output_kernel(updated, grad, dist_weight, pair_out, part, rows):
    for block in range(4):
        rows[pl.ds(block // 2 * 256 + block % 2, 128, stride=2), :] = updated[
            block * 128 : (block + 1) * 128, :
        ].astype(F32)
    pair_out[...] = rows[...].astype(BF16)
    part[128:256, :] = jnp.zeros((128, 128), F32)
    for n, block in enumerate((0, 2, 3)):
        slope = grad[n * 64 : (n + 1) * 64, :]
        high = slope.astype(BF16)
        low = (slope - high.astype(F32)).astype(BF16)
        part[block * 128 : (block + 1) * 128, :] = dot(high, dist_weight[...], TN) + dot(
            low, dist_weight[...], TN
        )


def last_kernel(got, part, place, dist_weight, grad_weight, loss, grad_pair, values, slopes):
    values[...] = got[...].astype(F32)
    for z in range(8):
        for y in range(4):
            at = z * 88 + 72 + y * 4
            slopes[y * 32 + z * 4 : y * 32 + z * 4 + 4, :] = values[at : at + 4, :]
    there = slopes[...].astype(BF16)
    none = jnp.zeros((64, 128), BF16)
    first = dot(there, jnp.concatenate([dist_weight[...], none], axis=0), NN)
    second = dot(there, jnp.concatenate([none, dist_weight[...]], axis=0), NN)
    device = lax.broadcasted_iota(jnp.int32, (128, 128), 0) * 2
    added = (
        jnp.where(device < place[0], first, 0.0),
        jnp.where(device <= place[0], second, first),
        None,
        jnp.where(device > place[0], second, 0.0),
    )
    for block in range(4):
        sums = part[block * 128 : (block + 1) * 128, :]
        grad_pair[pl.ds(block // 2 * 256 + block % 2, 128, stride=2), :] = (
            sums if added[block] is None else sums + added[block]
        )
    weights, total = add_sums(values[...], 8)
    grad_weight[...] = weights * (1.0 / 256)
    loss[0] = total[0, 0] * (1.0 / 65536)


def run(kernel, outs, scratch, args, room=24, **specs):
    shapes = [jax.ShapeDtypeStruct(s, d) for s, d in outs]
    moved = sum(x.size * x.dtype.itemsize for x in args)
    scratch = [pltpu.VMEM(*s) if isinstance(s, tuple) else s for s in scratch]
    return pl.pallas_call(
        kernel,
        out_shape=shapes,
        scratch_shapes=scratch,
        compiler_params=pltpu.CompilerParams(vmem_limit_bytes=room * 1024 * 1024),
        cost_estimate=pl.CostEstimate(flops=10_000_000, bytes_accessed=moved, transcendentals=0),
        **specs,
    )(*args)


VMEM, FAR = pl.BlockSpec(memory_space=pltpu.VMEM), pl.BlockSpec(memory_space=pl.ANY)
SMEM = pl.BlockSpec(memory_space=pltpu.SMEM)


def pack(*args):
    scratch = [
        ((512, 128), BF16),
        ((2, 256), jnp.int32),
        ((2, 256), jnp.int32),
        ((1, 128), F32),
        ((1, 128), F32),
        ((128, 512), BF16),
        ((512, 128), F32),
        ((3, 128, 256), F32),
        ((1536, 128), F32),
        pltpu.SemaphoreType.DMA((6,)),
    ]
    specs = [SMEM] + [FAR] * 6
    return run(pack_kernel, [((1536, 128), BF16)], scratch, args, 60, in_specs=specs)[0]


def triangle(got):
    scratch = [((1536, 128), F32), ((768, 128), F32)]
    return run(triangle_kernel, [((768, 128), BF16)], scratch, (got,))[0]


def gates(*args):
    outs = [((768, 128), F32), ((768, 128), F32), ((24, 128), F32)]
    scratch = [((512, 128), F32), ((1536, 128), F32), ((16, 256), F32)]
    return run(gate_kernel, outs, scratch, args, in_specs=[VMEM] * 5 + [SMEM] + [VMEM] * 6)


def head(*args):
    outs = [((512, 128), BF16), ((192, 128), F32), ((1280, 128), BF16)]
    scratch = [((768, 128), F32), ((128, 128), F32)]
    return run(head_kernel, outs, scratch, args, in_specs=[VMEM] * 4 + [SMEM] + [VMEM] * 2)


def middle(got):
    return run(middle_kernel, [((704, 128), BF16)], [((1280, 128), F32)], (got,))[0]


def outputs(updated, grad, dist_weight):
    outs = [((512, 128), BF16), ((512, 128), F32)]
    return run(output_kernel, outs, [((512, 128), F32)], (updated, grad, dist_weight))


def last(*args):
    outs = [((64, 128), F32), ((1,), F32), ((512, 128), F32)]
    scratch = [((704, 128), F32), ((128, 128), F32)]
    specs = {"in_specs": [VMEM, VMEM, SMEM, VMEM], "out_specs": [VMEM, SMEM, VMEM]}
    return run(last_kernel, outs, scratch, args, **specs)


def exchange(values, axes):
    return lax.all_to_all(values, axes, 0, 0, tiled=True)


def on_device(
    pair,
    chain,
    targets,
    pair_mask,
    ln_in_gain,
    ln_in_bias,
    in_weight,
    out_gate_weight,
    ln_out_gain,
    ln_out_bias,
    out_weight,
    dist_weight,
    dist_bias,
):
    flat = pair.reshape(512, 128)
    gain, bias = ln_in_gain.reshape(1, 128), ln_in_bias.reshape(1, 128)
    place = (lax.axis_index(GROUP) * 2).reshape(1)
    dist_weight = jnp.swapaxes(dist_weight, 0, 1)

    send = pack(place, flat, targets, pair_mask, gain, bias, in_weight)
    got = exchange(send.reshape(128, 6, 2, 128), GROUP).reshape(1536, 128)
    products = triangle(got)
    base, gate, marks = gates(
        flat, got, targets, pair_mask, chain.reshape(1, 256), place, gain, bias, out_gate_weight,
        ln_out_gain.reshape(1, 128), ln_out_bias.reshape(1, 128), dist_bias.reshape(1, 64),
    )
    hidden = exchange(products.reshape(128, 3, 2, 128), GROUP).reshape(768, 128)
    updated, grad, total = head(hidden, base, gate, marks, place, out_weight, dist_weight)
    total = middle(exchange(total.reshape(16, 80, 128), PLANE).reshape(1280, 128))
    pair_out, part = outputs(updated, grad, dist_weight)
    total = exchange(total.reshape(8, 88, 128), "zlo").reshape(704, 128)
    grad_weight, loss, grad_pair = last(total, part, place, dist_weight)
    return (
        pair_out.reshape(2, 256, 128),
        grad_pair.reshape(2, 256, 128),
        jnp.swapaxes(grad_weight, 0, 1),
        loss,
    )


def solution(mesh):
    fine = Mesh(mesh.devices.reshape(2, 2, 4, 8, 4), EVERY)
    part = ("zhi", "core")
    in_specs = (
        P(EVERY, None, None),
        P(part),
        P(EVERY, None),
        P(EVERY, None),
        P(),
        P(),
        P(),
        P(),
        P(),
        P(),
        P(),
        P(part, None),
        P(),
    )
    out_specs = (
        P(EVERY, None, None),
        P(EVERY, None, None),
        P(part, None),
        P(part),
    )
    return jax.shard_map(
        on_device, mesh=fine, in_specs=in_specs, out_specs=out_specs, check_vma=False
    )
```

```python
import jax
import jax.numpy as jnp
from jax import lax
from jax.experimental import pallas as pl
from jax.experimental.pallas import tpu as pltpu
from jax.sharding import Mesh
from jax.sharding import PartitionSpec as P

EVERY = ("zhi", "core", "y", "zlo", "x")
GROUP = ("y", "zlo", "x")
PLANE = ("y", "x")
BF16, F32 = jnp.bfloat16, jnp.float32
TN = (((0,), (0,)), ((), ()))
NT = (((1,), (1,)), ((), ()))
NN = (((1,), (0,)), ((), ()))
TT = (((0,), (1,)), ((), ()))


def dot(left, right, dims):
    return lax.dot_general(left, right, dims, preferred_element_type=F32)


def norm_lanes(values, gain, bias):
    center = jnp.mean(values, axis=1, keepdims=True)
    spread = jnp.mean(jnp.square(values - center), axis=1, keepdims=True)
    return (values - center) * lax.rsqrt(spread + 1e-05) * gain + bias


def picker(parity):
    rows = lax.broadcasted_iota(jnp.int32, (128, 256), 0)
    columns = lax.broadcasted_iota(jnp.int32, (128, 256), 1)
    return (columns == 2 * rows + parity).astype(F32).astype(BF16)


def pack_kernel(
    place, pair_far, targets_far, mask_far, gain_far, bias_far, weight_far, send, labels,
    pair, targets, mask, gain, bias, in_weight, flat, rows, sems,
):
    far = (targets_far, mask_far, pair_far, gain_far, bias_far, weight_far)
    near = (targets, mask, pair, gain, bias, in_weight)
    copies = [pltpu.make_async_copy(far[n], near[n], sems.at[n]) for n in range(6)]
    for copy in copies:
        copy.start()
    lower = lax.broadcasted_iota(jnp.int32, (128, 128), 0) * 2 <= place[0]
    even, odd = picker(0), picker(1)
    copies[0].wait()
    copies[1].wait()
    maskf = mask[...].astype(F32)
    label = jnp.where(mask[...] > 0, targets[...].astype(F32), 64.0)
    first, second, third = (
        dot(picked, jnp.broadcast_to(label[jr : jr + 1], (128, 256)).astype(BF16), NT)
        for picked, jr in ((even, 0), (odd, 0), (odd, 1))
    )
    labels[0:128, :] = jnp.where(lower, first, second)
    labels[128:256, :] = jnp.where(lower, second, third)
    copies[2].wait()
    flat[...] = pair[...].astype(F32)
    first, second, third = (
        flat[pl.ds(jr * 256 + ir, 128, stride=2), :] for ir, jr in ((0, 0), (1, 0), (1, 1))
    )
    rows[pl.ds(8, 128, stride=10), :] = jnp.where(lower, first, second)
    rows[pl.ds(9, 128, stride=10), :] = jnp.where(lower, second, third)
    for copy in copies[3:]:
        copy.wait()
    for r in range(2):
        normed = norm_lanes(flat[r * 256 : (r + 1) * 256, :], gain[...], bias[...]).astype(BF16)
        proj = dot(in_weight[...], normed, TT)
        projected = proj[:256] * jax.nn.sigmoid(proj[256:]) * maskf[r : r + 1]
        for side in range(2):
            for half in range(2):
                rows[pl.ds(side * 4 + r * 2 + half, 128, stride=10), :] = projected[
                    side * 128 : (side + 1) * 128, half * 128 : (half + 1) * 128
                ]
    send[...] = rows[...].astype(BF16)


def triangle_kernel(got, labels, send, rows, products):
    rows[...] = got[...].astype(F32)
    sides = []
    for side in range(2):
        for r in range(2):
            halves = [rows[pl.ds(side * 4 + r * 2 + half, 128, stride=10), :] for half in range(2)]
            sides.append(jnp.concatenate(halves, axis=1).astype(BF16))
    for r in range(2):
        for jr in range(2):
            products[pl.ds(r * 2 + jr, 128, stride=6), :] = dot(sides[r], sides[2 + jr], NT)
    first, second, third = (
        dot(sides[2 + r], sides[jr], NT) for r, jr in ((0, 0), (1, 0), (1, 1))
    )
    lane = lax.broadcasted_iota(jnp.int32, (128, 128), 1)
    device = lax.broadcasted_iota(jnp.int32, (128, 128), 0)
    products[pl.ds(4, 128, stride=6), :] = jnp.where(
        lane == device, labels[0:128, :], jnp.where(lane > device, first, second)
    )
    products[pl.ds(5, 128, stride=6), :] = jnp.where(
        lane == device, labels[128:256, :], jnp.where(lane > device, second, third)
    )
    send[...] = products[...].astype(BF16)


def gate_kernel(
    pair, got, targets, mask, chain, place, gain, bias, gate_weight, out_gain, out_bias, dist_bias,
    base, gate, marks, flat, rows, own,
):
    marks[...] = jnp.zeros((24, 128), F32)
    marks[16:17, :] = out_gain[...]
    marks[17:18, :] = out_bias[...]
    marks[18:19, :64] = dist_bias[...]
    flat[...] = pair[...].astype(F32)
    rows[...] = got[...].astype(F32)
    for block in range(4):
        base[block * 128 : (block + 1) * 128, :] = flat[
            pl.ds(block // 2 * 256 + block % 2, 128, stride=2), :
        ]
    base[512:640, :] = rows[pl.ds(8, 128, stride=10), :]
    base[640:768, :] = rows[pl.ds(9, 128, stride=10), :]
    normed = norm_lanes(base[...], gain[...], bias[...]).astype(BF16)
    gate[...] = jax.nn.sigmoid(dot(normed, gate_weight[...], NN))
    own[...] = jnp.zeros_like(own)
    own[0:2, :] = targets[...].astype(F32)
    own[2:4, :] = mask[...].astype(F32)
    columns = lax.broadcasted_iota(jnp.int32, (1, 256), 1)
    for r in range(2):
        here = jnp.sum(jnp.where(columns == place[0] + r, chain[...], 0), axis=1, keepdims=True)
        own[4 + r : 5 + r, :] = 1.0 + (chain[...] != here).astype(F32)
    even, odd = (dot(own[...].astype(BF16), picker(jr), NT) for jr in range(2))
    lanes = lax.broadcasted_iota(jnp.int32, (1, 128), 1) * 2
    higher, same = lanes >= place[0], lanes == place[0]
    target, valid, factor = (
        (
            jnp.where(higher, even[at : at + 1], even[at + 1 : at + 2]),
            jnp.where(higher, even[at + 1 : at + 2], odd[at + 1 : at + 2]),
            odd[at + 1 : at + 2],
        )
        for at in (0, 2, 4)
    )
    for group in range(2):
        marks[group : group + 1, :] = valid[group] * factor[group]
        marks[3 + group : 4 + group, :] = factor[group]
    alone = jnp.where(same, valid[2] * factor[2], 0.0)
    marks[2:3, :] = alone
    marks[5:6, :] = alone
    for group in range(3):
        marks[6 + group : 7 + group, :] = target[group]


def message(weights, loss, others):
    row = lax.broadcasted_iota(jnp.int32, (8, 128), 0)
    high = loss.astype(BF16).astype(F32)
    terms = jnp.where(row == 0, high, jnp.where(row == 1, loss - high, 0.0))
    pieces = [piece for other in others for piece in (weights, terms, other)]
    return jnp.concatenate(pieces, axis=0).astype(BF16)


def add_sums(values, peers):
    sums = jnp.sum(values.reshape(peers, values.shape[0] // peers, 128), axis=0)
    return sums[:64], sums[64:65, 0:1] + sums[65:66, 0:1]


def head_kernel(
    got, base, gate, marks, place, out_weight, dist_weight, updated, grad, total, hidden, slopes
):
    hidden[...] = got[...].astype(F32)
    columns = jnp.transpose(marks[16:24, :])
    gain, bias, dist_bias = columns[:, 0:1], columns[:, 1:2], columns[:64, 2:3]
    q = []
    kept = []
    lanes = lax.broadcasted_iota(jnp.int32, (128, 128), 1) * 2
    chosen = (lanes[:16] == place[0]).astype(F32).astype(BF16)
    heres = [hidden[pl.ds(block, 128, stride=6), :] for block in range(6)]
    labels = [dot(chosen, heres[4 + group].astype(BF16), NT)[0:1] for group in range(2)]
    for group in range(2):
        heres[4 + group] = jnp.where(lanes == place[0], heres[group], heres[4 + group])
    for block in range(6):
        here = heres[block]
        center = jnp.mean(here, axis=0, keepdims=True)
        spread = jnp.mean(jnp.square(here - center), axis=0, keepdims=True)
        normed = (here - center) * lax.rsqrt(spread + 1e-05)
        normed = (normed * gain + bias).astype(BF16)
        update = dot(normed, out_weight[...], TN)
        at = pl.ds(block * 128, 128)
        sums = (base[at, :] + gate[at, :] * update).astype(BF16)
        q.append(dot(dist_weight[...], sums, NT))
        kept.append(sums)
        if block < 4:
            updated[at, :] = sums
    lanes = lanes[:64]
    higher = lanes >= place[0]
    pairs = (
        jnp.where(higher, q[0], q[2]) + q[4],
        jnp.where(higher, q[2], q[3]) + q[5],
        q[3] + q[3],
    )
    bins = lax.broadcasted_iota(jnp.int32, (64, 128), 0).astype(F32)
    row = lambda at: marks[at : at + 1, :]
    mirrored = [jnp.where(labels[group] < 63.5, row(3 + group), 0.0) for group in range(2)]
    counted = [jnp.where(lanes[:1] == place[0], 0.0, mirrored[0]), mirrored[1]]
    mirrored.append(row(5))
    labels.append(row(8))
    losses = jnp.zeros((1, 128), F32)
    slope = []
    for group in range(3):
        logits = pairs[group] + dist_bias
        shifted = logits - jnp.max(logits, axis=0, keepdims=True)
        powers = jnp.exp(shifted)
        norms = jnp.sum(powers, axis=0, keepdims=True)
        log_probs = shifted - jnp.log(norms)
        probs = powers / norms
        onehot = (bins == row(6 + group)).astype(F32)
        onehot_back = (bins == labels[group]).astype(F32)
        losses = losses - row(group) * jnp.sum(onehot * log_probs, axis=0, keepdims=True)
        if group < 2:
            losses = losses - counted[group] * jnp.sum(onehot_back * log_probs, axis=0, keepdims=True)
        slope.append(row(group) * (probs - onehot) + mirrored[group] * (probs - onehot_back))
    blocks = (
        (0, jnp.where(higher, slope[0], 0.0)),
        (2, jnp.where(higher, slope[1], slope[0])),
        (3, jnp.where(higher, 0.0, slope[1]) + slope[2]),
        (4, jnp.where(lanes == place[0], 0.0, slope[0])),
        (5, slope[1]),
    )
    weights = jnp.zeros((64, 128), F32)
    for block, values in blocks:
        high = values.astype(BF16)
        low = (values - high.astype(F32)).astype(BF16)
        weights = weights + dot(high, kept[block], NN) + dot(low, kept[block], NN)
    for n in range(3):
        grad[n * 64 : (n + 1) * 64, :] = blocks[n][1]
    slopes[...] = jnp.transpose(jnp.concatenate(slope[:2], axis=0))
    others = [slopes[pl.ds(y * 32 + x, 8, stride=4), :] for y in range(4) for x in range(4)]
    total[...] = message(weights, jnp.sum(losses, axis=1, keepdims=True), others)


def middle_kernel(got, send, slopes):
    values = got[...].astype(F32)
    slopes[...] = values.reshape(16, 80, 128)[:, 72:80].reshape(128, 128)
    weights, loss = add_sums(values, 16)
    send[...] = message(weights, loss, [slopes[pl.ds(z, 16, stride=8), :] for z in range(8)])


def output_kernel(updated, grad, dist_weight, pair_out, part, rows):
    for block in range(4):
        rows[pl.ds(block // 2 * 256 + block % 2, 128, stride=2), :] = updated[
            block * 128 : (block + 1) * 128, :
        ].astype(F32)
    pair_out[...] = rows[...].astype(BF16)
    part[128:256, :] = jnp.zeros((128, 128), F32)
    for n, block in enumerate((0, 2, 3)):
        slope = grad[n * 64 : (n + 1) * 64, :]
        high = slope.astype(BF16)
        low = (slope - high.astype(F32)).astype(BF16)
        part[block * 128 : (block + 1) * 128, :] = dot(high, dist_weight[...], TN) + dot(
            low, dist_weight[...], TN
        )


def last_kernel(got, part, place, dist_weight, grad_weight, loss, grad_pair, slopes):
    values = got[...].astype(F32)
    for z in range(8):
        for y in range(4):
            at = z * 88 + 72 + y * 4
            slopes[y * 32 + z * 4 : y * 32 + z * 4 + 4, :] = values[at : at + 4]
    there = slopes[...].astype(BF16)
    none = jnp.zeros((64, 128), BF16)
    first = dot(there, jnp.concatenate([dist_weight[...], none], axis=0), NN)
    second = dot(there, jnp.concatenate([none, dist_weight[...]], axis=0), NN)
    device = lax.broadcasted_iota(jnp.int32, (128, 128), 0) * 2
    added = (
        jnp.where(device < place[0], first, 0.0),
        jnp.where(device <= place[0], second, first),
        None,
        jnp.where(device > place[0], second, 0.0),
    )
    for block in range(4):
        sums = part[block * 128 : (block + 1) * 128, :]
        grad_pair[pl.ds(block // 2 * 256 + block % 2, 128, stride=2), :] = (
            sums if added[block] is None else sums + added[block]
        )
    weights, total = add_sums(values, 8)
    grad_weight[...] = weights * (1.0 / 256)
    loss[0] = total[0, 0] * (1.0 / 65536)


def run(kernel, outs, scratch, args, **specs):
    shapes = [jax.ShapeDtypeStruct(s, d) for s, d in outs]
    moved = sum(x.size * x.dtype.itemsize for x in args)
    scratch = [pltpu.VMEM(*s) if isinstance(s, tuple) else s for s in scratch]
    return pl.pallas_call(
        kernel,
        out_shape=shapes,
        scratch_shapes=scratch,
        compiler_params=pltpu.CompilerParams(vmem_limit_bytes=24 * 1024 * 1024),
        cost_estimate=pl.CostEstimate(flops=10_000_000, bytes_accessed=moved, transcendentals=0),
        **specs,
    )(*args)


VMEM, FAR = pl.BlockSpec(memory_space=pltpu.VMEM), pl.BlockSpec(memory_space=pl.ANY)
SMEM = pl.BlockSpec(memory_space=pltpu.SMEM)


def pack(place, *args):
    scratch = [
        ((512, 128), BF16),
        ((2, 256), jnp.int32),
        ((2, 256), jnp.int32),
        ((1, 128), F32),
        ((1, 128), F32),
        ((128, 512), BF16),
        ((512, 128), F32),
        ((1280, 128), F32),
        pltpu.SemaphoreType.DMA((6,)),
    ]
    outs = [((1280, 128), BF16), ((256, 128), F32)]
    args = [pltpu.with_memory_space_constraint(arg, pltpu.HBM) for arg in args]
    return run(pack_kernel, outs, scratch, (place, *args), in_specs=[SMEM] + [FAR] * 6)


def triangle(got, labels):
    scratch = [((1280, 128), F32), ((768, 128), F32)]
    return run(triangle_kernel, [((768, 128), BF16)], scratch, (got, labels))[0]


def gates(*args):
    outs = [((768, 128), F32), ((768, 128), F32), ((24, 128), F32)]
    scratch = [((512, 128), F32), ((1280, 128), F32), ((16, 256), F32)]
    return run(gate_kernel, outs, scratch, args, in_specs=[VMEM] * 5 + [SMEM] + [VMEM] * 6)


def head(*args):
    outs = [((512, 128), BF16), ((192, 128), F32), ((1280, 128), BF16)]
    scratch = [((768, 128), F32), ((128, 128), F32)]
    return run(head_kernel, outs, scratch, args, in_specs=[VMEM] * 4 + [SMEM] + [VMEM] * 2)


def middle(got):
    return run(middle_kernel, [((704, 128), BF16)], [((128, 128), F32)], (got,))[0]


def outputs(updated, grad, dist_weight):
    outs = [((512, 128), BF16), ((512, 128), F32)]
    return run(output_kernel, outs, [((512, 128), F32)], (updated, grad, dist_weight))


def last(*args):
    outs = [((64, 128), F32), ((1,), F32), ((512, 128), F32)]
    scratch = [((128, 128), F32)]
    specs = {"in_specs": [VMEM, VMEM, SMEM, VMEM], "out_specs": [VMEM, SMEM, VMEM]}
    return run(last_kernel, outs, scratch, args, **specs)


def exchange(values, axes):
    return lax.all_to_all(values, axes, 0, 0, tiled=True)


def on_device(
    pair,
    chain,
    targets,
    pair_mask,
    ln_in_gain,
    ln_in_bias,
    in_weight,
    out_gate_weight,
    ln_out_gain,
    ln_out_bias,
    out_weight,
    dist_weight,
    dist_bias,
):
    flat = pair.reshape(512, 128)
    gain, bias = ln_in_gain.reshape(1, 128), ln_in_bias.reshape(1, 128)
    place = (lax.axis_index(GROUP) * 2).reshape(1)
    dist_weight = jnp.swapaxes(dist_weight, 0, 1)

    send, labels = pack(place, flat, targets, pair_mask, gain, bias, in_weight)
    got = exchange(send.reshape(128, 5, 2, 128), GROUP).reshape(1280, 128)
    products = triangle(got, labels)
    base, gate, marks = gates(
        flat, got, targets, pair_mask, chain.reshape(1, 256), place, gain, bias, out_gate_weight,
        ln_out_gain.reshape(1, 128), ln_out_bias.reshape(1, 128), dist_bias.reshape(1, 64),
    )
    hidden = exchange(products.reshape(128, 3, 2, 128), GROUP).reshape(768, 128)
    updated, grad, total = head(hidden, base, gate, marks, place, out_weight, dist_weight)
    total = middle(exchange(total.reshape(16, 80, 128), PLANE).reshape(1280, 128))
    pair_out, part = outputs(updated, grad, dist_weight)
    total = exchange(total.reshape(8, 88, 128), "zlo").reshape(704, 128)
    grad_weight, loss, grad_pair = last(total, part, place, dist_weight)
    return (
        pair_out.reshape(2, 256, 128),
        grad_pair.reshape(2, 256, 128),
        jnp.swapaxes(grad_weight, 0, 1),
        loss,
    )


def solution(mesh):
    fine = Mesh(mesh.devices.reshape(2, 2, 4, 8, 4), EVERY)
    part = ("zhi", "core")
    in_specs = (
        P(EVERY, None, None),
        P(part),
        P(EVERY, None),
        P(EVERY, None),
        P(),
        P(),
        P(),
        P(),
        P(),
        P(),
        P(),
        P(part, None),
        P(),
    )
    out_specs = (
        P(EVERY, None, None),
        P(EVERY, None, None),
        P(part, None),
        P(part),
    )
    return jax.shard_map(
        on_device, mesh=fine, in_specs=in_specs, out_specs=out_specs, check_vma=False
    )
```

```python
import jax
import jax.numpy as jnp
from jax import lax
from jax.experimental import pallas as pl
from jax.experimental.pallas import tpu as pltpu
from jax.sharding import Mesh
from jax.sharding import PartitionSpec as P

EVERY = ("zhi", "core", "y", "zlo", "x")
GROUP = ("y", "zlo", "x")
PLANE = ("y", "x")
BF16, F32 = jnp.bfloat16, jnp.float32
TN = (((0,), (0,)), ((), ()))
NT = (((1,), (1,)), ((), ()))
NN = (((1,), (0,)), ((), ()))
TT = (((0,), (1,)), ((), ()))


def dot(left, right, dims):
    return lax.dot_general(left, right, dims, preferred_element_type=F32)


def norm_lanes(values, gain, bias):
    center = jnp.mean(values, axis=1, keepdims=True)
    spread = jnp.mean(jnp.square(values - center), axis=1, keepdims=True)
    return (values - center) * lax.rsqrt(spread + 1e-05) * gain + bias


def picker(parity):
    rows = lax.broadcasted_iota(jnp.int32, (128, 256), 0)
    columns = lax.broadcasted_iota(jnp.int32, (128, 256), 1)
    return (columns == 2 * rows + parity).astype(F32).astype(BF16)


def pack_kernel(
    place, pair_far, targets_far, mask_far, gain_far, bias_far, weight_far, send, labels,
    pair, targets, mask, gain, bias, in_weight, flat, rows, sems,
):
    far = (targets_far, mask_far, pair_far, gain_far, bias_far, weight_far)
    near = (targets, mask, pair, gain, bias, in_weight)
    copies = [pltpu.make_async_copy(far[n], near[n], sems.at[n]) for n in range(6)]
    for copy in copies:
        copy.start()
    lower = lax.broadcasted_iota(jnp.int32, (128, 128), 0) * 2 <= place[0]
    even, odd = picker(0), picker(1)
    copies[0].wait()
    copies[1].wait()
    maskf = mask[...].astype(F32)
    label = jnp.where(mask[...] > 0, targets[...].astype(F32), 64.0)
    first, second, third = (
        dot(picked, jnp.broadcast_to(label[jr : jr + 1], (128, 256)).astype(BF16), NT)
        for picked, jr in ((even, 0), (odd, 0), (odd, 1))
    )
    labels[0:128, :] = jnp.where(lower, first, second)
    labels[128:256, :] = jnp.where(lower, second, third)
    copies[2].wait()
    flat[...] = pair[...].astype(F32)
    first, second, third = (
        flat[pl.ds(jr * 256 + ir, 128, stride=2), :] for ir, jr in ((0, 0), (1, 0), (1, 1))
    )
    rows[pl.ds(8, 128, stride=10), :] = jnp.where(lower, first, second)
    rows[pl.ds(9, 128, stride=10), :] = jnp.where(lower, second, third)
    for copy in copies[3:]:
        copy.wait()
    for r in range(2):
        normed = norm_lanes(flat[r * 256 : (r + 1) * 256, :], gain[...], bias[...]).astype(BF16)
        proj = dot(in_weight[...], normed, TT)
        projected = proj[:256] * jax.nn.sigmoid(proj[256:]) * maskf[r : r + 1]
        for side in range(2):
            for half in range(2):
                rows[pl.ds(side * 4 + r * 2 + half, 128, stride=10), :] = projected[
                    side * 128 : (side + 1) * 128, half * 128 : (half + 1) * 128
                ]
    send[...] = rows[...].astype(BF16)


def triangle_kernel(got, labels, send, rows, products):
    rows[...] = got[...].astype(F32)
    sides = []
    for side in range(2):
        for r in range(2):
            halves = [rows[pl.ds(side * 4 + r * 2 + half, 128, stride=10), :] for half in range(2)]
            sides.append(jnp.concatenate(halves, axis=1).astype(BF16))
    for r in range(2):
        for jr in range(2):
            products[pl.ds(r * 2 + jr, 128, stride=6), :] = dot(sides[r], sides[2 + jr], NT)
    first, second, third = (
        dot(sides[2 + r], sides[jr], NT) for r, jr in ((0, 0), (1, 0), (1, 1))
    )
    lane = lax.broadcasted_iota(jnp.int32, (128, 128), 1)
    device = lax.broadcasted_iota(jnp.int32, (128, 128), 0)
    products[pl.ds(4, 128, stride=6), :] = jnp.where(
        lane == device, labels[0:128, :], jnp.where(lane > device, first, second)
    )
    products[pl.ds(5, 128, stride=6), :] = jnp.where(
        lane == device, labels[128:256, :], jnp.where(lane > device, second, third)
    )
    send[...] = products[...].astype(BF16)


def gate_kernel(
    pair, got, targets, mask, chain, place, gain, bias, gate_weight, out_gain, out_bias, dist_bias,
    base, gate, marks, flat, rows, own,
):
    marks[...] = jnp.zeros((24, 128), F32)
    marks[16:17, :] = out_gain[...]
    marks[17:18, :] = out_bias[...]
    marks[18:19, :64] = dist_bias[...]
    flat[...] = pair[...].astype(F32)
    rows[...] = got[...].astype(F32)
    for block in range(4):
        base[block * 128 : (block + 1) * 128, :] = flat[
            pl.ds(block // 2 * 256 + block % 2, 128, stride=2), :
        ]
    base[512:640, :] = rows[pl.ds(8, 128, stride=10), :]
    base[640:768, :] = rows[pl.ds(9, 128, stride=10), :]
    normed = norm_lanes(base[...], gain[...], bias[...]).astype(BF16)
    gate[...] = jax.nn.sigmoid(dot(normed, gate_weight[...], NN))
    own[...] = jnp.zeros_like(own)
    own[0:2, :] = targets[...].astype(F32)
    own[2:4, :] = mask[...].astype(F32)
    columns = lax.broadcasted_iota(jnp.int32, (1, 256), 1)
    for r in range(2):
        here = jnp.sum(jnp.where(columns == place[0] + r, chain[...], 0), axis=1, keepdims=True)
        own[4 + r : 5 + r, :] = 1.0 + (chain[...] != here).astype(F32)
    even, odd = (dot(own[...].astype(BF16), picker(jr), NT) for jr in range(2))
    lanes = lax.broadcasted_iota(jnp.int32, (1, 128), 1) * 2
    higher, same = lanes >= place[0], lanes == place[0]
    target, valid, factor = (
        (
            jnp.where(higher, even[at : at + 1], even[at + 1 : at + 2]),
            jnp.where(higher, even[at + 1 : at + 2], odd[at + 1 : at + 2]),
            odd[at + 1 : at + 2],
        )
        for at in (0, 2, 4)
    )
    for group in range(2):
        marks[group : group + 1, :] = valid[group] * factor[group]
        marks[3 + group : 4 + group, :] = factor[group]
    alone = jnp.where(same, valid[2] * factor[2], 0.0)
    marks[2:3, :] = alone
    marks[5:6, :] = alone
    for group in range(3):
        marks[6 + group : 7 + group, :] = target[group]


def message(weights, loss, others):
    row = lax.broadcasted_iota(jnp.int32, (64, 128), 0)
    lane = lax.broadcasted_iota(jnp.int32, (1, 128), 1)
    high = loss.astype(BF16).astype(F32)
    terms = jnp.where(lane == 0, high, jnp.where(lane == 1, loss - high, 0.0))
    sums = jnp.where(row == 63, terms, weights)
    pieces = [piece for other in others for piece in (sums, other)]
    return jnp.concatenate(pieces, axis=0).astype(BF16)


def add_sums(values, peers):
    sums = jnp.sum(values.reshape(peers, values.shape[0] // peers, 128)[:, :64], axis=0)
    return sums, sums[63:64, 0:1] + sums[63:64, 1:2]


def head_kernel(
    got, base, gate, marks, place, out_weight, dist_weight, updated, grad, total, hidden, slopes
):
    hidden[...] = got[...].astype(F32)
    columns = jnp.transpose(marks[16:24, :])
    gain, bias, dist_bias = columns[:, 0:1], columns[:, 1:2], columns[:64, 2:3]
    q = []
    kept = []
    lanes = lax.broadcasted_iota(jnp.int32, (128, 128), 1) * 2
    chosen = (lanes[:16] == place[0]).astype(F32).astype(BF16)
    heres = [hidden[pl.ds(block, 128, stride=6), :] for block in range(6)]
    labels = [dot(chosen, heres[4 + group].astype(BF16), NT)[0:1] for group in range(2)]
    for group in range(2):
        heres[4 + group] = jnp.where(lanes == place[0], heres[group], heres[4 + group])
    for block in range(6):
        here = heres[block]
        center = jnp.mean(here, axis=0, keepdims=True)
        spread = jnp.mean(jnp.square(here - center), axis=0, keepdims=True)
        normed = (here - center) * lax.rsqrt(spread + 1e-05)
        normed = (normed * gain + bias).astype(BF16)
        update = dot(normed, out_weight[...], TN)
        at = pl.ds(block * 128, 128)
        sums = (base[at, :] + gate[at, :] * update).astype(BF16)
        q.append(dot(dist_weight[...], sums, NT))
        kept.append(sums)
        if block < 4:
            updated[at, :] = sums
    lanes = lanes[:64]
    higher = lanes >= place[0]
    pairs = (
        jnp.where(higher, q[0], q[2]) + q[4],
        jnp.where(higher, q[2], q[3]) + q[5],
        q[3] + q[3],
    )
    bins = lax.broadcasted_iota(jnp.int32, (64, 128), 0).astype(F32)
    row = lambda at: marks[at : at + 1, :]
    mirrored = [jnp.where(labels[group] < 63.5, row(3 + group), 0.0) for group in range(2)]
    counted = [jnp.where(lanes[:1] == place[0], 0.0, mirrored[0]), mirrored[1]]
    mirrored.append(row(5))
    labels.append(row(8))
    losses = jnp.zeros((1, 128), F32)
    slope = []
    for group in range(3):
        logits = pairs[group] + dist_bias
        shifted = logits - jnp.max(logits, axis=0, keepdims=True)
        powers = jnp.exp(shifted)
        norms = jnp.sum(powers, axis=0, keepdims=True)
        log_probs = shifted - jnp.log(norms)
        probs = powers / norms
        onehot = (bins == row(6 + group)).astype(F32)
        onehot_back = (bins == labels[group]).astype(F32)
        losses = losses - row(group) * jnp.sum(onehot * log_probs, axis=0, keepdims=True)
        if group < 2:
            losses = losses - counted[group] * jnp.sum(onehot_back * log_probs, axis=0, keepdims=True)
        slope.append(row(group) * (probs - onehot) + mirrored[group] * (probs - onehot_back))
    blocks = (
        (0, jnp.where(higher, slope[0], 0.0)),
        (2, jnp.where(higher, slope[1], slope[0])),
        (3, jnp.where(higher, 0.0, slope[1]) + slope[2]),
        (4, jnp.where(lanes == place[0], 0.0, slope[0])),
        (5, slope[1]),
    )
    weights = jnp.zeros((64, 128), F32)
    for block, values in blocks:
        high = values.astype(BF16)
        low = (values - high.astype(F32)).astype(BF16)
        weights = weights + dot(high, kept[block], NN) + dot(low, kept[block], NN)
    for n in range(3):
        grad[n * 64 : (n + 1) * 64, :] = blocks[n][1]
    slopes[...] = jnp.transpose(jnp.concatenate(slope[:2], axis=0))
    others = [slopes[pl.ds(y * 32 + x, 8, stride=4), :] for y in range(4) for x in range(4)]
    total[...] = message(weights, jnp.sum(losses, axis=1, keepdims=True), others)


def middle_kernel(got, send, slopes):
    values = got[...].astype(F32)
    slopes[...] = values.reshape(16, 72, 128)[:, 64:72].reshape(128, 128)
    weights, loss = add_sums(values, 16)
    send[...] = message(weights, loss, [slopes[pl.ds(z, 16, stride=8), :] for z in range(8)])


def output_kernel(updated, grad, dist_weight, pair_out, part, rows):
    for block in range(4):
        rows[pl.ds(block // 2 * 256 + block % 2, 128, stride=2), :] = updated[
            block * 128 : (block + 1) * 128, :
        ].astype(F32)
    pair_out[...] = rows[...].astype(BF16)
    part[128:256, :] = jnp.zeros((128, 128), F32)
    for n, block in enumerate((0, 2, 3)):
        slope = grad[n * 64 : (n + 1) * 64, :]
        high = slope.astype(BF16)
        low = (slope - high.astype(F32)).astype(BF16)
        part[block * 128 : (block + 1) * 128, :] = dot(high, dist_weight[...], TN) + dot(
            low, dist_weight[...], TN
        )


def last_kernel(got, part, place, dist_weight, grad_weight, loss, grad_pair, slopes):
    values = got[...].astype(F32)
    for z in range(8):
        for y in range(4):
            at = z * 80 + 64 + y * 4
            slopes[y * 32 + z * 4 : y * 32 + z * 4 + 4, :] = values[at : at + 4]
    there = slopes[...].astype(BF16)
    none = jnp.zeros((64, 128), BF16)
    first = dot(there, jnp.concatenate([dist_weight[...], none], axis=0), NN)
    second = dot(there, jnp.concatenate([none, dist_weight[...]], axis=0), NN)
    device = lax.broadcasted_iota(jnp.int32, (128, 128), 0) * 2
    added = (
        jnp.where(device < place[0], first, 0.0),
        jnp.where(device <= place[0], second, first),
        None,
        jnp.where(device > place[0], second, 0.0),
    )
    for block in range(4):
        sums = part[block * 128 : (block + 1) * 128, :]
        grad_pair[pl.ds(block // 2 * 256 + block % 2, 128, stride=2), :] = (
            sums if added[block] is None else sums + added[block]
        )
    weights, total = add_sums(values, 8)
    row = lax.broadcasted_iota(jnp.int32, (64, 128), 0)
    weights = jnp.where(row == 63, 0.0, weights)
    rest = jnp.sum(weights, axis=0, keepdims=True)
    grad_weight[...] = jnp.where(row == 63, -rest, weights) * (1.0 / 256)
    loss[0] = total[0, 0] * (1.0 / 65536)


def run(kernel, outs, scratch, args, **specs):
    shapes = [jax.ShapeDtypeStruct(s, d) for s, d in outs]
    moved = sum(x.size * x.dtype.itemsize for x in args)
    scratch = [pltpu.VMEM(*s) if isinstance(s, tuple) else s for s in scratch]
    return pl.pallas_call(
        kernel,
        out_shape=shapes,
        scratch_shapes=scratch,
        compiler_params=pltpu.CompilerParams(vmem_limit_bytes=24 * 1024 * 1024),
        cost_estimate=pl.CostEstimate(flops=10_000_000, bytes_accessed=moved, transcendentals=0),
        **specs,
    )(*args)


VMEM, FAR = pl.BlockSpec(memory_space=pltpu.VMEM), pl.BlockSpec(memory_space=pl.ANY)
SMEM = pl.BlockSpec(memory_space=pltpu.SMEM)


def pack(place, *args):
    scratch = [
        ((512, 128), BF16),
        ((2, 256), jnp.int32),
        ((2, 256), jnp.int32),
        ((1, 128), F32),
        ((1, 128), F32),
        ((128, 512), BF16),
        ((512, 128), F32),
        ((1280, 128), F32),
        pltpu.SemaphoreType.DMA((6,)),
    ]
    outs = [((1280, 128), BF16), ((256, 128), F32)]
    args = [pltpu.with_memory_space_constraint(arg, pltpu.HBM) for arg in args]
    return run(pack_kernel, outs, scratch, (place, *args), in_specs=[SMEM] + [FAR] * 6)


def triangle(got, labels):
    scratch = [((1280, 128), F32), ((768, 128), F32)]
    return run(triangle_kernel, [((768, 128), BF16)], scratch, (got, labels))[0]


def gates(*args):
    outs = [((768, 128), F32), ((768, 128), F32), ((24, 128), F32)]
    scratch = [((512, 128), F32), ((1280, 128), F32), ((16, 256), F32)]
    return run(gate_kernel, outs, scratch, args, in_specs=[VMEM] * 5 + [SMEM] + [VMEM] * 6)


def head(*args):
    outs = [((512, 128), BF16), ((192, 128), F32), ((1152, 128), BF16)]
    scratch = [((768, 128), F32), ((128, 128), F32)]
    return run(head_kernel, outs, scratch, args, in_specs=[VMEM] * 4 + [SMEM] + [VMEM] * 2)


def middle(got):
    return run(middle_kernel, [((640, 128), BF16)], [((128, 128), F32)], (got,))[0]


def outputs(updated, grad, dist_weight):
    outs = [((512, 128), BF16), ((512, 128), F32)]
    return run(output_kernel, outs, [((512, 128), F32)], (updated, grad, dist_weight))


def last(*args):
    outs = [((64, 128), F32), ((1,), F32), ((512, 128), F32)]
    scratch = [((128, 128), F32)]
    specs = {"in_specs": [VMEM, VMEM, SMEM, VMEM], "out_specs": [VMEM, SMEM, VMEM]}
    return run(last_kernel, outs, scratch, args, **specs)


def exchange(values, axes):
    return lax.all_to_all(values, axes, 0, 0, tiled=True)


def on_device(
    pair,
    chain,
    targets,
    pair_mask,
    ln_in_gain,
    ln_in_bias,
    in_weight,
    out_gate_weight,
    ln_out_gain,
    ln_out_bias,
    out_weight,
    dist_weight,
    dist_bias,
):
    flat = pair.reshape(512, 128)
    gain, bias = ln_in_gain.reshape(1, 128), ln_in_bias.reshape(1, 128)
    place = (lax.axis_index(GROUP) * 2).reshape(1)
    dist_weight = jnp.swapaxes(dist_weight, 0, 1)

    send, labels = pack(place, flat, targets, pair_mask, gain, bias, in_weight)
    got = exchange(send.reshape(128, 5, 2, 128), GROUP).reshape(1280, 128)
    products = triangle(got, labels)
    base, gate, marks = gates(
        flat, got, targets, pair_mask, chain.reshape(1, 256), place, gain, bias, out_gate_weight,
        ln_out_gain.reshape(1, 128), ln_out_bias.reshape(1, 128), dist_bias.reshape(1, 64),
    )
    hidden = exchange(products.reshape(128, 3, 2, 128), GROUP).reshape(768, 128)
    updated, grad, total = head(hidden, base, gate, marks, place, out_weight, dist_weight)
    total = middle(exchange(total.reshape(16, 72, 128), PLANE).reshape(1152, 128))
    pair_out, part = outputs(updated, grad, dist_weight)
    total = exchange(total.reshape(8, 80, 128), "zlo").reshape(640, 128)
    grad_weight, loss, grad_pair = last(total, part, place, dist_weight)
    return (
        pair_out.reshape(2, 256, 128),
        grad_pair.reshape(2, 256, 128),
        jnp.swapaxes(grad_weight, 0, 1),
        loss,
    )


def solution(mesh):
    fine = Mesh(mesh.devices.reshape(2, 2, 4, 8, 4), EVERY)
    part = ("zhi", "core")
    in_specs = (
        P(EVERY, None, None),
        P(part),
        P(EVERY, None),
        P(EVERY, None),
        P(),
        P(),
        P(),
        P(),
        P(),
        P(),
        P(),
        P(part, None),
        P(),
    )
    out_specs = (
        P(EVERY, None, None),
        P(EVERY, None, None),
        P(part, None),
        P(part),
    )
    return jax.shard_map(
        on_device, mesh=fine, in_specs=in_specs, out_specs=out_specs, check_vma=False
    )
```

```python
import jax
import jax.numpy as jnp
from jax import lax
from jax.experimental import pallas as pl
from jax.experimental.pallas import tpu as pltpu
from jax.sharding import Mesh
from jax.sharding import PartitionSpec as P

EVERY = ("zhi", "core", "y", "zlo", "x")
GROUP = ("y", "zlo", "x")
PLANE = ("y", "x")
BF16, F32 = jnp.bfloat16, jnp.float32
TN = (((0,), (0,)), ((), ()))
NT = (((1,), (1,)), ((), ()))
NN = (((1,), (0,)), ((), ()))
TT = (((0,), (1,)), ((), ()))


def dot(left, right, dims):
    return lax.dot_general(left, right, dims, preferred_element_type=F32)


def norm_lanes(values, gain, bias):
    center = jnp.mean(values, axis=1, keepdims=True)
    spread = jnp.mean(jnp.square(values - center), axis=1, keepdims=True)
    return (values - center) * lax.rsqrt(spread + 1e-05) * gain + bias


def picker(parity):
    rows = lax.broadcasted_iota(jnp.int32, (128, 256), 0)
    columns = lax.broadcasted_iota(jnp.int32, (128, 256), 1)
    return (columns == 2 * rows + parity).astype(F32).astype(BF16)


def pack_kernel(place, *refs):
    far, (send, labels, base, gate, marks, heavy) = refs[:13], refs[13:19]
    near, (flat, rows, own, sems) = refs[19:32], refs[32:]
    targets, mask, chain, pair, gain, bias, out_gain, out_bias, dist_bias = near[:9]
    in_weight, gate_weight, out_weight, dist_weight = near[9:]
    copies = [pltpu.make_async_copy(far[n], near[n], sems.at[n]) for n in range(13)]
    for copy in copies:
        copy.start()
    lower = lax.broadcasted_iota(jnp.int32, (128, 128), 0) * 2 <= place[0]
    pickers = picker(0), picker(1)
    for copy in copies[:3]:
        copy.wait()
    maskf = mask[...].astype(F32)
    label = jnp.where(mask[...] > 0, targets[...].astype(F32), 64.0)
    first, second, third = (
        dot(pickers[ir], jnp.broadcast_to(label[jr : jr + 1], (128, 256)).astype(BF16), NT)
        for ir, jr in ((0, 0), (1, 0), (1, 1))
    )
    labels[0:128, :] = jnp.where(lower, first, second)
    labels[128:256, :] = jnp.where(lower, second, third)
    own[...] = jnp.zeros_like(own)
    own[0:2, :] = targets[...].astype(F32)
    own[2:4, :] = maskf
    columns = lax.broadcasted_iota(jnp.int32, (1, 256), 1)
    for r in range(2):
        here = jnp.sum(jnp.where(columns == place[0] + r, chain[...], 0), axis=1, keepdims=True)
        own[4 + r : 5 + r, :] = 1.0 + (chain[...] != here).astype(F32)
    even, odd = (dot(own[...].astype(BF16), pickers[jr], NT) for jr in range(2))
    lanes = lax.broadcasted_iota(jnp.int32, (1, 128), 1) * 2
    higher, same = lanes >= place[0], lanes == place[0]
    target, valid, factor = (
        (
            jnp.where(higher, even[at : at + 1], even[at + 1 : at + 2]),
            jnp.where(higher, even[at + 1 : at + 2], odd[at + 1 : at + 2]),
            odd[at + 1 : at + 2],
        )
        for at in (0, 2, 4)
    )
    alone = jnp.where(same, valid[2] * factor[2], 0.0)
    marks[...] = jnp.zeros((24, 128), F32)
    for group in range(2):
        marks[group : group + 1, :] = valid[group] * factor[group]
        marks[3 + group : 4 + group, :] = factor[group]
    marks[2:3, :] = alone
    marks[5:6, :] = alone
    for group in range(3):
        marks[6 + group : 7 + group, :] = target[group]
    copies[3].wait()
    flat[...] = pair[...].astype(F32)
    for block in range(4):
        base[block * 128 : (block + 1) * 128, :] = flat[
            pl.ds(block // 2 * 256 + block % 2, 128, stride=2), :
        ]
    first, second, third = (
        flat[pl.ds(jr * 256 + ir, 128, stride=2), :] for ir, jr in ((0, 0), (1, 0), (1, 1))
    )
    rows[pl.ds(8, 128, stride=10), :] = jnp.where(lower, first, second)
    rows[pl.ds(9, 128, stride=10), :] = jnp.where(lower, second, third)
    for copy in copies[4:]:
        copy.wait()
    marks[16:17, :] = out_gain[...]
    marks[17:18, :] = out_bias[...]
    marks[18:19, :64] = dist_bias[...]
    marks[19:20, :] = gain[...]
    marks[20:21, :] = bias[...]
    heavy[0:128, :] = gate_weight[...]
    heavy[128:256, :] = out_weight[...]
    heavy[256:320, :] = dist_weight[...]
    normed = norm_lanes(flat[...], gain[...], bias[...]).astype(BF16)
    proj = dot(in_weight[...], normed, TT)
    for n in range(4):
        r, half = n // 2, n % 2
        at = slice(n * 128, (n + 1) * 128)
        here = jax.nn.sigmoid(proj[256:, at]) * maskf[r : r + 1, half * 128 : (half + 1) * 128]
        here = proj[:256, at] * here
        for side in range(2):
            rows[pl.ds(side * 4 + n, 128, stride=10), :] = here[side * 128 : (side + 1) * 128]
    send[...] = rows[...].astype(BF16)
    flat[...] = jax.nn.sigmoid(dot(normed, gate_weight[...], NN))
    for block in range(4):
        gate[block * 128 : (block + 1) * 128, :] = flat[
            pl.ds(block // 2 * 256 + block % 2, 128, stride=2), :
        ]


def triangle_kernel(got, labels, marks, heavy, send, base, gate, rows, products):
    rows[...] = got[...].astype(F32)
    sides = []
    for side in range(2):
        halves = []
        for half in range(2):
            parts = [
                rows[pl.ds(side * 4 + r * 2 + half, 128, stride=10), :].astype(BF16)
                for r in range(2)
            ]
            halves.append(jnp.concatenate(parts, axis=0))
        sides.append(jnp.concatenate(halves, axis=1))
    mixed = dot(sides[0], sides[1], NT)
    mirrored = dot(sides[1], sides[0], NT)
    for r in range(2):
        for jr in range(2):
            products[pl.ds(r * 2 + jr, 128, stride=6), :] = mixed[
                r * 128 : (r + 1) * 128, jr * 128 : (jr + 1) * 128
            ]
    first, second, third = mirrored[:128, :128], mirrored[128:, :128], mirrored[128:, 128:]
    lane = lax.broadcasted_iota(jnp.int32, (128, 128), 1)
    device = lax.broadcasted_iota(jnp.int32, (128, 128), 0)
    products[pl.ds(4, 128, stride=6), :] = jnp.where(
        lane == device, labels[0:128, :], jnp.where(lane > device, first, second)
    )
    products[pl.ds(5, 128, stride=6), :] = jnp.where(
        lane == device, labels[128:256, :], jnp.where(lane > device, second, third)
    )
    send[...] = products[...].astype(BF16)
    base[0:128, :] = rows[pl.ds(8, 128, stride=10), :]
    base[128:256, :] = rows[pl.ds(9, 128, stride=10), :]
    normed = norm_lanes(base[...], marks[19:20, :], marks[20:21, :]).astype(BF16)
    gate[...] = jax.nn.sigmoid(dot(normed, heavy[0:128, :], NN))


def message(weights, loss, others):
    row = lax.broadcasted_iota(jnp.int32, (8, 128), 0)
    high = loss.astype(BF16).astype(F32)
    terms = jnp.where(row == 0, high, jnp.where(row == 1, loss - high, 0.0))
    pieces = [piece for other in others for piece in (weights, terms, other)]
    return jnp.concatenate(pieces, axis=0).astype(BF16)


def add_sums(values, peers):
    sums = jnp.sum(values.reshape(peers, values.shape[0] // peers, 128), axis=0)
    return sums[:64], sums[64:65, 0:1] + sums[65:66, 0:1]


def head_kernel(
    got, base, gate, back_base, back_gate, marks, place, heavy,
    updated, grad, total, hidden, slopes,
):
    hidden[...] = got[...].astype(F32)
    columns = jnp.transpose(marks[16:24, :])
    gain, bias, dist_bias = columns[:, 0:1], columns[:, 1:2], columns[:64, 2:3]
    q = []
    kept = []
    lanes = lax.broadcasted_iota(jnp.int32, (128, 128), 1) * 2
    chosen = (lanes[:16] == place[0]).astype(F32).astype(BF16)
    heres = [hidden[pl.ds(block, 128, stride=6), :] for block in range(6)]
    labels = [dot(chosen, heres[4 + group].astype(BF16), NT)[0:1] for group in range(2)]
    for group in range(2):
        heres[4 + group] = jnp.where(lanes == place[0], heres[group], heres[4 + group])
    normeds = []
    for here in heres:
        center = jnp.mean(here, axis=0, keepdims=True)
        spread = jnp.mean(jnp.square(here - center), axis=0, keepdims=True)
        normed = (here - center) * lax.rsqrt(spread + 1e-05)
        normeds.append((normed * gain + bias).astype(BF16))
    update = dot(jnp.concatenate(normeds, axis=1), heavy[128:256, :], TN)
    sums = (base[...] + gate[...] * update[:512]).astype(BF16)
    back_sums = (back_base[...] + back_gate[...] * update[512:]).astype(BF16)
    updated[...] = sums
    sums = jnp.concatenate([sums, back_sums], axis=0)
    logit = dot(heavy[256:320, :], sums, NT)
    for block in range(6):
        at = slice(block * 128, (block + 1) * 128)
        q.append(logit[:, at])
        kept.append(sums[at])
    lanes = lanes[:64]
    higher = lanes >= place[0]
    pairs = (
        jnp.where(higher, q[0], q[2]) + q[4],
        jnp.where(higher, q[2], q[3]) + q[5],
        q[3] + q[3],
    )
    bins = lax.broadcasted_iota(jnp.int32, (64, 128), 0).astype(F32)
    row = lambda at: marks[at : at + 1, :]
    mirrored = [jnp.where(labels[group] < 63.5, row(3 + group), 0.0) for group in range(2)]
    counted = [jnp.where(lanes[:1] == place[0], 0.0, mirrored[0]), mirrored[1]]
    mirrored.append(row(5))
    labels.append(row(8))
    losses = jnp.zeros((1, 128), F32)
    slope = []
    for group in range(3):
        logits = pairs[group] + dist_bias
        shifted = logits - jnp.max(logits, axis=0, keepdims=True)
        powers = jnp.exp(shifted)
        norms = jnp.sum(powers, axis=0, keepdims=True)
        log_probs = shifted - jnp.log(norms)
        probs = powers / norms
        onehot = (bins == row(6 + group)).astype(F32)
        onehot_back = (bins == labels[group]).astype(F32)
        losses = losses - row(group) * jnp.sum(onehot * log_probs, axis=0, keepdims=True)
        if group < 2:
            losses = losses - counted[group] * jnp.sum(onehot_back * log_probs, axis=0, keepdims=True)
        slope.append(row(group) * (probs - onehot) + mirrored[group] * (probs - onehot_back))
    blocks = (
        (0, jnp.where(higher, slope[0], 0.0)),
        (2, jnp.where(higher, slope[1], slope[0])),
        (3, jnp.where(higher, 0.0, slope[1]) + slope[2]),
        (4, jnp.where(lanes == place[0], 0.0, slope[0])),
        (5, slope[1]),
    )
    weights = jnp.zeros((64, 128), F32)
    for block, values in blocks:
        high = values.astype(BF16)
        low = (values - high.astype(F32)).astype(BF16)
        weights = weights + dot(high, kept[block], NN) + dot(low, kept[block], NN)
    for n in range(3):
        grad[n * 64 : (n + 1) * 64, :] = blocks[n][1]
    slopes[...] = jnp.transpose(jnp.concatenate(slope[:2], axis=0))
    others = [slopes[pl.ds(y * 32 + x, 8, stride=4), :] for y in range(4) for x in range(4)]
    total[...] = message(weights, jnp.sum(losses, axis=1, keepdims=True), others)


def middle_kernel(got, send, slopes):
    values = got[...].astype(F32)
    slopes[...] = values.reshape(16, 80, 128)[:, 72:80].reshape(128, 128)
    weights, loss = add_sums(values, 16)
    send[...] = message(weights, loss, [slopes[pl.ds(z, 16, stride=8), :] for z in range(8)])


def last_kernel(
    got, updated, grad, place, heavy, grad_weight, loss, grad_pair, pair_out, slopes, rows
):
    for block in range(4):
        rows[pl.ds(block // 2 * 256 + block % 2, 128, stride=2), :] = updated[
            block * 128 : (block + 1) * 128, :
        ].astype(F32)
    pair_out[...] = rows[...].astype(BF16)
    dist_weight = heavy[256:320, :]
    part = {}
    for n, block in enumerate((0, 2, 3)):
        slope = grad[n * 64 : (n + 1) * 64, :]
        high = slope.astype(BF16)
        low = (slope - high.astype(F32)).astype(BF16)
        part[block] = dot(high, dist_weight, TN) + dot(low, dist_weight, TN)
    values = got[...].astype(F32)
    for z in range(8):
        for y in range(4):
            at = z * 88 + 72 + y * 4
            slopes[y * 32 + z * 4 : y * 32 + z * 4 + 4, :] = values[at : at + 4]
    there = slopes[...].astype(BF16)
    none = jnp.zeros((64, 128), BF16)
    first = dot(there, jnp.concatenate([dist_weight, none], axis=0), NN)
    second = dot(there, jnp.concatenate([none, dist_weight], axis=0), NN)
    device = lax.broadcasted_iota(jnp.int32, (128, 128), 0) * 2
    results = (
        part[0] + jnp.where(device < place[0], first, 0.0),
        jnp.where(device <= place[0], second, first),
        part[2],
        part[3] + jnp.where(device > place[0], second, 0.0),
    )
    for block in range(4):
        grad_pair[pl.ds(block // 2 * 256 + block % 2, 128, stride=2), :] = results[block]
    weights, total = add_sums(values, 8)
    grad_weight[...] = weights * (1.0 / 256)
    loss[0] = total[0, 0] * (1.0 / 65536)


def run(kernel, outs, scratch, args, **specs):
    shapes = [jax.ShapeDtypeStruct(s, d) for s, d in outs]
    moved = sum(x.size * x.dtype.itemsize for x in args)
    scratch = [pltpu.VMEM(*s) if isinstance(s, tuple) else s for s in scratch]
    return pl.pallas_call(
        kernel,
        out_shape=shapes,
        scratch_shapes=scratch,
        compiler_params=pltpu.CompilerParams(vmem_limit_bytes=24 * 1024 * 1024),
        cost_estimate=pl.CostEstimate(flops=10_000_000, bytes_accessed=moved, transcendentals=0),
        **specs,
    )(*args)


VMEM, FAR = pl.BlockSpec(memory_space=pltpu.VMEM), pl.BlockSpec(memory_space=pl.ANY)
SMEM = pl.BlockSpec(memory_space=pltpu.SMEM)


def pack(place, *args):
    scratch = [(arg.shape, arg.dtype) for arg in args]
    scratch += [((512, 128), F32), ((1280, 128), F32), ((16, 256), F32)]
    scratch += [pltpu.SemaphoreType.DMA((13,))]
    outs = [
        ((1280, 128), BF16),
        ((256, 128), F32),
        ((512, 128), F32),
        ((512, 128), F32),
        ((24, 128), F32),
        ((320, 128), BF16),
    ]
    args = [pltpu.with_memory_space_constraint(arg, pltpu.HBM) for arg in args]
    return run(pack_kernel, outs, scratch, (place, *args), in_specs=[SMEM] + [FAR] * 13)


def triangle(*args):
    outs = [((768, 128), BF16), ((256, 128), F32), ((256, 128), F32)]
    return run(triangle_kernel, outs, [((1280, 128), F32), ((768, 128), F32)], args)


def head(*args):
    outs = [((512, 128), BF16), ((192, 128), F32), ((1280, 128), BF16)]
    scratch = [((768, 128), F32), ((128, 128), F32)]
    return run(head_kernel, outs, scratch, args, in_specs=[VMEM] * 6 + [SMEM] + [VMEM])


def middle(got):
    return run(middle_kernel, [((704, 128), BF16)], [((128, 128), F32)], (got,))[0]


def last(*args):
    outs = [((64, 128), F32), ((1,), F32), ((512, 128), F32), ((512, 128), BF16)]
    scratch = [((128, 128), F32), ((512, 128), F32)]
    specs = {"in_specs": [VMEM] * 3 + [SMEM, VMEM], "out_specs": [VMEM, SMEM, VMEM, VMEM]}
    return run(last_kernel, outs, scratch, args, **specs)


def exchange(values, axes):
    return lax.all_to_all(values, axes, 0, 0, tiled=True)


def on_device(
    pair,
    chain,
    targets,
    pair_mask,
    ln_in_gain,
    ln_in_bias,
    in_weight,
    out_gate_weight,
    ln_out_gain,
    ln_out_bias,
    out_weight,
    dist_weight,
    dist_bias,
):
    place = (lax.axis_index(GROUP) * 2).reshape(1)
    row = lambda values: values.reshape(1, values.shape[0])
    send, labels, base, gate, marks, heavy = pack(
        place,
        targets,
        pair_mask,
        row(chain),
        pair.reshape(512, 128),
        row(ln_in_gain),
        row(ln_in_bias),
        row(ln_out_gain),
        row(ln_out_bias),
        row(dist_bias),
        in_weight,
        out_gate_weight,
        out_weight,
        jnp.swapaxes(dist_weight, 0, 1),
    )
    got = exchange(send.reshape(128, 5, 2, 128), GROUP).reshape(1280, 128)
    products, back_base, back_gate = triangle(got, labels, marks, heavy)
    hidden = exchange(products.reshape(128, 3, 2, 128), GROUP).reshape(768, 128)
    updated, grad, total = head(hidden, base, gate, back_base, back_gate, marks, place, heavy)
    total = middle(exchange(total.reshape(16, 80, 128), PLANE).reshape(1280, 128))
    total = exchange(total.reshape(8, 88, 128), "zlo").reshape(704, 128)
    grad_weight, loss, grad_pair, pair_out = last(total, updated, grad, place, heavy)
    return (
        pair_out.reshape(2, 256, 128),
        grad_pair.reshape(2, 256, 128),
        jnp.swapaxes(grad_weight, 0, 1),
        loss,
    )


def solution(mesh):
    fine = Mesh(mesh.devices.reshape(2, 2, 4, 8, 4), EVERY)
    part = ("zhi", "core")
    in_specs = (
        P(EVERY, None, None),
        P(part),
        P(EVERY, None),
        P(EVERY, None),
        P(),
        P(),
        P(),
        P(),
        P(),
        P(),
        P(),
        P(part, None),
        P(),
    )
    out_specs = (
        P(EVERY, None, None),
        P(EVERY, None, None),
        P(part, None),
        P(part),
    )
    return jax.shard_map(
        on_device, mesh=fine, in_specs=in_specs, out_specs=out_specs, check_vma=False
    )
```

```python
import jax
import jax.numpy as jnp
from jax import lax
from jax.experimental import pallas as pl
from jax.experimental.pallas import tpu as pltpu
from jax.sharding import Mesh
from jax.sharding import PartitionSpec as P

EVERY = ("zhi", "core", "y", "zlo", "x")
GROUP = ("y", "zlo", "x")
PLANE = ("y", "x")
BF16, F32 = jnp.bfloat16, jnp.float32
TN = (((0,), (0,)), ((), ()))
NT = (((1,), (1,)), ((), ()))
NN = (((1,), (0,)), ((), ()))
TT = (((0,), (1,)), ((), ()))


def dot(left, right, dims):
    return lax.dot_general(left, right, dims, preferred_element_type=F32)


def norm_lanes(values, gain, bias):
    center = jnp.mean(values, axis=1, keepdims=True)
    spread = jnp.mean(jnp.square(values - center), axis=1, keepdims=True)
    return (values - center) * lax.rsqrt(spread + 1e-05) * gain + bias


def picker(parity):
    rows = lax.broadcasted_iota(jnp.int32, (128, 256), 0)
    columns = lax.broadcasted_iota(jnp.int32, (128, 256), 1)
    return (columns == 2 * rows + parity).astype(F32).astype(BF16)


def pack_kernel(place, *refs):
    far, (send, labels, base, gate, marks, heavy) = refs[:13], refs[13:19]
    near, (flat, rows, own, sems) = refs[19:32], refs[32:]
    targets, mask, chain, pair, gain, bias, out_gain, out_bias, dist_bias = near[:9]
    in_weight, gate_weight, out_weight, dist_weight = near[9:]
    copies = [pltpu.make_async_copy(far[n], near[n], sems.at[n]) for n in range(13)]
    for copy in copies:
        copy.start()
    lower = lax.broadcasted_iota(jnp.int32, (128, 128), 0) * 2 <= place[0]
    pickers = picker(0), picker(1)
    for copy in copies[:3]:
        copy.wait()
    maskf = mask[...].astype(F32)
    label = jnp.where(mask[...] > 0, targets[...].astype(F32), 64.0)
    first, second, third = (
        dot(pickers[ir], jnp.broadcast_to(label[jr : jr + 1], (128, 256)).astype(BF16), NT)
        for ir, jr in ((0, 0), (1, 0), (1, 1))
    )
    labels[0:128, :] = jnp.where(lower, first, second)
    labels[128:256, :] = jnp.where(lower, second, third)
    own[...] = jnp.zeros_like(own)
    own[0:2, :] = targets[...].astype(F32)
    own[2:4, :] = maskf
    columns = lax.broadcasted_iota(jnp.int32, (1, 256), 1)
    for r in range(2):
        here = jnp.sum(jnp.where(columns == place[0] + r, chain[...], 0), axis=1, keepdims=True)
        own[4 + r : 5 + r, :] = 1.0 + (chain[...] != here).astype(F32)
    even, odd = (dot(own[...].astype(BF16), pickers[jr], NT) for jr in range(2))
    lanes = lax.broadcasted_iota(jnp.int32, (1, 128), 1) * 2
    higher, same = lanes >= place[0], lanes == place[0]
    target, valid, factor = (
        (
            jnp.where(higher, even[at : at + 1], even[at + 1 : at + 2]),
            jnp.where(higher, even[at + 1 : at + 2], odd[at + 1 : at + 2]),
            odd[at + 1 : at + 2],
        )
        for at in (0, 2, 4)
    )
    alone = jnp.where(same, valid[2] * factor[2], 0.0)
    marks[...] = jnp.zeros((24, 128), F32)
    for group in range(2):
        marks[group : group + 1, :] = valid[group] * factor[group]
        marks[3 + group : 4 + group, :] = factor[group]
    marks[2:3, :] = alone
    marks[5:6, :] = alone
    for group in range(3):
        marks[6 + group : 7 + group, :] = target[group]
    copies[3].wait()
    flat[0:512, :] = pair[...].astype(F32)
    for block in range(4):
        base[block * 128 : (block + 1) * 128, :] = flat[
            pl.ds(block // 2 * 256 + block % 2, 128, stride=2), :
        ]
    first, second, third = (
        flat[pl.ds(jr * 256 + ir, 128, stride=2), :] for ir, jr in ((0, 0), (1, 0), (1, 1))
    )
    rows[pl.ds(8, 128, stride=10), :] = jnp.where(lower, first, second)
    rows[pl.ds(9, 128, stride=10), :] = jnp.where(lower, second, third)
    for copy in copies[4:]:
        copy.wait()
    marks[16:17, :] = out_gain[...]
    marks[17:18, :] = out_bias[...]
    marks[18:19, :64] = dist_bias[...]
    marks[19:20, :] = gain[...]
    marks[20:21, :] = bias[...]
    heavy[0:128, :] = gate_weight[...]
    heavy[128:256, :] = out_weight[...]
    heavy[256:320, :] = dist_weight[...]
    normed = norm_lanes(flat[0:512, :], gain[...], bias[...]).astype(BF16)
    proj = dot(in_weight[...], normed, TT)
    for n in range(4):
        r, half = n // 2, n % 2
        at = slice(n * 128, (n + 1) * 128)
        here = jax.nn.sigmoid(proj[256:, at]) * maskf[r : r + 1, half * 128 : (half + 1) * 128]
        here = proj[:256, at] * here
        for side in range(2):
            rows[pl.ds(side * 4 + n, 128, stride=10), :] = here[side * 128 : (side + 1) * 128]
    send[...] = rows[0:1280, :].astype(BF16)
    flat[0:512, :] = jax.nn.sigmoid(dot(normed, gate_weight[...], NN))
    for block in range(4):
        gate[block * 128 : (block + 1) * 128, :] = flat[
            pl.ds(block // 2 * 256 + block % 2, 128, stride=2), :
        ]


def triangle_kernel(got, labels, marks, heavy, send, base, gate, rows, products):
    rows[0:1280, :] = got[...].astype(F32)
    sides = []
    for side in range(2):
        halves = []
        for half in range(2):
            parts = [
                rows[pl.ds(side * 4 + r * 2 + half, 128, stride=10), :].astype(BF16)
                for r in range(2)
            ]
            halves.append(jnp.concatenate(parts, axis=0))
        sides.append(jnp.concatenate(halves, axis=1))
    mixed = dot(sides[0], sides[1], NT)
    mirrored = dot(sides[1], sides[0], NT)
    for r in range(2):
        for jr in range(2):
            products[pl.ds(r * 2 + jr, 128, stride=6), :] = mixed[
                r * 128 : (r + 1) * 128, jr * 128 : (jr + 1) * 128
            ]
    first, second, third = mirrored[:128, :128], mirrored[128:, :128], mirrored[128:, 128:]
    lane = lax.broadcasted_iota(jnp.int32, (128, 128), 1)
    device = lax.broadcasted_iota(jnp.int32, (128, 128), 0)
    products[pl.ds(4, 128, stride=6), :] = jnp.where(
        lane == device, labels[0:128, :], jnp.where(lane > device, first, second)
    )
    products[pl.ds(5, 128, stride=6), :] = jnp.where(
        lane == device, labels[128:256, :], jnp.where(lane > device, second, third)
    )
    send[...] = products[0:768, :].astype(BF16)
    base[0:128, :] = rows[pl.ds(8, 128, stride=10), :]
    base[128:256, :] = rows[pl.ds(9, 128, stride=10), :]
    normed = norm_lanes(base[...], marks[19:20, :], marks[20:21, :]).astype(BF16)
    gate[...] = jax.nn.sigmoid(dot(normed, heavy[0:128, :], NN))


def message(weights, loss, others):
    row = lax.broadcasted_iota(jnp.int32, (8, 128), 0)
    high = loss.astype(BF16).astype(F32)
    terms = jnp.where(row == 0, high, jnp.where(row == 1, loss - high, 0.0))
    pieces = [piece for other in others for piece in (weights, terms, other)]
    return jnp.concatenate(pieces, axis=0).astype(BF16)


def add_sums(values, peers):
    sums = jnp.sum(values.reshape(peers, values.shape[0] // peers, 128), axis=0)
    return sums[:64], sums[64:65, 0:1] + sums[65:66, 0:1]


def head_kernel(
    got, base, gate, back_base, back_gate, marks, place, heavy,
    updated, grad, total, hidden, slopes,
):
    hidden[0:768, :] = got[...].astype(F32)
    columns = jnp.transpose(marks[16:24, :])
    gain, bias, dist_bias = columns[:, 0:1], columns[:, 1:2], columns[:64, 2:3]
    q = []
    kept = []
    lanes = lax.broadcasted_iota(jnp.int32, (128, 128), 1) * 2
    chosen = (lanes[:16] == place[0]).astype(F32).astype(BF16)
    heres = [hidden[pl.ds(block, 128, stride=6), :] for block in range(6)]
    labels = [dot(chosen, heres[4 + group].astype(BF16), NT)[0:1] for group in range(2)]
    for group in range(2):
        heres[4 + group] = jnp.where(lanes == place[0], heres[group], heres[4 + group])
    normeds = []
    for here in heres:
        center = jnp.mean(here, axis=0, keepdims=True)
        spread = jnp.mean(jnp.square(here - center), axis=0, keepdims=True)
        normed = (here - center) * lax.rsqrt(spread + 1e-05)
        normeds.append((normed * gain + bias).astype(BF16))
    update = dot(jnp.concatenate(normeds, axis=1), heavy[128:256, :], TN)
    sums = (base[...] + gate[...] * update[:512]).astype(BF16)
    back_sums = (back_base[...] + back_gate[...] * update[512:]).astype(BF16)
    updated[...] = sums
    sums = jnp.concatenate([sums, back_sums], axis=0)
    logit = dot(heavy[256:320, :], sums, NT)
    for block in range(6):
        at = slice(block * 128, (block + 1) * 128)
        q.append(logit[:, at])
        kept.append(sums[at])
    lanes = lanes[:64]
    higher = lanes >= place[0]
    pairs = (
        jnp.where(higher, q[0], q[2]) + q[4],
        jnp.where(higher, q[2], q[3]) + q[5],
        q[3] + q[3],
    )
    bins = lax.broadcasted_iota(jnp.int32, (64, 128), 0).astype(F32)
    row = lambda at: marks[at : at + 1, :]
    mirrored = [jnp.where(labels[group] < 63.5, row(3 + group), 0.0) for group in range(2)]
    counted = [jnp.where(lanes[:1] == place[0], 0.0, mirrored[0]), mirrored[1]]
    mirrored.append(row(5))
    labels.append(row(8))
    losses = jnp.zeros((1, 128), F32)
    slope = []
    for group in range(3):
        logits = pairs[group] + dist_bias
        shifted = logits - jnp.max(logits, axis=0, keepdims=True)
        powers = jnp.exp(shifted)
        norms = jnp.sum(powers, axis=0, keepdims=True)
        log_probs = shifted - jnp.log(norms)
        probs = powers / norms
        onehot = (bins == row(6 + group)).astype(F32)
        onehot_back = (bins == labels[group]).astype(F32)
        losses = losses - row(group) * jnp.sum(onehot * log_probs, axis=0, keepdims=True)
        if group < 2:
            losses = losses - counted[group] * jnp.sum(onehot_back * log_probs, axis=0, keepdims=True)
        slope.append(row(group) * (probs - onehot) + mirrored[group] * (probs - onehot_back))
    blocks = (
        (0, jnp.where(higher, slope[0], 0.0)),
        (2, jnp.where(higher, slope[1], slope[0])),
        (3, jnp.where(higher, 0.0, slope[1]) + slope[2]),
        (4, jnp.where(lanes == place[0], 0.0, slope[0])),
        (5, slope[1]),
    )
    weights = jnp.zeros((64, 128), F32)
    for block, values in blocks:
        high = values.astype(BF16)
        low = (values - high.astype(F32)).astype(BF16)
        weights = weights + dot(high, kept[block], NN) + dot(low, kept[block], NN)
    for n in range(3):
        grad[n * 64 : (n + 1) * 64, :] = blocks[n][1]
    slopes[0:128, :] = jnp.transpose(jnp.concatenate(slope[:2], axis=0))
    others = [slopes[pl.ds(y * 32 + x, 8, stride=4), :] for y in range(4) for x in range(4)]
    total[...] = message(weights, jnp.sum(losses, axis=1, keepdims=True), others)


def middle_kernel(got, send, slopes):
    values = got[...].astype(F32)
    slopes[0:128, :] = values.reshape(16, 80, 128)[:, 72:80].reshape(128, 128)
    weights, loss = add_sums(values, 16)
    send[...] = message(weights, loss, [slopes[pl.ds(z, 16, stride=8), :] for z in range(8)])


def last_kernel(
    got, updated, grad, place, heavy, grad_weight, loss, grad_far, pair_far,
    slopes, rows, grad_pair, pair_out, sems,
):
    for block in range(4):
        rows[pl.ds(block // 2 * 256 + block % 2, 128, stride=2), :] = updated[
            block * 128 : (block + 1) * 128, :
        ].astype(F32)
    pair_out[...] = rows[0:512, :].astype(BF16)
    copies = [pltpu.make_async_copy(pair_out, pair_far, sems.at[0])]
    copies[0].start()
    dist_weight = heavy[256:320, :]
    part = {}
    for n, block in enumerate((0, 2, 3)):
        slope = grad[n * 64 : (n + 1) * 64, :]
        high = slope.astype(BF16)
        low = (slope - high.astype(F32)).astype(BF16)
        part[block] = dot(high, dist_weight, TN) + dot(low, dist_weight, TN)
    values = got[...].astype(F32)
    for z in range(8):
        for y in range(4):
            at = z * 88 + 72 + y * 4
            slopes[y * 32 + z * 4 : y * 32 + z * 4 + 4, :] = values[at : at + 4]
    there = slopes[...].astype(BF16)
    none = jnp.zeros((64, 128), BF16)
    first = dot(there, jnp.concatenate([dist_weight, none], axis=0), NN)
    second = dot(there, jnp.concatenate([none, dist_weight], axis=0), NN)
    device = lax.broadcasted_iota(jnp.int32, (128, 128), 0) * 2
    results = (
        part[0] + jnp.where(device < place[0], first, 0.0),
        jnp.where(device <= place[0], second, first),
        part[2],
        part[3] + jnp.where(device > place[0], second, 0.0),
    )
    for block in range(4):
        grad_pair[pl.ds(block // 2 * 256 + block % 2, 128, stride=2), :] = results[block]
        if block % 2:
            half = pl.ds(block // 2 * 256, 256)
            copies.append(
                pltpu.make_async_copy(
                    grad_pair.at[half], grad_far.at[half], sems.at[1 + block // 2]
                )
            )
            copies[-1].start()
    weights, total = add_sums(values, 8)
    grad_weight[...] = weights * (1.0 / 256)
    loss[0] = total[0, 0] * (1.0 / 65536)
    for copy in copies:
        copy.wait()


def run(kernel, outs, scratch, args, **specs):
    shapes = [jax.ShapeDtypeStruct(s, d) for s, d in outs]
    moved = sum(x.size * x.dtype.itemsize for x in args)
    scratch = [pltpu.VMEM(*s) if isinstance(s, tuple) else s for s in scratch]
    return pl.pallas_call(
        kernel,
        out_shape=shapes,
        scratch_shapes=scratch,
        compiler_params=pltpu.CompilerParams(vmem_limit_bytes=24 * 1024 * 1024),
        cost_estimate=pl.CostEstimate(flops=10_000_000, bytes_accessed=moved, transcendentals=0),
        **specs,
    )(*args)


VMEM, FAR = pl.BlockSpec(memory_space=pltpu.VMEM), pl.BlockSpec(memory_space=pl.ANY)
SMEM = pl.BlockSpec(memory_space=pltpu.SMEM)


def pack(place, *args):
    scratch = [(arg.shape, arg.dtype) for arg in args]
    scratch += [((520, 128), F32), ((1296, 128), F32), ((16, 256), F32)]
    scratch += [pltpu.SemaphoreType.DMA((13,))]
    outs = [
        ((1280, 128), BF16),
        ((256, 128), F32),
        ((512, 128), F32),
        ((512, 128), F32),
        ((24, 128), F32),
        ((320, 128), BF16),
    ]
    args = [pltpu.with_memory_space_constraint(arg, pltpu.HBM) for arg in args]
    return run(pack_kernel, outs, scratch, (place, *args), in_specs=[SMEM] + [FAR] * 13)


def triangle(*args):
    outs = [((768, 128), BF16), ((256, 128), F32), ((256, 128), F32)]
    return run(triangle_kernel, outs, [((1296, 128), F32), ((784, 128), F32)], args)


def head(*args):
    outs = [((512, 128), BF16), ((192, 128), F32), ((1280, 128), BF16)]
    scratch = [((784, 128), F32), ((136, 128), F32)]
    return run(head_kernel, outs, scratch, args, in_specs=[VMEM] * 6 + [SMEM] + [VMEM])


def middle(got):
    return run(middle_kernel, [((704, 128), BF16)], [((136, 128), F32)], (got,))[0]


def last(*args):
    outs = [((64, 128), F32), ((1,), F32), ((512, 128), F32), ((512, 128), BF16)]
    scratch = [((128, 128), F32), ((520, 128), F32), ((520, 128), F32), ((512, 128), BF16)]
    scratch += [pltpu.SemaphoreType.DMA((3,))]
    specs = {"in_specs": [VMEM] * 3 + [SMEM, VMEM], "out_specs": [VMEM, SMEM, FAR, FAR]}
    return run(last_kernel, outs, scratch, args, **specs)


def exchange(values, axes):
    return lax.all_to_all(values, axes, 0, 0, tiled=True)


def on_device(
    pair,
    chain,
    targets,
    pair_mask,
    ln_in_gain,
    ln_in_bias,
    in_weight,
    out_gate_weight,
    ln_out_gain,
    ln_out_bias,
    out_weight,
    dist_weight,
    dist_bias,
):
    place = (lax.axis_index(GROUP) * 2).reshape(1)
    row = lambda values: values.reshape(1, values.shape[0])
    send, labels, base, gate, marks, heavy = pack(
        place,
        targets,
        pair_mask,
        row(chain),
        pair.reshape(512, 128),
        row(ln_in_gain),
        row(ln_in_bias),
        row(ln_out_gain),
        row(ln_out_bias),
        row(dist_bias),
        in_weight,
        out_gate_weight,
        out_weight,
        jnp.swapaxes(dist_weight, 0, 1),
    )
    got = exchange(send.reshape(128, 5, 2, 128), GROUP).reshape(1280, 128)
    products, back_base, back_gate = triangle(got, labels, marks, heavy)
    hidden = exchange(products.reshape(128, 3, 2, 128), GROUP).reshape(768, 128)
    updated, grad, total = head(hidden, base, gate, back_base, back_gate, marks, place, heavy)
    total = middle(exchange(total.reshape(16, 80, 128), PLANE).reshape(1280, 128))
    total = exchange(total.reshape(8, 88, 128), "zlo").reshape(704, 128)
    grad_weight, loss, grad_pair, pair_out = last(total, updated, grad, place, heavy)
    return (
        pair_out.reshape(2, 256, 128),
        grad_pair.reshape(2, 256, 128),
        jnp.swapaxes(grad_weight, 0, 1),
        loss,
    )


def solution(mesh):
    fine = Mesh(mesh.devices.reshape(2, 2, 4, 8, 4), EVERY)
    part = ("zhi", "core")
    in_specs = (
        P(EVERY, None, None),
        P(part),
        P(EVERY, None),
        P(EVERY, None),
        P(),
        P(),
        P(),
        P(),
        P(),
        P(),
        P(),
        P(part, None),
        P(),
    )
    out_specs = (
        P(EVERY, None, None),
        P(EVERY, None, None),
        P(part, None),
        P(part),
    )
    return jax.shard_map(
        on_device, mesh=fine, in_specs=in_specs, out_specs=out_specs, check_vma=False
    )
```

```python
import jax
import jax.numpy as jnp
from jax import lax
from jax.experimental import pallas as pl
from jax.experimental.pallas import tpu as pltpu
from jax.sharding import Mesh
from jax.sharding import PartitionSpec as P

EVERY = ("zhi", "core", "y", "zlo", "x")
GROUP = ("y", "zlo", "x")
PLANE = ("y", "x")
BF16, F32 = jnp.bfloat16, jnp.float32
TN = (((0,), (0,)), ((), ()))
NT = (((1,), (1,)), ((), ()))
NN = (((1,), (0,)), ((), ()))
TT = (((0,), (1,)), ((), ()))


def dot(left, right, dims):
    return lax.dot_general(left, right, dims, preferred_element_type=F32)


def norm_lanes(values, gain, bias):
    center = jnp.mean(values, axis=1, keepdims=True)
    spread = jnp.mean(jnp.square(values - center), axis=1, keepdims=True)
    return (values - center) * lax.rsqrt(spread + 1e-05) * gain + bias


def picker(parity):
    rows = lax.broadcasted_iota(jnp.int32, (128, 256), 0)
    columns = lax.broadcasted_iota(jnp.int32, (128, 256), 1)
    return (columns == 2 * rows + parity).astype(F32).astype(BF16)


def pack_kernel(place, *refs):
    far, (send, labels, base, gate, marks, heavy) = refs[:13], refs[13:19]
    near, (flat, rows, own, sems) = refs[19:32], refs[32:]
    targets, mask, chain, pair, gain, bias, out_gain, out_bias, dist_bias = near[:9]
    in_weight, gate_weight, out_weight, dist_weight = near[9:]
    copies = [pltpu.make_async_copy(far[n], near[n], sems.at[n]) for n in range(13)]
    for copy in copies:
        copy.start()
    lower = lax.broadcasted_iota(jnp.int32, (128, 128), 0) * 2 <= place[0]
    pickers = picker(0), picker(1)
    for copy in copies[:3]:
        copy.wait()
    maskf = mask[...].astype(F32)
    label = jnp.where(mask[...] > 0, targets[...].astype(F32), 64.0)
    first, second, third = (
        dot(pickers[ir], jnp.broadcast_to(label[jr : jr + 1], (128, 256)).astype(BF16), NT)
        for ir, jr in ((0, 0), (1, 0), (1, 1))
    )
    labels[0:128, :] = jnp.where(lower, first, second)
    labels[128:256, :] = jnp.where(lower, second, third)
    own[...] = jnp.zeros_like(own)
    own[0:2, :] = targets[...].astype(F32)
    own[2:4, :] = maskf
    columns = lax.broadcasted_iota(jnp.int32, (1, 256), 1)
    for r in range(2):
        here = jnp.sum(jnp.where(columns == place[0] + r, chain[...], 0), axis=1, keepdims=True)
        own[4 + r : 5 + r, :] = 1.0 + (chain[...] != here).astype(F32)
    even, odd = (dot(own[...].astype(BF16), pickers[jr], NT) for jr in range(2))
    lanes = lax.broadcasted_iota(jnp.int32, (1, 128), 1) * 2
    higher, same = lanes >= place[0], lanes == place[0]
    target, valid, factor = (
        (
            jnp.where(higher, even[at : at + 1], even[at + 1 : at + 2]),
            jnp.where(higher, even[at + 1 : at + 2], odd[at + 1 : at + 2]),
            odd[at + 1 : at + 2],
        )
        for at in (0, 2, 4)
    )
    alone = jnp.where(same, valid[2] * factor[2], 0.0)
    marks[...] = jnp.zeros((24, 128), F32)
    for group in range(2):
        marks[group : group + 1, :] = valid[group] * factor[group]
        marks[3 + group : 4 + group, :] = factor[group]
    marks[2:3, :] = alone
    marks[5:6, :] = alone
    for group in range(3):
        marks[6 + group : 7 + group, :] = target[group]
    copies[3].wait()
    flat[0:512, :] = pair[...].astype(F32)
    for block in range(4):
        base[block * 128 : (block + 1) * 128, :] = flat[
            pl.ds(block // 2 * 256 + block % 2, 128, stride=2), :
        ]
    first, second, third = (
        flat[pl.ds(jr * 256 + ir, 128, stride=2), :] for ir, jr in ((0, 0), (1, 0), (1, 1))
    )
    rows[pl.ds(8, 128, stride=10), :] = jnp.where(lower, first, second)
    rows[pl.ds(9, 128, stride=10), :] = jnp.where(lower, second, third)
    for copy in copies[4:]:
        copy.wait()
    marks[16:17, :] = out_gain[...]
    marks[17:18, :] = out_bias[...]
    marks[18:19, :64] = dist_bias[...]
    marks[19:20, :] = gain[...]
    marks[20:21, :] = bias[...]
    heavy[0:128, :] = gate_weight[...]
    heavy[128:256, :] = out_weight[...]
    heavy[256:320, :] = dist_weight[...]
    normed = norm_lanes(flat[0:512, :], gain[...], bias[...]).astype(BF16)
    proj = dot(in_weight[...], normed, TT)
    for n in range(4):
        r, half = n // 2, n % 2
        at = slice(n * 128, (n + 1) * 128)
        here = jax.nn.sigmoid(proj[256:, at]) * maskf[r : r + 1, half * 128 : (half + 1) * 128]
        here = proj[:256, at] * here
        for side in range(2):
            rows[pl.ds(side * 4 + n, 128, stride=10), :] = here[side * 128 : (side + 1) * 128]
    send[...] = rows[0:1280, :].astype(BF16)
    flat[0:512, :] = jax.nn.sigmoid(dot(normed, gate_weight[...], NN))
    for block in range(4):
        gate[block * 128 : (block + 1) * 128, :] = flat[
            pl.ds(block // 2 * 256 + block % 2, 128, stride=2), :
        ]


def triangle_kernel(got, labels, marks, heavy, send, base, gate, rows, products):
    rows[0:1280, :] = got[...].astype(F32)
    sides = []
    for side in range(2):
        halves = []
        for half in range(2):
            parts = [
                rows[pl.ds(side * 4 + r * 2 + half, 128, stride=10), :].astype(BF16)
                for r in range(2)
            ]
            halves.append(jnp.concatenate(parts, axis=0))
        sides.append(jnp.concatenate(halves, axis=1))
    mixed = dot(sides[0], sides[1], NT)
    mirrored = dot(sides[1], sides[0], NT)
    for r in range(2):
        for jr in range(2):
            products[pl.ds(r * 2 + jr, 128, stride=6), :] = mixed[
                r * 128 : (r + 1) * 128, jr * 128 : (jr + 1) * 128
            ]
    first, second, third = mirrored[:128, :128], mirrored[128:, :128], mirrored[128:, 128:]
    lane = lax.broadcasted_iota(jnp.int32, (128, 128), 1)
    device = lax.broadcasted_iota(jnp.int32, (128, 128), 0)
    products[pl.ds(4, 128, stride=6), :] = jnp.where(
        lane == device, labels[0:128, :], jnp.where(lane > device, first, second)
    )
    products[pl.ds(5, 128, stride=6), :] = jnp.where(
        lane == device, labels[128:256, :], jnp.where(lane > device, second, third)
    )
    send[...] = products[0:768, :].astype(BF16)
    base[0:128, :] = rows[pl.ds(8, 128, stride=10), :]
    base[128:256, :] = rows[pl.ds(9, 128, stride=10), :]
    normed = norm_lanes(base[...], marks[19:20, :], marks[20:21, :]).astype(BF16)
    gate[...] = jax.nn.sigmoid(dot(normed, heavy[0:128, :], NN))


def message(weights, loss, others):
    row = lax.broadcasted_iota(jnp.int32, (8, 128), 0)
    high = loss.astype(BF16).astype(F32)
    terms = jnp.where(row == 0, high, jnp.where(row == 1, loss - high, 0.0))
    pieces = [piece for other in others for piece in (weights, terms, other)]
    return jnp.concatenate(pieces, axis=0).astype(BF16)


def add_sums(values, peers):
    sums = jnp.sum(values.reshape(peers, values.shape[0] // peers, 128), axis=0)
    return sums[:64], sums[64:65, 0:1] + sums[65:66, 0:1]


def head_kernel(
    got, base, gate, back_base, back_gate, marks, place, heavy,
    updated, grad, total, hidden, slopes,
):
    hidden[0:768, :] = got[...].astype(F32)
    columns = jnp.transpose(marks[16:24, :])
    gain, bias, dist_bias = columns[:, 0:1], columns[:, 1:2], columns[:64, 2:3]
    q = []
    kept = []
    lanes = lax.broadcasted_iota(jnp.int32, (128, 128), 1) * 2
    chosen = (lanes[:16] == place[0]).astype(F32).astype(BF16)
    heres = [hidden[pl.ds(block, 128, stride=6), :] for block in range(6)]
    labels = [dot(chosen, heres[4 + group].astype(BF16), NT)[0:1] for group in range(2)]
    for group in range(2):
        heres[4 + group] = jnp.where(lanes == place[0], heres[group], heres[4 + group])
    normeds = []
    for here in heres:
        center = jnp.mean(here, axis=0, keepdims=True)
        spread = jnp.mean(jnp.square(here - center), axis=0, keepdims=True)
        normed = (here - center) * lax.rsqrt(spread + 1e-05)
        normeds.append((normed * gain + bias).astype(BF16))
    update = dot(jnp.concatenate(normeds, axis=1), heavy[128:256, :], TN)
    sums = (base[...] + gate[...] * update[:512]).astype(BF16)
    back_sums = (back_base[...] + back_gate[...] * update[512:]).astype(BF16)
    updated[...] = sums
    sums = jnp.concatenate([sums, back_sums], axis=0)
    logit = dot(heavy[256:320, :], sums, NT)
    for block in range(6):
        at = slice(block * 128, (block + 1) * 128)
        q.append(logit[:, at])
        kept.append(sums[at])
    lanes = lanes[:64]
    higher = lanes >= place[0]
    pairs = (
        jnp.where(higher, q[0], q[2]) + q[4],
        jnp.where(higher, q[2], q[3]) + q[5],
        q[3] + q[3],
    )
    bins = lax.broadcasted_iota(jnp.int32, (64, 128), 0).astype(F32)
    row = lambda at: marks[at : at + 1, :]
    mirrored = [jnp.where(labels[group] < 63.5, row(3 + group), 0.0) for group in range(2)]
    counted = [jnp.where(lanes[:1] == place[0], 0.0, mirrored[0]), mirrored[1]]
    mirrored.append(row(5))
    labels.append(row(8))
    losses = jnp.zeros((1, 128), F32)
    slope = []
    for group in range(3):
        logits = pairs[group] + dist_bias
        shifted = logits - jnp.max(logits, axis=0, keepdims=True)
        powers = jnp.exp(shifted)
        norms = jnp.sum(powers, axis=0, keepdims=True)
        log_probs = shifted - jnp.log(norms)
        probs = powers / norms
        onehot = (bins == row(6 + group)).astype(F32)
        onehot_back = (bins == labels[group]).astype(F32)
        losses = losses - row(group) * jnp.sum(onehot * log_probs, axis=0, keepdims=True)
        if group < 2:
            losses = losses - counted[group] * jnp.sum(onehot_back * log_probs, axis=0, keepdims=True)
        slope.append(row(group) * (probs - onehot) + mirrored[group] * (probs - onehot_back))
    blocks = (
        (0, jnp.where(higher, slope[0], 0.0)),
        (2, jnp.where(higher, slope[1], slope[0])),
        (3, jnp.where(higher, 0.0, slope[1]) + slope[2]),
        (4, jnp.where(lanes == place[0], 0.0, slope[0])),
        (5, slope[1]),
    )
    weights = jnp.zeros((64, 128), F32)
    for block, values in blocks:
        high = values.astype(BF16)
        low = (values - high.astype(F32)).astype(BF16)
        weights = weights + dot(high, kept[block], NN) + dot(low, kept[block], NN)
    for n in range(3):
        grad[n * 64 : (n + 1) * 64, :] = blocks[n][1]
    slopes[0:128, :] = jnp.transpose(jnp.concatenate(slope[:2], axis=0))
    others = [slopes[pl.ds(y * 32 + x, 8, stride=4), :] for y in range(4) for x in range(4)]
    total[...] = message(weights, jnp.sum(losses, axis=1, keepdims=True), others)


def middle_kernel(got, send, slopes):
    values = got[...].astype(F32)
    slopes[0:128, :] = values.reshape(16, 80, 128)[:, 72:80].reshape(128, 128)
    weights, loss = add_sums(values, 16)
    send[...] = message(weights, loss, [slopes[pl.ds(z, 16, stride=8), :] for z in range(8)])


def last_kernel(
    got, updated, grad, place, heavy, grad_weight, loss, grad_pair, pair_out,
    slopes, rows, order,
):
    for block in range(4):
        rows[pl.ds(block // 2 * 256 + block % 2, 128, stride=2), :] = updated[
            block * 128 : (block + 1) * 128, :
        ].astype(F32)
    pair_out[...] = rows[0:512, :].astype(BF16)
    dist_weight = heavy[256:320, :]
    part = {}
    for n, block in enumerate((0, 2, 3)):
        slope = grad[n * 64 : (n + 1) * 64, :]
        high = slope.astype(BF16)
        low = (slope - high.astype(F32)).astype(BF16)
        part[block] = dot(high, dist_weight, TN) + dot(low, dist_weight, TN)
    values = got[...].astype(F32)
    for z in range(8):
        for y in range(4):
            at = z * 88 + 72 + y * 4
            slopes[y * 32 + z * 4 : y * 32 + z * 4 + 4, :] = values[at : at + 4]
    there = slopes[...].astype(BF16)
    none = jnp.zeros((64, 128), BF16)
    first = dot(there, jnp.concatenate([dist_weight, none], axis=0), NN)
    second = dot(there, jnp.concatenate([none, dist_weight], axis=0), NN)
    device = lax.broadcasted_iota(jnp.int32, (128, 128), 0) * 2
    results = (
        part[0] + jnp.where(device < place[0], first, 0.0),
        jnp.where(device <= place[0], second, first),
        part[2],
        part[3] + jnp.where(device > place[0], second, 0.0),
    )
    for block in range(4):
        order[pl.ds(block // 2 * 256 + block % 2, 128, stride=2), :] = results[block]
    grad_pair[...] = order[0:512, :]
    weights, total = add_sums(values, 8)
    grad_weight[...] = weights * (1.0 / 256)
    loss[0] = total[0, 0] * (1.0 / 65536)


def run(kernel, outs, scratch, args, **specs):
    shapes = [jax.ShapeDtypeStruct(s, d) for s, d in outs]
    moved = sum(x.size * x.dtype.itemsize for x in args)
    scratch = [pltpu.VMEM(*s) if isinstance(s, tuple) else s for s in scratch]
    return pl.pallas_call(
        kernel,
        out_shape=shapes,
        scratch_shapes=scratch,
        compiler_params=pltpu.CompilerParams(vmem_limit_bytes=24 * 1024 * 1024),
        cost_estimate=pl.CostEstimate(flops=10_000_000, bytes_accessed=moved, transcendentals=0),
        **specs,
    )(*args)


VMEM, FAR = pl.BlockSpec(memory_space=pltpu.VMEM), pl.BlockSpec(memory_space=pl.ANY)
SMEM = pl.BlockSpec(memory_space=pltpu.SMEM)


def pack(place, *args):
    scratch = [(arg.shape, arg.dtype) for arg in args]
    scratch += [((520, 128), F32), ((1296, 128), F32), ((16, 256), F32)]
    scratch += [pltpu.SemaphoreType.DMA((13,))]
    outs = [
        ((1280, 128), BF16),
        ((256, 128), F32),
        ((512, 128), F32),
        ((512, 128), F32),
        ((24, 128), F32),
        ((320, 128), BF16),
    ]
    args = [pltpu.with_memory_space_constraint(arg, pltpu.HBM) for arg in args]
    return run(pack_kernel, outs, scratch, (place, *args), in_specs=[SMEM] + [FAR] * 13)


def triangle(*args):
    outs = [((768, 128), BF16), ((256, 128), F32), ((256, 128), F32)]
    return run(triangle_kernel, outs, [((1296, 128), F32), ((784, 128), F32)], args)


def head(*args):
    outs = [((512, 128), BF16), ((192, 128), F32), ((1280, 128), BF16)]
    scratch = [((784, 128), F32), ((136, 128), F32)]
    return run(head_kernel, outs, scratch, args, in_specs=[VMEM] * 6 + [SMEM] + [VMEM])


def middle(got):
    return run(middle_kernel, [((704, 128), BF16)], [((136, 128), F32)], (got,))[0]


def last(*args):
    outs = [((64, 128), F32), ((1,), F32), ((512, 128), F32), ((512, 128), BF16)]
    scratch = [((128, 128), F32), ((520, 128), F32), ((520, 128), F32)]
    specs = {"in_specs": [VMEM] * 3 + [SMEM, VMEM], "out_specs": [VMEM, SMEM, VMEM, VMEM]}
    return run(last_kernel, outs, scratch, args, **specs)


def exchange(values, axes):
    return lax.all_to_all(values, axes, 0, 0, tiled=True)


def on_device(
    pair,
    chain,
    targets,
    pair_mask,
    ln_in_gain,
    ln_in_bias,
    in_weight,
    out_gate_weight,
    ln_out_gain,
    ln_out_bias,
    out_weight,
    dist_weight,
    dist_bias,
):
    place = (lax.axis_index(GROUP) * 2).reshape(1)
    row = lambda values: values.reshape(1, values.shape[0])
    send, labels, base, gate, marks, heavy = pack(
        place,
        targets,
        pair_mask,
        row(chain),
        pair.reshape(512, 128),
        row(ln_in_gain),
        row(ln_in_bias),
        row(ln_out_gain),
        row(ln_out_bias),
        row(dist_bias),
        in_weight,
        out_gate_weight,
        out_weight,
        jnp.swapaxes(dist_weight, 0, 1),
    )
    got = exchange(send.reshape(128, 5, 2, 128), GROUP).reshape(1280, 128)
    products, back_base, back_gate = triangle(got, labels, marks, heavy)
    hidden = exchange(products.reshape(128, 3, 2, 128), GROUP).reshape(768, 128)
    updated, grad, total = head(hidden, base, gate, back_base, back_gate, marks, place, heavy)
    total = middle(exchange(total.reshape(16, 80, 128), PLANE).reshape(1280, 128))
    total = exchange(total.reshape(8, 88, 128), "zlo").reshape(704, 128)
    grad_weight, loss, grad_pair, pair_out = last(total, updated, grad, place, heavy)
    return (
        pair_out.reshape(2, 256, 128),
        grad_pair.reshape(2, 256, 128),
        jnp.swapaxes(grad_weight, 0, 1),
        loss,
    )


def solution(mesh):
    fine = Mesh(mesh.devices.reshape(2, 2, 4, 8, 4), EVERY)
    part = ("zhi", "core")
    in_specs = (
        P(EVERY, None, None),
        P(part),
        P(EVERY, None),
        P(EVERY, None),
        P(),
        P(),
        P(),
        P(),
        P(),
        P(),
        P(),
        P(part, None),
        P(),
    )
    out_specs = (
        P(EVERY, None, None),
        P(EVERY, None, None),
        P(part, None),
        P(part),
    )
    return jax.shard_map(
        on_device, mesh=fine, in_specs=in_specs, out_specs=out_specs, check_vma=False
    )
```

```python
import jax
import jax.numpy as jnp
from jax import lax
from jax.experimental import pallas as pl
from jax.experimental.pallas import tpu as pltpu
from jax.sharding import Mesh
from jax.sharding import PartitionSpec as P

EVERY = ("zhi", "core", "y", "zlo", "x")
GROUP = ("y", "zlo", "x")
PLANE = ("y", "x")
BF16, F32 = jnp.bfloat16, jnp.float32
TN = (((0,), (0,)), ((), ()))
NT = (((1,), (1,)), ((), ()))
NN = (((1,), (0,)), ((), ()))
TT = (((0,), (1,)), ((), ()))


def dot(left, right, dims):
    return lax.dot_general(left, right, dims, preferred_element_type=F32)


def norm_lanes(values, gain, bias):
    center = jnp.mean(values, axis=1, keepdims=True)
    spread = jnp.mean(jnp.square(values - center), axis=1, keepdims=True)
    return (values - center) * lax.rsqrt(spread + 1e-05) * gain + bias


def sigmoid(values):
    return 0.5 * jnp.tanh(0.5 * values) + 0.5


def picker(parity):
    rows = lax.broadcasted_iota(jnp.int32, (128, 256), 0)
    columns = lax.broadcasted_iota(jnp.int32, (128, 256), 1)
    return (columns == 2 * rows + parity).astype(F32).astype(BF16)


def pack_kernel(place, *refs):
    far, (send, labels, base, gate, marks, heavy) = refs[:13], refs[13:19]
    near, (flat, rows, own, sems) = refs[19:32], refs[32:]
    targets, mask, chain, pair, gain, bias, out_gain, out_bias, dist_bias = near[:9]
    in_weight, gate_weight, out_weight, dist_weight = near[9:]
    copies = [pltpu.make_async_copy(far[n], near[n], sems.at[n]) for n in range(13)]
    for n in (3, 9, 0, 1, 2, 4, 5, 6, 7, 8, 10, 11, 12):
        copies[n].start()
    lower = lax.broadcasted_iota(jnp.int32, (128, 128), 0) * 2 <= place[0]
    pickers = picker(0), picker(1)
    for copy in copies[:3]:
        copy.wait()
    maskf = mask[...].astype(F32)
    label = jnp.where(mask[...] > 0, targets[...].astype(F32), 64.0)
    first, second, third = (
        dot(pickers[ir], jnp.broadcast_to(label[jr : jr + 1], (128, 256)).astype(BF16), NT)
        for ir, jr in ((0, 0), (1, 0), (1, 1))
    )
    labels[0:128, :] = jnp.where(lower, first, second)
    labels[128:256, :] = jnp.where(lower, second, third)
    own[...] = jnp.zeros_like(own)
    own[0:2, :] = targets[...].astype(F32)
    own[2:4, :] = maskf
    columns = lax.broadcasted_iota(jnp.int32, (1, 256), 1)
    for r in range(2):
        here = jnp.sum(jnp.where(columns == place[0] + r, chain[...], 0), axis=1, keepdims=True)
        own[4 + r : 5 + r, :] = 1.0 + (chain[...] != here).astype(F32)
    even, odd = (dot(own[...].astype(BF16), pickers[jr], NT) for jr in range(2))
    lanes = lax.broadcasted_iota(jnp.int32, (1, 128), 1) * 2
    higher, same = lanes >= place[0], lanes == place[0]
    target, valid, factor = (
        (
            jnp.where(higher, even[at : at + 1], even[at + 1 : at + 2]),
            jnp.where(higher, even[at + 1 : at + 2], odd[at + 1 : at + 2]),
            odd[at + 1 : at + 2],
        )
        for at in (0, 2, 4)
    )
    alone = jnp.where(same, valid[2] * factor[2], 0.0)
    marks[...] = jnp.zeros((24, 128), F32)
    for group in range(2):
        marks[group : group + 1, :] = valid[group] * factor[group]
        marks[3 + group : 4 + group, :] = factor[group]
    marks[2:3, :] = alone
    marks[5:6, :] = alone
    for group in range(3):
        marks[6 + group : 7 + group, :] = target[group]
    copies[3].wait()
    flat[0:512, :] = pair[...].astype(F32)
    for block in range(4):
        base[block * 128 : (block + 1) * 128, :] = flat[
            pl.ds(block // 2 * 256 + block % 2, 128, stride=2), :
        ]
    first, second, third = (
        flat[pl.ds(jr * 256 + ir, 128, stride=2), :] for ir, jr in ((0, 0), (1, 0), (1, 1))
    )
    rows[pl.ds(8, 128, stride=10), :] = jnp.where(lower, first, second)
    rows[pl.ds(9, 128, stride=10), :] = jnp.where(lower, second, third)
    for n in (4, 5, 9):
        copies[n].wait()
    normed = norm_lanes(flat[0:512, :], gain[...], bias[...]).astype(BF16)
    proj = dot(in_weight[...], normed, TT)
    for n in range(4):
        r, half = n // 2, n % 2
        at = slice(n * 128, (n + 1) * 128)
        here = sigmoid(proj[256:, at]) * maskf[r : r + 1, half * 128 : (half + 1) * 128]
        here = proj[:256, at] * here
        for side in range(2):
            rows[pl.ds(side * 4 + n, 128, stride=10), :] = here[side * 128 : (side + 1) * 128]
    send[...] = rows[0:1280, :].astype(BF16)
    for n in (6, 7, 8, 10, 11, 12):
        copies[n].wait()
    marks[16:17, :] = out_gain[...]
    marks[17:18, :] = out_bias[...]
    marks[18:19, :64] = dist_bias[...]
    marks[19:20, :] = gain[...]
    marks[20:21, :] = bias[...]
    heavy[0:128, :] = gate_weight[...]
    heavy[128:256, :] = out_weight[...]
    heavy[256:320, :] = dist_weight[...]
    flat[0:512, :] = sigmoid(dot(normed, gate_weight[...], NN))
    for block in range(4):
        gate[block * 128 : (block + 1) * 128, :] = flat[
            pl.ds(block // 2 * 256 + block % 2, 128, stride=2), :
        ]


def triangle_kernel(got, labels, marks, heavy, send, base, gate, rows, products):
    rows[0:1280, :] = got[...].astype(F32)
    sides = []
    for side in range(2):
        halves = []
        for half in range(2):
            parts = [
                rows[pl.ds(side * 4 + r * 2 + half, 128, stride=10), :].astype(BF16)
                for r in range(2)
            ]
            halves.append(jnp.concatenate(parts, axis=0))
        sides.append(jnp.concatenate(halves, axis=1))
    mixed = dot(sides[0], sides[1], NT)
    mirrored = dot(sides[1], sides[0], NT)
    for r in range(2):
        for jr in range(2):
            products[pl.ds(r * 2 + jr, 128, stride=6), :] = mixed[
                r * 128 : (r + 1) * 128, jr * 128 : (jr + 1) * 128
            ]
    first, second, third = mirrored[:128, :128], mirrored[128:, :128], mirrored[128:, 128:]
    lane = lax.broadcasted_iota(jnp.int32, (128, 128), 1)
    device = lax.broadcasted_iota(jnp.int32, (128, 128), 0)
    products[pl.ds(4, 128, stride=6), :] = jnp.where(
        lane == device, labels[0:128, :], jnp.where(lane > device, first, second)
    )
    products[pl.ds(5, 128, stride=6), :] = jnp.where(
        lane == device, labels[128:256, :], jnp.where(lane > device, second, third)
    )
    send[...] = products[0:768, :].astype(BF16)
    base[0:128, :] = rows[pl.ds(8, 128, stride=10), :]
    base[128:256, :] = rows[pl.ds(9, 128, stride=10), :]
    normed = norm_lanes(base[...], marks[19:20, :], marks[20:21, :]).astype(BF16)
    gate[...] = sigmoid(dot(normed, heavy[0:128, :], NN))


def message(weights, loss, others):
    row = lax.broadcasted_iota(jnp.int32, (8, 128), 0)
    high = loss.astype(BF16).astype(F32)
    terms = jnp.where(row == 0, high, jnp.where(row == 1, loss - high, 0.0))
    pieces = [piece for other in others for piece in (weights, terms, other)]
    return jnp.concatenate(pieces, axis=0).astype(BF16)


def add_sums(values, peers):
    sums = jnp.sum(values.reshape(peers, values.shape[0] // peers, 128), axis=0)
    return sums[:64], sums[64:65, 0:1] + sums[65:66, 0:1]


def head_kernel(
    got, base, gate, back_base, back_gate, marks, place, heavy,
    updated, grad, total, hidden, slopes,
):
    hidden[0:768, :] = got[...].astype(F32)
    columns = jnp.transpose(marks[16:24, :])
    gain, bias, dist_bias = columns[:, 0:1], columns[:, 1:2], columns[:64, 2:3]
    q = []
    kept = []
    lanes = lax.broadcasted_iota(jnp.int32, (128, 128), 1) * 2
    chosen = (lanes[:16] == place[0]).astype(F32).astype(BF16)
    heres = [hidden[pl.ds(block, 128, stride=6), :] for block in range(6)]
    labels = [dot(chosen, heres[4 + group].astype(BF16), NT)[0:1] for group in range(2)]
    for group in range(2):
        heres[4 + group] = jnp.where(lanes == place[0], heres[group], heres[4 + group])
    normeds = []
    for here in heres:
        center = jnp.mean(here, axis=0, keepdims=True)
        spread = jnp.mean(jnp.square(here - center), axis=0, keepdims=True)
        normed = (here - center) * lax.rsqrt(spread + 1e-05)
        normeds.append((normed * gain + bias).astype(BF16))
    update = dot(jnp.concatenate(normeds, axis=1), heavy[128:256, :], TN)
    sums = (base[...] + gate[...] * update[:512]).astype(BF16)
    back_sums = (back_base[...] + back_gate[...] * update[512:]).astype(BF16)
    updated[...] = sums
    sums = jnp.concatenate([sums, back_sums], axis=0)
    logit = dot(heavy[256:320, :], sums, NT)
    for block in range(6):
        at = slice(block * 128, (block + 1) * 128)
        q.append(logit[:, at])
        kept.append(sums[at])
    lanes = lanes[:64]
    higher = lanes >= place[0]
    pairs = (
        jnp.where(higher, q[0], q[2]) + q[4],
        jnp.where(higher, q[2], q[3]) + q[5],
        q[3] + q[3],
    )
    bins = lax.broadcasted_iota(jnp.int32, (64, 128), 0).astype(F32)
    row = lambda at: marks[at : at + 1, :]
    mirrored = [jnp.where(labels[group] < 63.5, row(3 + group), 0.0) for group in range(2)]
    counted = [jnp.where(lanes[:1] == place[0], 0.0, mirrored[0]), mirrored[1]]
    mirrored.append(row(5))
    labels.append(row(8))
    losses = jnp.zeros((1, 128), F32)
    slope = []
    for group in range(3):
        logits = pairs[group] + dist_bias
        shifted = logits - jnp.max(logits, axis=0, keepdims=True)
        powers = jnp.exp(shifted)
        norms = jnp.sum(powers, axis=0, keepdims=True)
        log_probs = shifted - jnp.log(norms)
        probs = powers * (1.0 / norms)
        onehot = (bins == row(6 + group)).astype(F32)
        onehot_back = (bins == labels[group]).astype(F32)
        losses = losses - row(group) * jnp.sum(onehot * log_probs, axis=0, keepdims=True)
        if group < 2:
            losses = losses - counted[group] * jnp.sum(onehot_back * log_probs, axis=0, keepdims=True)
        slope.append(row(group) * (probs - onehot) + mirrored[group] * (probs - onehot_back))
    blocks = (
        (0, jnp.where(higher, slope[0], 0.0)),
        (2, jnp.where(higher, slope[1], slope[0])),
        (3, jnp.where(higher, 0.0, slope[1]) + slope[2]),
        (4, jnp.where(lanes == place[0], 0.0, slope[0])),
        (5, slope[1]),
    )
    weights = jnp.zeros((64, 128), F32)
    for block, values in blocks:
        high = values.astype(BF16)
        low = (values - high.astype(F32)).astype(BF16)
        weights = weights + dot(high, kept[block], NN) + dot(low, kept[block], NN)
    for n in range(3):
        grad[n * 64 : (n + 1) * 64, :] = blocks[n][1]
    slopes[0:128, :] = jnp.transpose(jnp.concatenate(slope[:2], axis=0))
    others = [slopes[pl.ds(y * 32 + x, 8, stride=4), :] for y in range(4) for x in range(4)]
    total[...] = message(weights, jnp.sum(losses, axis=1, keepdims=True), others)


def middle_kernel(got, send, slopes):
    values = got[...].astype(F32)
    slopes[0:128, :] = values.reshape(16, 80, 128)[:, 72:80].reshape(128, 128)
    weights, loss = add_sums(values, 16)
    send[...] = message(weights, loss, [slopes[pl.ds(z, 16, stride=8), :] for z in range(8)])


def last_kernel(
    got, updated, grad, place, heavy, grad_weight, loss, grad_pair, pair_out,
    slopes, rows, order,
):
    for block in range(4):
        rows[pl.ds(block // 2 * 256 + block % 2, 128, stride=2), :] = updated[
            block * 128 : (block + 1) * 128, :
        ].astype(F32)
    pair_out[...] = rows[0:512, :].astype(BF16)
    dist_weight = heavy[256:320, :]
    part = {}
    for n, block in enumerate((0, 2, 3)):
        slope = grad[n * 64 : (n + 1) * 64, :]
        high = slope.astype(BF16)
        low = (slope - high.astype(F32)).astype(BF16)
        part[block] = dot(high, dist_weight, TN) + dot(low, dist_weight, TN)
    values = got[...].astype(F32)
    for z in range(8):
        for y in range(4):
            at = z * 88 + 72 + y * 4
            slopes[y * 32 + z * 4 : y * 32 + z * 4 + 4, :] = values[at : at + 4]
    there = slopes[...].astype(BF16)
    none = jnp.zeros((64, 128), BF16)
    first = dot(there, jnp.concatenate([dist_weight, none], axis=0), NN)
    second = dot(there, jnp.concatenate([none, dist_weight], axis=0), NN)
    device = lax.broadcasted_iota(jnp.int32, (128, 128), 0) * 2
    results = (
        part[0] + jnp.where(device < place[0], first, 0.0),
        jnp.where(device <= place[0], second, first),
        part[2],
        part[3] + jnp.where(device > place[0], second, 0.0),
    )
    for block in range(4):
        order[pl.ds(block // 2 * 256 + block % 2, 128, stride=2), :] = results[block]
    grad_pair[...] = order[0:512, :]
    weights, total = add_sums(values, 8)
    grad_weight[...] = weights * (1.0 / 256)
    loss[0] = total[0, 0] * (1.0 / 65536)


def run(kernel, outs, scratch, args, **specs):
    shapes = [jax.ShapeDtypeStruct(s, d) for s, d in outs]
    moved = sum(x.size * x.dtype.itemsize for x in args)
    scratch = [pltpu.VMEM(*s) if isinstance(s, tuple) else s for s in scratch]
    return pl.pallas_call(
        kernel,
        out_shape=shapes,
        scratch_shapes=scratch,
        compiler_params=pltpu.CompilerParams(vmem_limit_bytes=24 * 1024 * 1024),
        cost_estimate=pl.CostEstimate(flops=10_000_000, bytes_accessed=moved, transcendentals=0),
        **specs,
    )(*args)


VMEM, FAR = pl.BlockSpec(memory_space=pltpu.VMEM), pl.BlockSpec(memory_space=pl.ANY)
SMEM = pl.BlockSpec(memory_space=pltpu.SMEM)


def pack(place, *args):
    scratch = [(arg.shape, arg.dtype) for arg in args]
    scratch += [((520, 128), F32), ((1296, 128), F32), ((16, 256), F32)]
    scratch += [pltpu.SemaphoreType.DMA((13,))]
    outs = [
        ((1280, 128), BF16),
        ((256, 128), F32),
        ((512, 128), F32),
        ((512, 128), F32),
        ((24, 128), F32),
        ((320, 128), BF16),
    ]
    args = [pltpu.with_memory_space_constraint(arg, pltpu.HBM) for arg in args]
    return run(pack_kernel, outs, scratch, (place, *args), in_specs=[SMEM] + [FAR] * 13)


def triangle(*args):
    outs = [((768, 128), BF16), ((256, 128), F32), ((256, 128), F32)]
    return run(triangle_kernel, outs, [((1296, 128), F32), ((784, 128), F32)], args)


def head(*args):
    outs = [((512, 128), BF16), ((192, 128), F32), ((1280, 128), BF16)]
    scratch = [((784, 128), F32), ((136, 128), F32)]
    return run(head_kernel, outs, scratch, args, in_specs=[VMEM] * 6 + [SMEM] + [VMEM])


def middle(got):
    return run(middle_kernel, [((704, 128), BF16)], [((136, 128), F32)], (got,))[0]


def last(*args):
    outs = [((64, 128), F32), ((1,), F32), ((512, 128), F32), ((512, 128), BF16)]
    scratch = [((128, 128), F32), ((520, 128), F32), ((520, 128), F32)]
    specs = {"in_specs": [VMEM] * 3 + [SMEM, VMEM], "out_specs": [VMEM, SMEM, VMEM, VMEM]}
    return run(last_kernel, outs, scratch, args, **specs)


def exchange(values, axes):
    return lax.all_to_all(values, axes, 0, 0, tiled=True)


def on_device(
    pair,
    chain,
    targets,
    pair_mask,
    ln_in_gain,
    ln_in_bias,
    in_weight,
    out_gate_weight,
    ln_out_gain,
    ln_out_bias,
    out_weight,
    dist_weight,
    dist_bias,
):
    place = (lax.axis_index(GROUP) * 2).reshape(1)
    row = lambda values: values.reshape(1, values.shape[0])
    send, labels, base, gate, marks, heavy = pack(
        place,
        targets,
        pair_mask,
        row(chain),
        pair.reshape(512, 128),
        row(ln_in_gain),
        row(ln_in_bias),
        row(ln_out_gain),
        row(ln_out_bias),
        row(dist_bias),
        in_weight,
        out_gate_weight,
        out_weight,
        jnp.swapaxes(dist_weight, 0, 1),
    )
    got = exchange(send.reshape(128, 5, 2, 128), GROUP).reshape(1280, 128)
    products, back_base, back_gate = triangle(got, labels, marks, heavy)
    hidden = exchange(products.reshape(128, 3, 2, 128), GROUP).reshape(768, 128)
    updated, grad, total = head(hidden, base, gate, back_base, back_gate, marks, place, heavy)
    total = middle(exchange(total.reshape(16, 80, 128), PLANE).reshape(1280, 128))
    total = exchange(total.reshape(8, 88, 128), "zlo").reshape(704, 128)
    grad_weight, loss, grad_pair, pair_out = last(total, updated, grad, place, heavy)
    return (
        pair_out.reshape(2, 256, 128),
        grad_pair.reshape(2, 256, 128),
        jnp.swapaxes(grad_weight, 0, 1),
        loss,
    )


def solution(mesh):
    fine = Mesh(mesh.devices.reshape(2, 2, 4, 8, 4), EVERY)
    part = ("zhi", "core")
    in_specs = (
        P(EVERY, None, None),
        P(part),
        P(EVERY, None),
        P(EVERY, None),
        P(),
        P(),
        P(),
        P(),
        P(),
        P(),
        P(),
        P(part, None),
        P(),
    )
    out_specs = (
        P(EVERY, None, None),
        P(EVERY, None, None),
        P(part, None),
        P(part),
    )
    return jax.shard_map(
        on_device, mesh=fine, in_specs=in_specs, out_specs=out_specs, check_vma=False
    )
```

```python
import jax
import jax.numpy as jnp
from jax import lax
from jax.experimental import pallas as pl
from jax.experimental.pallas import tpu as pltpu
from jax.sharding import Mesh
from jax.sharding import PartitionSpec as P

EVERY = ("zhi", "core", "y", "zlo", "x")
GROUP = ("y", "zlo", "x")
PLANE = ("y", "x")
BF16, F32 = jnp.bfloat16, jnp.float32
TN = (((0,), (0,)), ((), ()))
NT = (((1,), (1,)), ((), ()))
NN = (((1,), (0,)), ((), ()))
TT = (((0,), (1,)), ((), ()))


def dot(left, right, dims):
    return lax.dot_general(left, right, dims, preferred_element_type=F32)


def norm_lanes(values, gain, bias):
    center = jnp.mean(values, axis=1, keepdims=True)
    spread = jnp.mean(jnp.square(values - center), axis=1, keepdims=True)
    return (values - center) * lax.rsqrt(spread + 1e-05) * gain + bias


def picker(parity):
    rows = lax.broadcasted_iota(jnp.int32, (128, 256), 0)
    columns = lax.broadcasted_iota(jnp.int32, (128, 256), 1)
    return (columns == 2 * rows + parity).astype(F32).astype(BF16)


def pack_kernel(place, *refs):
    far, (send, labels, base, gate, marks, heavy) = refs[:13], refs[13:19]
    near, (flat, rows, own, sems) = refs[19:32], refs[32:]
    targets, mask, chain, pair, gain, bias, out_gain, out_bias, dist_bias = near[:9]
    in_weight, gate_weight, out_weight, dist_weight = near[9:]
    copies = [pltpu.make_async_copy(far[n], near[n], sems.at[n]) for n in range(13)]
    for copy in copies:
        copy.start()
    lower = lax.broadcasted_iota(jnp.int32, (128, 128), 0) * 2 <= place[0]
    pickers = picker(0), picker(1)
    for copy in copies[:3]:
        copy.wait()
    maskf = mask[...].astype(F32)
    label = jnp.where(mask[...] > 0, targets[...].astype(F32), 64.0)
    first, second, third = (
        dot(pickers[ir], jnp.broadcast_to(label[jr : jr + 1], (128, 256)).astype(BF16), NT)
        for ir, jr in ((0, 0), (1, 0), (1, 1))
    )
    labels[0:128, :] = jnp.where(lower, first, second)
    labels[128:256, :] = jnp.where(lower, second, third)
    own[...] = jnp.zeros_like(own)
    own[0:2, :] = targets[...].astype(F32)
    own[2:4, :] = maskf
    columns = lax.broadcasted_iota(jnp.int32, (1, 256), 1)
    for r in range(2):
        here = jnp.sum(jnp.where(columns == place[0] + r, chain[...], 0), axis=1, keepdims=True)
        own[4 + r : 5 + r, :] = 1.0 + (chain[...] != here).astype(F32)
    even, odd = (dot(own[...].astype(BF16), pickers[jr], NT) for jr in range(2))
    lanes = lax.broadcasted_iota(jnp.int32, (1, 128), 1) * 2
    higher, same = lanes >= place[0], lanes == place[0]
    target, valid, factor = (
        (
            jnp.where(higher, even[at : at + 1], even[at + 1 : at + 2]),
            jnp.where(higher, even[at + 1 : at + 2], odd[at + 1 : at + 2]),
            odd[at + 1 : at + 2],
        )
        for at in (0, 2, 4)
    )
    alone = jnp.where(same, valid[2] * factor[2], 0.0)
    marks[...] = jnp.zeros((24, 128), F32)
    for group in range(2):
        marks[group : group + 1, :] = valid[group] * factor[group]
        marks[3 + group : 4 + group, :] = factor[group]
    marks[2:3, :] = alone
    marks[5:6, :] = alone
    for group in range(3):
        marks[6 + group : 7 + group, :] = target[group]
    copies[3].wait()
    flat[0:512, :] = pair[...].astype(F32)
    for block in range(4):
        base[block * 128 : (block + 1) * 128, :] = flat[
            pl.ds(block // 2 * 256 + block % 2, 128, stride=2), :
        ]
    first, second, third = (
        flat[pl.ds(jr * 256 + ir, 128, stride=2), :] for ir, jr in ((0, 0), (1, 0), (1, 1))
    )
    rows[pl.ds(8, 128, stride=10), :] = jnp.where(lower, first, second)
    rows[pl.ds(9, 128, stride=10), :] = jnp.where(lower, second, third)
    for copy in copies[4:]:
        copy.wait()
    marks[16:17, :] = out_gain[...]
    marks[17:18, :] = out_bias[...]
    marks[18:19, :64] = dist_bias[...]
    marks[19:20, :] = gain[...]
    marks[20:21, :] = bias[...]
    heavy[0:128, :] = gate_weight[...]
    heavy[128:256, :] = out_weight[...]
    heavy[256:320, :] = dist_weight[...]
    normed = norm_lanes(flat[0:512, :], gain[...], bias[...]).astype(BF16)
    proj = dot(in_weight[...], normed, TT)
    for n in range(4):
        r, half = n // 2, n % 2
        at = slice(n * 128, (n + 1) * 128)
        here = jax.nn.sigmoid(proj[256:, at]) * maskf[r : r + 1, half * 128 : (half + 1) * 128]
        here = proj[:256, at] * here
        for side in range(2):
            rows[pl.ds(side * 4 + n, 128, stride=10), :] = here[side * 128 : (side + 1) * 128]
    send[...] = rows[0:1280, :].astype(BF16)
    flat[0:512, :] = jax.nn.sigmoid(dot(normed, gate_weight[...], NN))
    for block in range(4):
        gate[block * 128 : (block + 1) * 128, :] = flat[
            pl.ds(block // 2 * 256 + block % 2, 128, stride=2), :
        ]


def triangle_kernel(got, labels, marks, heavy, send, base, gate, rows, products):
    rows[0:1280, :] = got[...].astype(F32)
    sides = []
    for side in range(2):
        halves = []
        for half in range(2):
            parts = [
                rows[pl.ds(side * 4 + r * 2 + half, 128, stride=10), :].astype(BF16)
                for r in range(2)
            ]
            halves.append(jnp.concatenate(parts, axis=0))
        sides.append(jnp.concatenate(halves, axis=1))
    mixed = dot(sides[0], sides[1], NT)
    mirrored = dot(sides[1], sides[0], NT)
    for r in range(2):
        for jr in range(2):
            products[pl.ds(r * 2 + jr, 128, stride=6), :] = mixed[
                r * 128 : (r + 1) * 128, jr * 128 : (jr + 1) * 128
            ]
    first, second, third = mirrored[:128, :128], mirrored[128:, :128], mirrored[128:, 128:]
    lane = lax.broadcasted_iota(jnp.int32, (128, 128), 1)
    device = lax.broadcasted_iota(jnp.int32, (128, 128), 0)
    products[pl.ds(4, 128, stride=6), :] = jnp.where(
        lane == device, labels[0:128, :], jnp.where(lane > device, first, second)
    )
    products[pl.ds(5, 128, stride=6), :] = jnp.where(
        lane == device, labels[128:256, :], jnp.where(lane > device, second, third)
    )
    send[...] = products[0:768, :].astype(BF16)
    base[0:128, :] = rows[pl.ds(8, 128, stride=10), :]
    base[128:256, :] = rows[pl.ds(9, 128, stride=10), :]
    normed = norm_lanes(base[...], marks[19:20, :], marks[20:21, :]).astype(BF16)
    gate[...] = jax.nn.sigmoid(dot(normed, heavy[0:128, :], NN))


def message(weights, loss, others):
    row = lax.broadcasted_iota(jnp.int32, (64, 128), 0)
    lane = lax.broadcasted_iota(jnp.int32, (1, 128), 1)
    high = loss.astype(BF16).astype(F32)
    terms = jnp.where(lane == 0, high, jnp.where(lane == 1, loss - high, 0.0))
    sums = jnp.where(row == 63, terms, weights)
    pieces = [piece for other in others for piece in (sums, other)]
    return jnp.concatenate(pieces, axis=0).astype(BF16)


def add_sums(values, peers):
    sums = jnp.sum(values.reshape(peers, values.shape[0] // peers, 128)[:, :64], axis=0)
    return sums, sums[63:64, 0:1] + sums[63:64, 1:2]


def head_kernel(
    got, base, gate, back_base, back_gate, marks, place, heavy,
    updated, grad, total, hidden, slopes,
):
    hidden[0:768, :] = got[...].astype(F32)
    columns = jnp.transpose(marks[16:24, :])
    gain, bias, dist_bias = columns[:, 0:1], columns[:, 1:2], columns[:64, 2:3]
    q = []
    kept = []
    lanes = lax.broadcasted_iota(jnp.int32, (128, 128), 1) * 2
    chosen = (lanes[:16] == place[0]).astype(F32).astype(BF16)
    heres = [hidden[pl.ds(block, 128, stride=6), :] for block in range(6)]
    labels = [dot(chosen, heres[4 + group].astype(BF16), NT)[0:1] for group in range(2)]
    for group in range(2):
        heres[4 + group] = jnp.where(lanes == place[0], heres[group], heres[4 + group])
    normeds = []
    for here in heres:
        center = jnp.mean(here, axis=0, keepdims=True)
        spread = jnp.mean(jnp.square(here - center), axis=0, keepdims=True)
        normed = (here - center) * lax.rsqrt(spread + 1e-05)
        normeds.append((normed * gain + bias).astype(BF16))
    update = dot(jnp.concatenate(normeds, axis=1), heavy[128:256, :], TN)
    sums = (base[...] + gate[...] * update[:512]).astype(BF16)
    back_sums = (back_base[...] + back_gate[...] * update[512:]).astype(BF16)
    updated[...] = sums
    sums = jnp.concatenate([sums, back_sums], axis=0)
    logit = dot(heavy[256:320, :], sums, NT)
    for block in range(6):
        at = slice(block * 128, (block + 1) * 128)
        q.append(logit[:, at])
        kept.append(sums[at])
    lanes = lanes[:64]
    higher = lanes >= place[0]
    pairs = (
        jnp.where(higher, q[0], q[2]) + q[4],
        jnp.where(higher, q[2], q[3]) + q[5],
        q[3] + q[3],
    )
    bins = lax.broadcasted_iota(jnp.int32, (64, 128), 0).astype(F32)
    row = lambda at: marks[at : at + 1, :]
    mirrored = [jnp.where(labels[group] < 63.5, row(3 + group), 0.0) for group in range(2)]
    counted = [jnp.where(lanes[:1] == place[0], 0.0, mirrored[0]), mirrored[1]]
    mirrored.append(row(5))
    labels.append(row(8))
    losses = jnp.zeros((1, 128), F32)
    slope = []
    for group in range(3):
        logits = pairs[group] + dist_bias
        shifted = logits - jnp.max(logits, axis=0, keepdims=True)
        powers = jnp.exp(shifted)
        norms = jnp.sum(powers, axis=0, keepdims=True)
        log_probs = shifted - jnp.log(norms)
        probs = powers / norms
        onehot = (bins == row(6 + group)).astype(F32)
        onehot_back = (bins == labels[group]).astype(F32)
        losses = losses - row(group) * jnp.sum(onehot * log_probs, axis=0, keepdims=True)
        if group < 2:
            losses = losses - counted[group] * jnp.sum(onehot_back * log_probs, axis=0, keepdims=True)
        slope.append(row(group) * (probs - onehot) + mirrored[group] * (probs - onehot_back))
    blocks = (
        (0, jnp.where(higher, slope[0], 0.0)),
        (2, jnp.where(higher, slope[1], slope[0])),
        (3, jnp.where(higher, 0.0, slope[1]) + slope[2]),
        (4, jnp.where(lanes == place[0], 0.0, slope[0])),
        (5, slope[1]),
    )
    weights = jnp.zeros((64, 128), F32)
    for block, values in blocks:
        high = values.astype(BF16)
        low = (values - high.astype(F32)).astype(BF16)
        weights = weights + dot(high, kept[block], NN) + dot(low, kept[block], NN)
    for n in range(3):
        grad[n * 64 : (n + 1) * 64, :] = blocks[n][1]
    slopes[0:128, :] = jnp.transpose(jnp.concatenate(slope[:2], axis=0))
    others = [slopes[pl.ds(y * 32 + x, 8, stride=4), :] for y in range(4) for x in range(4)]
    total[...] = message(weights, jnp.sum(losses, axis=1, keepdims=True), others)


def middle_kernel(got, send, slopes):
    values = got[...].astype(F32)
    slopes[0:128, :] = values.reshape(16, 72, 128)[:, 64:72].reshape(128, 128)
    weights, loss = add_sums(values, 16)
    send[...] = message(weights, loss, [slopes[pl.ds(z, 16, stride=8), :] for z in range(8)])


def last_kernel(
    got, updated, grad, place, heavy, grad_weight, loss, grad_pair, pair_out,
    slopes, rows, order,
):
    for block in range(4):
        rows[pl.ds(block // 2 * 256 + block % 2, 128, stride=2), :] = updated[
            block * 128 : (block + 1) * 128, :
        ].astype(F32)
    pair_out[...] = rows[0:512, :].astype(BF16)
    dist_weight = heavy[256:320, :]
    part = {}
    for n, block in enumerate((0, 2, 3)):
        slope = grad[n * 64 : (n + 1) * 64, :]
        high = slope.astype(BF16)
        low = (slope - high.astype(F32)).astype(BF16)
        part[block] = dot(high, dist_weight, TN) + dot(low, dist_weight, TN)
    values = got[...].astype(F32)
    for z in range(8):
        for y in range(4):
            at = z * 80 + 64 + y * 4
            slopes[y * 32 + z * 4 : y * 32 + z * 4 + 4, :] = values[at : at + 4]
    there = slopes[...].astype(BF16)
    none = jnp.zeros((64, 128), BF16)
    first = dot(there, jnp.concatenate([dist_weight, none], axis=0), NN)
    second = dot(there, jnp.concatenate([none, dist_weight], axis=0), NN)
    device = lax.broadcasted_iota(jnp.int32, (128, 128), 0) * 2
    results = (
        part[0] + jnp.where(device < place[0], first, 0.0),
        jnp.where(device <= place[0], second, first),
        part[2],
        part[3] + jnp.where(device > place[0], second, 0.0),
    )
    for block in range(4):
        order[pl.ds(block // 2 * 256 + block % 2, 128, stride=2), :] = results[block]
    grad_pair[...] = order[0:512, :]
    weights, total = add_sums(values, 8)
    row = lax.broadcasted_iota(jnp.int32, (64, 128), 0)
    weights = jnp.where(row == 63, 0.0, weights)
    rest = jnp.sum(weights, axis=0, keepdims=True)
    grad_weight[...] = jnp.where(row == 63, -rest, weights) * (1.0 / 256)
    loss[0] = total[0, 0] * (1.0 / 65536)


def run(kernel, outs, scratch, args, **specs):
    shapes = [jax.ShapeDtypeStruct(s, d) for s, d in outs]
    moved = sum(x.size * x.dtype.itemsize for x in args)
    scratch = [pltpu.VMEM(*s) if isinstance(s, tuple) else s for s in scratch]
    return pl.pallas_call(
        kernel,
        out_shape=shapes,
        scratch_shapes=scratch,
        compiler_params=pltpu.CompilerParams(vmem_limit_bytes=24 * 1024 * 1024),
        cost_estimate=pl.CostEstimate(flops=10_000_000, bytes_accessed=moved, transcendentals=0),
        **specs,
    )(*args)


VMEM, FAR = pl.BlockSpec(memory_space=pltpu.VMEM), pl.BlockSpec(memory_space=pl.ANY)
SMEM = pl.BlockSpec(memory_space=pltpu.SMEM)


def pack(place, *args):
    scratch = [(arg.shape, arg.dtype) for arg in args]
    scratch += [((520, 128), F32), ((1296, 128), F32), ((16, 256), F32)]
    scratch += [pltpu.SemaphoreType.DMA((13,))]
    outs = [
        ((1280, 128), BF16),
        ((256, 128), F32),
        ((512, 128), F32),
        ((512, 128), F32),
        ((24, 128), F32),
        ((320, 128), BF16),
    ]
    args = [pltpu.with_memory_space_constraint(arg, pltpu.HBM) for arg in args]
    return run(pack_kernel, outs, scratch, (place, *args), in_specs=[SMEM] + [FAR] * 13)


def triangle(*args):
    outs = [((768, 128), BF16), ((256, 128), F32), ((256, 128), F32)]
    return run(triangle_kernel, outs, [((1296, 128), F32), ((784, 128), F32)], args)


def head(*args):
    outs = [((512, 128), BF16), ((192, 128), F32), ((1152, 128), BF16)]
    scratch = [((784, 128), F32), ((136, 128), F32)]
    return run(head_kernel, outs, scratch, args, in_specs=[VMEM] * 6 + [SMEM] + [VMEM])


def middle(got):
    return run(middle_kernel, [((640, 128), BF16)], [((136, 128), F32)], (got,))[0]


def last(*args):
    outs = [((64, 128), F32), ((1,), F32), ((512, 128), F32), ((512, 128), BF16)]
    scratch = [((128, 128), F32), ((520, 128), F32), ((520, 128), F32)]
    specs = {"in_specs": [VMEM] * 3 + [SMEM, VMEM], "out_specs": [VMEM, SMEM, VMEM, VMEM]}
    return run(last_kernel, outs, scratch, args, **specs)


def exchange(values, axes):
    return lax.all_to_all(values, axes, 0, 0, tiled=True)


def on_device(
    pair,
    chain,
    targets,
    pair_mask,
    ln_in_gain,
    ln_in_bias,
    in_weight,
    out_gate_weight,
    ln_out_gain,
    ln_out_bias,
    out_weight,
    dist_weight,
    dist_bias,
):
    place = (lax.axis_index(GROUP) * 2).reshape(1)
    row = lambda values: values.reshape(1, values.shape[0])
    send, labels, base, gate, marks, heavy = pack(
        place,
        targets,
        pair_mask,
        row(chain),
        pair.reshape(512, 128),
        row(ln_in_gain),
        row(ln_in_bias),
        row(ln_out_gain),
        row(ln_out_bias),
        row(dist_bias),
        in_weight,
        out_gate_weight,
        out_weight,
        jnp.swapaxes(dist_weight, 0, 1),
    )
    got = exchange(send.reshape(128, 5, 2, 128), GROUP).reshape(1280, 128)
    products, back_base, back_gate = triangle(got, labels, marks, heavy)
    hidden = exchange(products.reshape(128, 3, 2, 128), GROUP).reshape(768, 128)
    updated, grad, total = head(hidden, base, gate, back_base, back_gate, marks, place, heavy)
    total = middle(exchange(total.reshape(16, 72, 128), PLANE).reshape(1152, 128))
    total = exchange(total.reshape(8, 80, 128), "zlo").reshape(640, 128)
    grad_weight, loss, grad_pair, pair_out = last(total, updated, grad, place, heavy)
    return (
        pair_out.reshape(2, 256, 128),
        grad_pair.reshape(2, 256, 128),
        jnp.swapaxes(grad_weight, 0, 1),
        loss,
    )


def solution(mesh):
    fine = Mesh(mesh.devices.reshape(2, 2, 4, 8, 4), EVERY)
    part = ("zhi", "core")
    in_specs = (
        P(EVERY, None, None),
        P(part),
        P(EVERY, None),
        P(EVERY, None),
        P(),
        P(),
        P(),
        P(),
        P(),
        P(),
        P(),
        P(part, None),
        P(),
    )
    out_specs = (
        P(EVERY, None, None),
        P(EVERY, None, None),
        P(part, None),
        P(part),
    )
    return jax.shard_map(
        on_device, mesh=fine, in_specs=in_specs, out_specs=out_specs, check_vma=False
    )
```

```python
import jax
import jax.numpy as jnp
from jax import lax
from jax.experimental import pallas as pl
from jax.experimental.pallas import tpu as pltpu
from jax.sharding import Mesh
from jax.sharding import PartitionSpec as P

EVERY = ("zhi", "core", "y", "zlo", "x")
GROUP = ("y", "zlo", "x")
PLANE = ("y", "x")
BF16, F32 = jnp.bfloat16, jnp.float32
TN = (((0,), (0,)), ((), ()))
NT = (((1,), (1,)), ((), ()))
NN = (((1,), (0,)), ((), ()))
TT = (((0,), (1,)), ((), ()))


def dot(left, right, dims):
    return lax.dot_general(left, right, dims, preferred_element_type=F32)


def norm_lanes(values, gain, bias):
    center = jnp.mean(values, axis=1, keepdims=True)
    spread = jnp.mean(jnp.square(values - center), axis=1, keepdims=True)
    return (values - center) * lax.rsqrt(spread + 1e-05) * gain + bias


def picker(parity):
    rows = lax.broadcasted_iota(jnp.int32, (128, 256), 0)
    columns = lax.broadcasted_iota(jnp.int32, (128, 256), 1)
    return (columns == 2 * rows + parity).astype(F32).astype(BF16)


def pack_kernel(place, *refs):
    far, (send, labels, base, gate, marks, heavy) = refs[:13], refs[13:19]
    near, (flat, rows, own, sems) = refs[19:32], refs[32:]
    targets, mask, chain, pair, gain, bias, out_gain, out_bias, dist_bias = near[:9]
    in_weight, gate_weight, out_weight, dist_weight = near[9:]
    copies = [pltpu.make_async_copy(far[n], near[n], sems.at[n]) for n in range(13)]
    for copy in copies:
        copy.start()
    lower = lax.broadcasted_iota(jnp.int32, (128, 128), 0) * 2 <= place[0]
    pickers = picker(0), picker(1)
    for copy in copies[:3]:
        copy.wait()
    maskf = mask[...].astype(F32)
    label = jnp.where(mask[...] > 0, targets[...].astype(F32), 64.0)
    first, second, third = (
        dot(pickers[ir], jnp.broadcast_to(label[jr : jr + 1], (128, 256)).astype(BF16), NT)
        for ir, jr in ((0, 0), (1, 0), (1, 1))
    )
    labels[0:128, :] = jnp.where(lower, first, second)
    labels[128:256, :] = jnp.where(lower, second, third)
    own[...] = jnp.zeros_like(own)
    own[0:2, :] = targets[...].astype(F32)
    own[2:4, :] = maskf
    columns = lax.broadcasted_iota(jnp.int32, (1, 256), 1)
    for r in range(2):
        here = jnp.sum(jnp.where(columns == place[0] + r, chain[...], 0), axis=1, keepdims=True)
        own[4 + r : 5 + r, :] = 1.0 + (chain[...] != here).astype(F32)
    even, odd = (dot(own[...].astype(BF16), pickers[jr], NT) for jr in range(2))
    lanes = lax.broadcasted_iota(jnp.int32, (1, 128), 1) * 2
    higher, same = lanes >= place[0], lanes == place[0]
    target, valid, factor = (
        (
            jnp.where(higher, even[at : at + 1], even[at + 1 : at + 2]),
            jnp.where(higher, even[at + 1 : at + 2], odd[at + 1 : at + 2]),
            odd[at + 1 : at + 2],
        )
        for at in (0, 2, 4)
    )
    alone = jnp.where(same, valid[2] * factor[2], 0.0)
    marks[...] = jnp.zeros((24, 128), F32)
    for group in range(2):
        marks[group : group + 1, :] = valid[group] * factor[group]
        marks[3 + group : 4 + group, :] = factor[group]
    marks[2:3, :] = alone
    marks[5:6, :] = alone
    for group in range(3):
        marks[6 + group : 7 + group, :] = target[group]
    copies[3].wait()
    flat[0:512, :] = pair[...].astype(F32)
    for block in range(4):
        base[block * 128 : (block + 1) * 128, :] = flat[
            pl.ds(block // 2 * 256 + block % 2, 128, stride=2), :
        ]
    first, second, third = (
        flat[pl.ds(jr * 256 + ir, 128, stride=2), :] for ir, jr in ((0, 0), (1, 0), (1, 1))
    )
    rows[pl.ds(8, 128, stride=10), :] = jnp.where(lower, first, second)
    rows[pl.ds(9, 128, stride=10), :] = jnp.where(lower, second, third)
    for copy in copies[4:]:
        copy.wait()
    marks[16:17, :] = out_gain[...]
    marks[17:18, :] = out_bias[...]
    marks[18:19, :64] = dist_bias[...]
    marks[19:20, :] = gain[...]
    marks[20:21, :] = bias[...]
    heavy[0:128, :] = gate_weight[...]
    heavy[128:256, :] = out_weight[...]
    heavy[256:320, :] = dist_weight[...]
    normed = norm_lanes(flat[0:512, :], gain[...], bias[...]).astype(BF16)
    proj = dot(in_weight[...], normed, TT)
    for n in range(4):
        r, half = n // 2, n % 2
        at = slice(n * 128, (n + 1) * 128)
        here = jax.nn.sigmoid(proj[256:, at]) * maskf[r : r + 1, half * 128 : (half + 1) * 128]
        here = proj[:256, at] * here
        for side in range(2):
            rows[pl.ds(side * 4 + n, 128, stride=10), :] = here[side * 128 : (side + 1) * 128]
    send[...] = rows[0:1280, :].astype(BF16)
    flat[0:512, :] = jax.nn.sigmoid(dot(normed, gate_weight[...], NN))
    for block in range(4):
        gate[block * 128 : (block + 1) * 128, :] = flat[
            pl.ds(block // 2 * 256 + block % 2, 128, stride=2), :
        ]


def triangle_kernel(got, labels, marks, heavy, send, base, gate, rows, products):
    rows[0:1280, :] = got[...].astype(F32)
    sides = []
    for side in range(2):
        halves = []
        for half in range(2):
            parts = [
                rows[pl.ds(side * 4 + r * 2 + half, 128, stride=10), :].astype(BF16)
                for r in range(2)
            ]
            halves.append(jnp.concatenate(parts, axis=0))
        sides.append(jnp.concatenate(halves, axis=1))
    mixed = dot(sides[0], sides[1], NT)
    mirrored = dot(sides[1], sides[0], NT)
    for r in range(2):
        for jr in range(2):
            products[pl.ds(r * 2 + jr, 128, stride=6), :] = mixed[
                r * 128 : (r + 1) * 128, jr * 128 : (jr + 1) * 128
            ]
    first, second, third = mirrored[:128, :128], mirrored[128:, :128], mirrored[128:, 128:]
    lane = lax.broadcasted_iota(jnp.int32, (128, 128), 1)
    device = lax.broadcasted_iota(jnp.int32, (128, 128), 0)
    products[pl.ds(4, 128, stride=6), :] = jnp.where(
        lane == device, labels[0:128, :], jnp.where(lane > device, first, second)
    )
    products[pl.ds(5, 128, stride=6), :] = jnp.where(
        lane == device, labels[128:256, :], jnp.where(lane > device, second, third)
    )
    send[...] = products[0:768, :].astype(BF16)
    base[0:128, :] = rows[pl.ds(8, 128, stride=10), :]
    base[128:256, :] = rows[pl.ds(9, 128, stride=10), :]
    normed = norm_lanes(base[...], marks[19:20, :], marks[20:21, :]).astype(BF16)
    gate[...] = jax.nn.sigmoid(dot(normed, heavy[0:128, :], NN))


def message(weights, loss, others):
    row = lax.broadcasted_iota(jnp.int32, (64, 128), 0)
    lane = lax.broadcasted_iota(jnp.int32, (1, 128), 1)
    high = loss.astype(BF16).astype(F32)
    terms = jnp.where(lane == 0, high, jnp.where(lane == 1, loss - high, 0.0))
    sums = jnp.where(row == 63, terms, weights)
    pieces = [piece for other in others for piece in (sums, other)]
    return jnp.concatenate(pieces, axis=0).astype(BF16)


def add_sums(values, peers):
    sums = jnp.sum(values.reshape(peers, values.shape[0] // peers, 128)[:, :64], axis=0)
    return sums, sums[63:64, 0:1] + sums[63:64, 1:2]


def head_kernel(
    got, base, gate, back_base, back_gate, marks, place, heavy,
    updated, grad, total, hidden, slopes,
):
    hidden[0:768, :] = got[...].astype(F32)
    columns = jnp.transpose(marks[16:24, :])
    gain, bias, dist_bias = columns[:, 0:1], columns[:, 1:2], columns[:64, 2:3]
    q = []
    kept = []
    lanes = lax.broadcasted_iota(jnp.int32, (128, 128), 1) * 2
    chosen = (lanes[:16] == place[0]).astype(F32).astype(BF16)
    heres = [hidden[pl.ds(block, 128, stride=6), :] for block in range(6)]
    labels = [dot(chosen, heres[4 + group].astype(BF16), NT)[0:1] for group in range(2)]
    for group in range(2):
        heres[4 + group] = jnp.where(lanes == place[0], heres[group], heres[4 + group])
    normeds = []
    for here in heres:
        center = jnp.mean(here, axis=0, keepdims=True)
        spread = jnp.mean(jnp.square(here - center), axis=0, keepdims=True)
        normed = (here - center) * lax.rsqrt(spread + 1e-05)
        normeds.append((normed * gain + bias).astype(BF16))
    update = dot(jnp.concatenate(normeds, axis=1), heavy[128:256, :], TN)
    sums = (base[...] + gate[...] * update[:512]).astype(BF16)
    back_sums = (back_base[...] + back_gate[...] * update[512:]).astype(BF16)
    updated[...] = sums
    sums = jnp.concatenate([sums, back_sums], axis=0)
    logit = dot(heavy[256:320, :], sums, NT)
    for block in range(6):
        at = slice(block * 128, (block + 1) * 128)
        q.append(logit[:, at])
        kept.append(sums[at])
    lanes = lanes[:64]
    higher = lanes >= place[0]
    pairs = (
        jnp.where(higher, q[0], q[2]) + q[4],
        jnp.where(higher, q[2], q[3]) + q[5],
        q[3] + q[3],
    )
    bins = lax.broadcasted_iota(jnp.int32, (64, 128), 0).astype(F32)
    row = lambda at: marks[at : at + 1, :]
    mirrored = [jnp.where(labels[group] < 63.5, row(3 + group), 0.0) for group in range(2)]
    counted = [jnp.where(lanes[:1] == place[0], 0.0, mirrored[0]), mirrored[1]]
    mirrored.append(row(5))
    labels.append(row(8))
    losses = jnp.zeros((1, 128), F32)
    slope = []
    for group in range(3):
        logits = pairs[group] + dist_bias
        shifted = logits - jnp.max(logits, axis=0, keepdims=True)
        powers = jnp.exp(shifted)
        norms = jnp.sum(powers, axis=0, keepdims=True)
        log_probs = shifted - jnp.log(norms)
        probs = powers * (1.0 / norms)
        onehot = (bins == row(6 + group)).astype(F32)
        onehot_back = (bins == labels[group]).astype(F32)
        losses = losses - row(group) * jnp.sum(onehot * log_probs, axis=0, keepdims=True)
        if group < 2:
            losses = losses - counted[group] * jnp.sum(onehot_back * log_probs, axis=0, keepdims=True)
        slope.append(row(group) * (probs - onehot) + mirrored[group] * (probs - onehot_back))
    blocks = (
        (0, jnp.where(higher, slope[0], 0.0)),
        (2, jnp.where(higher, slope[1], slope[0])),
        (3, jnp.where(higher, 0.0, slope[1]) + slope[2]),
        (4, jnp.where(lanes == place[0], 0.0, slope[0])),
        (5, slope[1]),
    )
    weights = jnp.zeros((64, 128), F32)
    for block, values in blocks:
        high = values.astype(BF16)
        low = (values - high.astype(F32)).astype(BF16)
        weights = weights + dot(high, kept[block], NN) + dot(low, kept[block], NN)
    for n in range(3):
        grad[n * 64 : (n + 1) * 64, :] = blocks[n][1]
    slopes[0:128, :] = jnp.transpose(jnp.concatenate(slope[:2], axis=0))
    others = [slopes[pl.ds(y * 32 + x, 8, stride=4), :] for y in range(4) for x in range(4)]
    total[...] = message(weights, jnp.sum(losses, axis=1, keepdims=True), others)


def middle_kernel(got, send, slopes):
    values = got[...].astype(F32)
    slopes[0:128, :] = values.reshape(16, 72, 128)[:, 64:72].reshape(128, 128)
    weights, loss = add_sums(values, 16)
    send[...] = message(weights, loss, [slopes[pl.ds(z, 16, stride=8), :] for z in range(8)])


def last_kernel(
    got, updated, grad, place, heavy, grad_weight, loss, grad_pair, pair_out,
    slopes, rows, order,
):
    for block in range(4):
        rows[pl.ds(block // 2 * 256 + block % 2, 128, stride=2), :] = updated[
            block * 128 : (block + 1) * 128, :
        ].astype(F32)
    pair_out[...] = rows[0:512, :].astype(BF16)
    dist_weight = heavy[256:320, :]
    part = {}
    for n, block in enumerate((0, 2, 3)):
        slope = grad[n * 64 : (n + 1) * 64, :]
        high = slope.astype(BF16)
        low = (slope - high.astype(F32)).astype(BF16)
        part[block] = dot(high, dist_weight, TN) + dot(low, dist_weight, TN)
    values = got[...].astype(F32)
    for z in range(8):
        for y in range(4):
            at = z * 80 + 64 + y * 4
            slopes[y * 32 + z * 4 : y * 32 + z * 4 + 4, :] = values[at : at + 4]
    there = slopes[...].astype(BF16)
    none = jnp.zeros((64, 128), BF16)
    first = dot(there, jnp.concatenate([dist_weight, none], axis=0), NN)
    second = dot(there, jnp.concatenate([none, dist_weight], axis=0), NN)
    device = lax.broadcasted_iota(jnp.int32, (128, 128), 0) * 2
    results = (
        part[0] + jnp.where(device < place[0], first, 0.0),
        jnp.where(device <= place[0], second, first),
        part[2],
        part[3] + jnp.where(device > place[0], second, 0.0),
    )
    for block in range(4):
        order[pl.ds(block // 2 * 256 + block % 2, 128, stride=2), :] = results[block]
    grad_pair[...] = order[0:512, :]
    weights, total = add_sums(values, 8)
    row = lax.broadcasted_iota(jnp.int32, (64, 128), 0)
    weights = jnp.where(row == 63, 0.0, weights)
    rest = jnp.sum(weights, axis=0, keepdims=True)
    grad_weight[...] = jnp.where(row == 63, -rest, weights) * (1.0 / 256)
    loss[0] = total[0, 0] * (1.0 / 65536)


def run(kernel, outs, scratch, args, **specs):
    shapes = [jax.ShapeDtypeStruct(s, d) for s, d in outs]
    moved = sum(x.size * x.dtype.itemsize for x in args)
    scratch = [pltpu.VMEM(*s) if isinstance(s, tuple) else s for s in scratch]
    return pl.pallas_call(
        kernel,
        out_shape=shapes,
        scratch_shapes=scratch,
        compiler_params=pltpu.CompilerParams(vmem_limit_bytes=24 * 1024 * 1024),
        cost_estimate=pl.CostEstimate(flops=10_000_000, bytes_accessed=moved, transcendentals=0),
        **specs,
    )(*args)


VMEM, FAR = pl.BlockSpec(memory_space=pltpu.VMEM), pl.BlockSpec(memory_space=pl.ANY)
SMEM = pl.BlockSpec(memory_space=pltpu.SMEM)


def pack(place, *args):
    scratch = [(arg.shape, arg.dtype) for arg in args]
    scratch += [((520, 128), F32), ((1296, 128), F32), ((16, 256), F32)]
    scratch += [pltpu.SemaphoreType.DMA((13,))]
    outs = [
        ((1280, 128), BF16),
        ((256, 128), F32),
        ((512, 128), F32),
        ((512, 128), F32),
        ((24, 128), F32),
        ((320, 128), BF16),
    ]
    args = [pltpu.with_memory_space_constraint(arg, pltpu.HBM) for arg in args]
    return run(pack_kernel, outs, scratch, (place, *args), in_specs=[SMEM] + [FAR] * 13)


def triangle(*args):
    outs = [((768, 128), BF16), ((256, 128), F32), ((256, 128), F32)]
    return run(triangle_kernel, outs, [((1296, 128), F32), ((784, 128), F32)], args)


def head(*args):
    outs = [((512, 128), BF16), ((192, 128), F32), ((1152, 128), BF16)]
    scratch = [((784, 128), F32), ((136, 128), F32)]
    return run(head_kernel, outs, scratch, args, in_specs=[VMEM] * 6 + [SMEM] + [VMEM])


def middle(got):
    return run(middle_kernel, [((640, 128), BF16)], [((136, 128), F32)], (got,))[0]


def last(*args):
    outs = [((64, 128), F32), ((1,), F32), ((512, 128), F32), ((512, 128), BF16)]
    scratch = [((128, 128), F32), ((520, 128), F32), ((520, 128), F32)]
    specs = {"in_specs": [VMEM] * 3 + [SMEM, VMEM], "out_specs": [VMEM, SMEM, VMEM, VMEM]}
    return run(last_kernel, outs, scratch, args, **specs)


def exchange(values, axes):
    return lax.all_to_all(values, axes, 0, 0, tiled=True)


def on_device(
    pair,
    chain,
    targets,
    pair_mask,
    ln_in_gain,
    ln_in_bias,
    in_weight,
    out_gate_weight,
    ln_out_gain,
    ln_out_bias,
    out_weight,
    dist_weight,
    dist_bias,
):
    place = (lax.axis_index(GROUP) * 2).reshape(1)
    row = lambda values: values.reshape(1, values.shape[0])
    send, labels, base, gate, marks, heavy = pack(
        place,
        targets,
        pair_mask,
        row(chain),
        pair.reshape(512, 128),
        row(ln_in_gain),
        row(ln_in_bias),
        row(ln_out_gain),
        row(ln_out_bias),
        row(dist_bias),
        in_weight,
        out_gate_weight,
        out_weight,
        jnp.swapaxes(dist_weight, 0, 1),
    )
    got = exchange(send.reshape(128, 5, 2, 128), GROUP).reshape(1280, 128)
    products, back_base, back_gate = triangle(got, labels, marks, heavy)
    hidden = exchange(products.reshape(128, 3, 2, 128), GROUP).reshape(768, 128)
    updated, grad, total = head(hidden, base, gate, back_base, back_gate, marks, place, heavy)
    total = middle(exchange(total.reshape(16, 72, 128), PLANE).reshape(1152, 128))
    total = exchange(total.reshape(8, 80, 128), "zlo").reshape(640, 128)
    grad_weight, loss, grad_pair, pair_out = last(total, updated, grad, place, heavy)
    return (
        pair_out.reshape(2, 256, 128),
        grad_pair.reshape(2, 256, 128),
        jnp.swapaxes(grad_weight, 0, 1),
        loss,
    )


def solution(mesh):
    fine = Mesh(mesh.devices.reshape(2, 2, 4, 8, 4), EVERY)
    part = ("zhi", "core")
    in_specs = (
        P(EVERY, None, None),
        P(part),
        P(EVERY, None),
        P(EVERY, None),
        P(),
        P(),
        P(),
        P(),
        P(),
        P(),
        P(),
        P(part, None),
        P(),
    )
    out_specs = (
        P(EVERY, None, None),
        P(EVERY, None, None),
        P(part, None),
        P(part),
    )
    return jax.shard_map(
        on_device, mesh=fine, in_specs=in_specs, out_specs=out_specs, check_vma=False
    )
```
